32 devices in a mesh: groups: 1, dp: 32 (over z, y, x, core).
Axes of the slice: x: 2, y: 2, z: 4, core: 2. Of those that a mesh axis runs over, the one named last changes fastest.
Arguments:
- queries: bfloat16 [128, 128, 576], P(('groups', 'dp')), may hold values from -900 to 900
- latent_cache: bfloat16 [128, 512, 576], P(('groups', 'dp')), may hold values from -6 to 6
- lengths: int32 [128], P(('groups', 'dp')), may hold values from 2 to 512, as said below
- hidden_in: bfloat16 [128, 7168], P(('groups', 'dp')), may hold values from -0.75 to 0.75
- route_ids: int32 [128, 2], P(('groups', 'dp')), may hold values from 0 to 3, all different within a row; in each aligned block of 4 rows (0 to 3, 4 to 7, ...) at most 2 rows name the same one
- route_weights: float32 [128, 2], P(('groups', 'dp')), may hold values from 0.3 to 1.5
- value_up: bfloat16 [128, 512, 128], P('dp'), may hold values from -0.25 to 0.25
- out_proj: bfloat16 [16384, 7168], P('dp'), may hold values from -0.046875 to 0.046875
- norm_gain: bfloat16 [7168], replicated, may hold values from 0.099609375 to 1.8984375
- gate_up: bfloat16 [2, 7168, 4096], P(None, None, 'dp'), may hold values from -0.0625 to 0.0625
- down_proj: bfloat16 [4096, 7168], P('dp'), may hold values from -0.1875 to 0.1875
Outputs:
- hidden_out: bfloat16 [128, 7168], P(('groups', 'dp'))
The draws below stay inside these ranges and needn't reach their ends.
Inputs may be any that keep to these rules, and one draw needn't show every extreme that they name: `route_ids`: within one device's 4 rows no expert is picked more than 2 times; the picks of a row are distinct. `lengths`: some row has exactly 512 live slots.
All inputs are finite; a program needn't handle non-finite values.
Results may differ from the reference program's by a relative error of at most 0.011.
Values may be sent and summed in bfloat16 or wider, within the bound.
No kernel may reach another device: no remote copies, remote signals or barrier semaphores. Data moves between devices by JAX's collectives and lax.ppermute only.
A program may use at most 128 MiB of HBM per device.

```python
import math
import jax
import jax.numpy as jnp
import numpy as np
from jax import lax

D = 7168
HEADS = 128
LAT = 512
ROPE = 64
VH = 128
FFW = 1024
TOPW = 2
RD = 4
MAXLEN = 512
ROWS = 128
EXPERTS = 4
CAP = 2


def cache_normal(key):
    return jax.random.normal(key, (ROWS, MAXLEN, LAT + ROPE), jnp.float32)


def draw_latent_cache(key, part):
    base = jnp.clip(cache_normal(key), -6.0, 6.0)
    return base.astype(jnp.bfloat16)


def draw_queries(key, part):
    key = jax.random.fold_in(key, 23)
    fresh = jnp.clip(jax.random.normal(key, (ROWS, HEADS, LAT + ROPE), jnp.float32), -6.0, 6.0)
    return fresh.astype(jnp.bfloat16)


def draw_lengths(key, part):
    key = jax.random.fold_in(key, 37)
    key_list = jax.random.split(key, 3)
    factor = jax.random.randint(key_list[0], (ROWS // RD,), 1, 9)
    raw_draw = jax.random.randint(key_list[1], (ROWS,), 0, MAXLEN - 1)
    length_rows = 2 + raw_draw * jnp.repeat(factor, RD) // 8
    longest = jax.random.randint(key_list[2], (), 0, ROWS)
    return jnp.where(jnp.arange(ROWS) == longest, MAXLEN, length_rows).astype(jnp.int32)


def block_scale(own_key, dims, pieces, least, top_value):
    def one(axis_at, parts):
        steps = jax.random.uniform(jax.random.fold_in(jax.random.fold_in(own_key, 6), axis_at), (parts,), jnp.float32, least / len(pieces), top_value / len(pieces))
        return jnp.repeat(jnp.exp(steps), dims[axis_at] // parts).reshape((-1,) + (1,) * (len(dims) - axis_at - 1))

    level = one(*pieces[0])
    for cut in pieces[1:]:
        level = level * one(*cut)
    return level


def assign_block(key, own, number, rows, amount, top, limit, slope):
    sequence = jax.random.permutation(key, amount)
    heavy_load, common = portions_of(amount, rows * top, limit, slope, True), portions_of(amount, rows * top, limit, slope, False)
    places = jnp.arange(amount)

    def named(sizes, rotation):
        used = int((sizes > 0).sum())
        fixed = max(1, used // 4)
        shifted = fixed + (places - fixed + rotation * (used - fixed)) % max(1, amount - fixed)
        return jnp.zeros((amount,), jnp.int32).at[sequence[jnp.where(places < fixed, places, shifted)]].set(jnp.asarray(sizes, jnp.int32))

    sizes = jnp.where(number % 4 == 0, named(heavy_load, number // 4), named(common, number - number // 4 - 1))
    mixed = jax.random.permutation(jax.random.fold_in(own, 3), amount)
    donor, receiver = mixed[0:amount // 2 * 2:2], mixed[1:amount // 2 * 2:2]
    room = jnp.minimum(sizes[donor] - 1, limit - sizes[receiver]) // 2
    room = jnp.where((donor == sequence[0]) | (receiver == sequence[0]) | (sizes[receiver] == 0), 0, jnp.maximum(room, 0))
    shifted = jax.random.randint(jax.random.fold_in(own, 4), (amount // 2,), 0, 1 << 20) % (room + 1)
    sizes = sizes.at[donor].add(-shifted).at[receiver].add(shifted)
    members = jnp.searchsorted(jnp.cumsum(sizes), jnp.arange(rows * top), side="right").astype(jnp.int32)
    grid = members.reshape(top, rows).T
    grid = grid[jax.random.permutation(jax.random.fold_in(own, 1), rows)]
    rotation = jax.random.randint(jax.random.fold_in(own, 2), (rows, 1), 0, top)
    return jnp.take_along_axis(grid, (jnp.arange(top)[None, :] + rotation) % top, axis=1)


def portions_of(number_of, total, bound, lean, full):
    weights = [(1 << 20) // math.isqrt(rank ** lean) + 1 for rank in range(1, number_of + 1)]
    largest = bound if full else min(bound, max(-(-total // number_of), total * weights[0] // sum(weights)))
    least = 1 if total - largest >= number_of - 1 else 0
    holding, spare = [largest] + [least] * (number_of - 1), total - largest - least * (number_of - 1)
    while spare > 0:
        movable = [i for i in range(1, number_of) if holding[i] < largest] or [i for i in range(1, number_of) if holding[i] < bound]
        whole, remaining = sum([weights[i] for i in movable]), spare
        for i in movable:
            addition = min(bound - holding[i], max(1, remaining * weights[i] // whole), spare)
            holding[i] = holding[i] + addition
            spare = spare - addition
    return np.array(holding)


def noise(rng, shape, scale, limit, shards=(), kind=jnp.bfloat16):
    array = scale * jax.random.normal(rng, shape, jnp.float32)
    if shards:
        array = array * block_scale(rng, shape, shards, -0.22, 0.18)
    return jnp.clip(array, -limit, limit).astype(kind)


def setup_inputs(seed: int = 0, part: int = 0) -> dict:
    key_of = jax.random.split(jax.random.key(seed), 12)
    own_keys = jax.random.split(jax.random.fold_in(key_of[11], part), 12)
    queries = draw_queries(jax.random.fold_in(jax.random.fold_in(key_of[11], part), 71), part)
    latent_cache = draw_latent_cache(jax.random.fold_in(jax.random.fold_in(key_of[11], part), 71), part)
    lengths = draw_lengths(jax.random.fold_in(jax.random.fold_in(key_of[11], part), 71), part)
    hidden_in = noise(own_keys[3], (ROWS, D), 0.05, 0.75, ((0, 32),))
    route_ids_keys = jax.random.split(jax.random.fold_in(own_keys[4], 1), ROWS // RD)
    route_ids_turns = jax.random.permutation(jax.random.fold_in(own_keys[4], 3), ROWS // RD)
    route_ids = jax.vmap(lambda own, number: assign_block(jax.random.fold_in(own_keys[4], 2), own, number, RD, EXPERTS, TOPW, CAP, 2))(route_ids_keys, route_ids_turns).reshape((ROWS, TOPW))
    route_weights = jnp.clip(0.3 + 1.2 * jax.random.uniform(own_keys[5], (ROWS, TOPW), jnp.float32) ** block_scale(own_keys[5], (ROWS, TOPW), ((0, 32),), -0.2, 0.2), 0.3, 1.5)
    value_up = noise(key_of[6], (HEADS, LAT, VH), LAT ** -0.5, 0.25, ((0, 32),))
    out_proj = noise(key_of[7], (HEADS * VH, D), (HEADS * VH) ** -0.5, 0.046875, ((0, 32),))
    norm_gain = jnp.clip(1.0 + 0.18 * jax.random.normal(key_of[8], (D,), jnp.float32), 0.099609375, 1.8984375).astype(jnp.bfloat16)
    gate_up = noise(key_of[9], (2, D, EXPERTS * FFW), D ** -0.5, 0.0625, ((2, 32),))
    down_proj = noise(key_of[10], (EXPERTS * FFW, D), FFW ** -0.5, 0.1875, ((0, 32),))
    return dict(queries=queries, latent_cache=latent_cache, lengths=lengths, hidden_in=hidden_in, route_ids=route_ids, route_weights=route_weights, value_up=value_up, out_proj=out_proj, norm_gain=norm_gain, gate_up=gate_up, down_proj=down_proj)


MASKED = -1e+30
EPSILON = 1e-06

def reference(queries, latent_cache, lengths, hidden_in, route_ids, route_weights, value_up, out_proj, norm_gain, gate_up, down_proj):
    scale_factor = (VH + ROPE) ** (-0.5)
    scores = jnp.einsum('rhc,rpc->rhp', queries.astype(jnp.float32), latent_cache.astype(jnp.float32)) * scale_factor
    position_ids = jnp.arange(MAXLEN, dtype=jnp.int32)
    scores = jnp.where(position_ids[None, None, :] < lengths[:, None, None], scores, MASKED)
    row_max = lax.optimization_barrier(jnp.max(scores, axis=2, keepdims=True))
    exp_terms = jnp.exp(scores - row_max)
    exp_total = lax.optimization_barrier(jnp.sum(exp_terms, axis=2, keepdims=True))
    prob_bf = exp_terms.astype(jnp.bfloat16)
    numerator = jnp.einsum('rhp,rpc->rhc', prob_bf.astype(jnp.float32), latent_cache[:, :, :LAT].astype(jnp.float32))
    latent_out = (numerator / exp_total).astype(jnp.bfloat16)
    head_values = jnp.einsum('rhc,hcv->rhv', latent_out.astype(jnp.float32), value_up.astype(jnp.float32)).astype(jnp.bfloat16)
    attention = jnp.dot(head_values.reshape(ROWS, HEADS * VH), out_proj, preferred_element_type=jnp.float32)
    residual = (hidden_in.astype(jnp.float32) + attention).astype(jnp.bfloat16)
    resid_wide = residual.astype(jnp.float32)
    mean_square = lax.optimization_barrier(jnp.mean(resid_wide * resid_wide, axis=1, keepdims=True))
    normed = (resid_wide * lax.rsqrt(mean_square + EPSILON) * norm_gain.astype(jnp.float32)).astype(jnp.bfloat16)
    expert_list = jnp.arange(EXPERTS, dtype=jnp.int32)
    expert_weight = lax.optimization_barrier(jnp.sum(route_weights[:, :, None] * (route_ids[:, :, None] == expert_list[None, None, :]).astype(jnp.float32), axis=1))

    def one_expert(mixture, expert):
        gate_cols = lax.dynamic_slice_in_dim(gate_up[0], expert * FFW, FFW, 1)
        up_cols = lax.dynamic_slice_in_dim(gate_up[1], expert * FFW, FFW, 1)
        gate_part = jnp.dot(normed, gate_cols, preferred_element_type=jnp.float32)
        up_part = jnp.dot(normed, up_cols, preferred_element_type=jnp.float32)
        activated = (jax.nn.silu(gate_part) * up_part).astype(jnp.bfloat16)
        down_rows = lax.dynamic_slice_in_dim(down_proj, expert * FFW, FFW, 0)
        expert_out = jnp.dot(activated, down_rows, preferred_element_type=jnp.float32)
        column = lax.optimization_barrier(jnp.sum(expert_weight * (expert_list == expert).astype(jnp.float32)[None, :], axis=1))
        return (mixture + column[:, None] * expert_out, None)
    mixture, unused = lax.scan(one_expert, jnp.zeros((ROWS, D), jnp.float32), expert_list)
    return (resid_wide + mixture).astype(jnp.bfloat16)
```

```python
import functools

import jax
import jax.numpy as jnp
from jax import lax
from jax.experimental import pallas as pl
from jax.experimental.pallas import tpu as pltpu
from jax.sharding import PartitionSpec as P

LAT = 512
ROPE = 64
VH = 128
SPLIT = 8

MASKED = -1e30
EPSILON = 1e-06
VMEM = 24 * 1024 * 1024

F32 = jnp.float32
BF16 = jnp.bfloat16
SCALARS = pl.BlockSpec(memory_space=pltpu.SMEM)


def sds(shape, dtype):
    return jax.ShapeDtypeStruct(shape, dtype)


def params():
    return pltpu.CompilerParams(vmem_limit_bytes=VMEM)


def whole(shape):
    return pl.BlockSpec(shape, lambda *_: (0,) * len(shape))


def attention_kernel(rows, lengths, q_ref, k_ref, o_ref, lat):
    row = pl.program_id(0)
    heads = q_ref.shape[2]
    slots = k_ref.shape[2]
    keys = k_ref[0]
    scores = lax.dot_general(
        q_ref[0], keys, (((0,), (0,)), ((), ())), preferred_element_type=F32
    ) * ((VH + ROPE) ** -0.5)
    position = lax.broadcasted_iota(jnp.int32, scores.shape, 1)
    scores = jnp.where(position < lengths[row], scores, MASKED)
    terms = jnp.exp(scores - jnp.max(scores, axis=1, keepdims=True))
    total = jnp.sum(terms, axis=1, keepdims=True)
    numerator = lax.dot_general(
        terms.astype(BF16), keys[:LAT], (((1,), (1,)), ((), ())), preferred_element_type=F32
    )
    lat[pl.ds(pl.multiple_of(row * heads, heads), heads), :] = (numerator / total).astype(BF16)

    @pl.when(row == rows - 1)
    def _():
        size = rows * heads
        i = lax.broadcasted_iota(jnp.int32, (size, size), 0)
        k = lax.broadcasted_iota(jnp.int32, (size, size), 1)
        pick = jnp.where(k == (i % rows) * heads + i // rows, 1.0, 0.0).astype(BF16)
        o_ref[...] = jnp.dot(pick, lat[...], preferred_element_type=F32).astype(BF16)


def attention(queries, latent_cache, lengths):
    rows, heads, width = queries.shape
    slots = latent_cache.shape[1]
    q_t = jnp.swapaxes(queries, 1, 2)
    k_t = jnp.swapaxes(latent_cache, 1, 2)
    return pl.pallas_call(
        functools.partial(attention_kernel, rows),
        grid=(rows,),
        in_specs=[
            SCALARS,
            pl.BlockSpec((1, width, heads), lambda r: (r, 0, 0)),
            pl.BlockSpec((1, width, slots), lambda r: (r, 0, 0)),
        ],
        out_specs=whole((rows * heads, LAT)),
        out_shape=sds((rows * heads, LAT), BF16),
        scratch_shapes=[pltpu.VMEM((rows * heads, LAT), BF16)],
        compiler_params=params(),
        name="latent_attention",
    )(lengths, q_t, k_t)


def project_kernel(planes, rows, me, x_ref, v_ref, w_ref, own_ref, other_ref, flat):
    heads = v_ref.shape[0]

    @pl.when(pl.program_id(0) == 0)
    def _():
        count = flat.shape[0]
        i = lax.broadcasted_iota(jnp.int32, (count, x_ref.shape[0]), 0)
        k = lax.broadcasted_iota(jnp.int32, (count, x_ref.shape[0]), 1)
        row = i % rows
        plane = (i // rows) % planes
        rest = i // (rows * planes)
        home = me[0] ^ (plane * 8 + (rest % 4) * 2 + rest // 4)
        target = home * (heads * rows) + row
        for h in range(heads):
            pick = jnp.where(k == target + h * rows, 1.0, 0.0).astype(BF16)
            mine = jnp.dot(pick, x_ref[...], preferred_element_type=F32).astype(BF16)
            flat[:, h * VH : (h + 1) * VH] = jnp.dot(
                mine, v_ref[h], preferred_element_type=F32
            ).astype(BF16)

    out = jnp.dot(flat[...], w_ref[...], preferred_element_type=F32)
    half = out.shape[0] // 2
    own_ref[...] = out[:half]
    other_ref[...] = out[half:].astype(BF16)


def project(me, by_heads, value_up, out_proj, planes, rows):
    count = planes * 8 * rows
    depth, features = out_proj.shape
    tile = features // 4
    half = count // 2
    return pl.pallas_call(
        functools.partial(project_kernel, planes, rows),
        grid=(features // tile,),
        in_specs=[
            SCALARS,
            whole(by_heads.shape),
            whole(value_up.shape),
            pl.BlockSpec((depth, tile), lambda t: (0, t)),
        ],
        out_specs=[
            pl.BlockSpec((half, tile), lambda t: (0, t)),
            pl.BlockSpec((half, tile), lambda t: (0, t)),
        ],
        out_shape=[sds((half, features), F32), sds((half, features), BF16)],
        scratch_shapes=[pltpu.VMEM((count, depth), BF16)],
        compiler_params=params(),
        name="projections",
    )(me, by_heads, value_up, out_proj)


def add_kernel(arrived, parts, *refs):
    total = refs[0][...]
    for ref in refs[1 : 1 + arrived]:
        total = total + ref[...].astype(F32)
    outs = refs[1 + arrived :]
    size = total.shape[0] // parts
    outs[0][...] = total[:size]
    for p in range(1, parts):
        outs[p][...] = total[p * size : (p + 1) * size].astype(BF16)


def add_and_cut(own, received, parts, name, steps=2):
    count, features = own.shape
    size = count // parts
    tile = features // steps
    return pl.pallas_call(
        functools.partial(add_kernel, len(received), parts),
        grid=(steps,),
        in_specs=[pl.BlockSpec((count, tile), lambda t: (0, t))] * (1 + len(received)),
        out_specs=[pl.BlockSpec((size, tile), lambda t: (0, t))] * parts,
        out_shape=[sds((size, features), F32)] + [sds((size, features), BF16)] * (parts - 1),
        compiler_params=params(),
        name=name,
    )(own, *received)


def norm_kernel(planes, cap, me, ids, own_ref, *refs):
    received = refs[: planes - 1]
    hidden_ref, gain_ref = refs[planes - 1 : planes + 1]
    resid_ref = refs[planes + 1]
    packs = refs[planes + 2 : 2 * planes + 2]
    normed, packed = refs[2 * planes + 2 :]
    total = own_ref[...]
    for ref in received:
        total = total + ref[...].astype(F32)
    resid = (hidden_ref[...].astype(F32) + total).astype(BF16)
    resid_ref[...] = resid
    wide = resid.astype(F32)
    scale = lax.rsqrt(jnp.mean(wide * wide, axis=1, keepdims=True) + EPSILON)
    normed[...] = (wide * scale * gain_ref[...].astype(F32)).astype(BF16).astype(F32)
    rows, picks = ids.shape
    plane = me[0] // 8
    for k in range(planes):
        expert = plane ^ k
        places = [jnp.int32(0)] * cap
        seen = jnp.int32(0)
        for r in range(rows):
            has = ids[r, 0] == expert
            for t in range(1, picks):
                has = has | (ids[r, t] == expert)
            for s in range(cap):
                places[s] = jnp.where(has & (seen == s), r, places[s])
            seen = seen + has.astype(jnp.int32)
        for s in range(cap):
            packed[k * cap + s : k * cap + s + 1, :] = normed[pl.ds(places[s], 1), :]
        packs[k][...] = packed[k * cap : (k + 1) * cap, :].astype(BF16)


def norm_and_pack(me, ids, own, received, hidden, gain, planes, cap):
    rows, features = own.shape
    vec = pl.BlockSpec(memory_space=pltpu.VMEM)
    return pl.pallas_call(
        functools.partial(norm_kernel, planes, cap),
        in_specs=[SCALARS, SCALARS] + [vec] * (2 + planes),
        out_specs=[vec] * (1 + planes),
        out_shape=[sds((rows, features), BF16)] + [sds((cap, features), BF16)] * planes,
        scratch_shapes=[
            pltpu.VMEM((rows, features), F32),
            pltpu.VMEM((planes * cap, features), F32),
        ],
        compiler_params=params(),
        name="norm_and_pack",
    )(me, ids, own, *received, hidden, gain)


def stack_kernel(*refs):
    wide = refs[-1]
    out = refs[-2]
    size = refs[0].shape[0]
    for k, ref in enumerate(refs[:-2]):
        wide[k * size : (k + 1) * size, :] = ref[...].astype(F32)
    out[...] = wide[...].astype(BF16)


def stack(pieces):
    size, features = pieces[0].shape
    vec = pl.BlockSpec(memory_space=pltpu.VMEM)
    shape = (size * len(pieces), features)
    return pl.pallas_call(
        stack_kernel,
        in_specs=[vec] * len(pieces),
        out_specs=vec,
        out_shape=sds(shape, BF16),
        scratch_shapes=[pltpu.VMEM(shape, F32)],
        compiler_params=params(),
        name="stack_rows",
    )(*pieces)


def expert_kernel(pieces, steps, *refs):
    xs = refs[:pieces]
    gu_ref, down_ref, own_ref, other_ref, gate, up, act = refs[pieces:]
    step = pl.program_id(0)

    @pl.when(step == 0)
    def _():
        gate[...] = jnp.zeros_like(gate)
        up[...] = jnp.zeros_like(up)

    @pl.when(step < steps)
    def _():
        x = jnp.concatenate([ref[...].astype(F32) for ref in xs], axis=0).astype(BF16)
        gate[...] += jnp.dot(x, gu_ref[0], preferred_element_type=F32)
        up[...] += jnp.dot(x, gu_ref[1], preferred_element_type=F32)

    @pl.when(step == steps - 1)
    def _():
        g = gate[...]
        act[...] = (g / (1.0 + jnp.exp(-g)) * up[...]).astype(BF16)

    @pl.when(step >= steps)
    def _():
        out = jnp.dot(act[...], down_ref[...], preferred_element_type=F32)
        half = out.shape[0] // 2
        own_ref[...] = out[:half]
        other_ref[...] = out[half:].astype(BF16)


def expert(pieces, gate_up, down_proj, steps=4):
    size, features = pieces[0].shape
    count = size * len(pieces)
    hidden = gate_up.shape[2]
    tile = features // steps
    half = count // 2
    return pl.pallas_call(
        functools.partial(expert_kernel, len(pieces), steps),
        grid=(2 * steps,),
        in_specs=[pl.BlockSpec((size, tile), lambda t: (0, jnp.minimum(t, steps - 1)))]
        * len(pieces)
        + [
            pl.BlockSpec((2, tile, hidden), lambda t: (0, jnp.minimum(t, steps - 1), 0)),
            pl.BlockSpec((hidden, tile), lambda t: (0, jnp.maximum(t - steps, 0))),
        ],
        out_specs=[pl.BlockSpec((half, tile), lambda t: (0, jnp.maximum(t - steps, 0)))] * 2,
        out_shape=[sds((half, features), F32), sds((half, features), BF16)],
        scratch_shapes=[
            pltpu.VMEM((count, hidden), F32),
            pltpu.VMEM((count, hidden), F32),
            pltpu.VMEM((count, hidden), BF16),
        ],
        compiler_params=params(),
        name="expert",
    )(*pieces, gate_up, down_proj)


def combine_kernel(planes, cap, me, ids, weights, own_ref, *refs):
    received = refs[: planes - 1]
    resid_ref, out_ref, table, mixed = refs[planes - 1 :]
    table[:cap, :] = own_ref[...]
    for k, ref in enumerate(received):
        table[(k + 1) * cap : (k + 2) * cap, :] = ref[...].astype(F32)
    rows, picks = ids.shape
    plane = me[0] // 8
    for r in range(rows):
        total = None
        for t in range(picks):
            expert_id = ids[r, t]
            seen = jnp.int32(0)
            for b in range(r):
                for u in range(picks):
                    seen = seen + (ids[b, u] == expert_id).astype(jnp.int32)
            place = (expert_id ^ plane) * cap + seen
            term = weights[r, t] * table[pl.ds(place, 1), :]
            total = term if total is None else total + term
        mixed[r : r + 1, :] = total
    out_ref[...] = (resid_ref[...].astype(F32) + mixed[...]).astype(BF16)


def combine(me, ids, weights, own, received, resid, planes, cap):
    rows, features = resid.shape
    vec = pl.BlockSpec(memory_space=pltpu.VMEM)
    return pl.pallas_call(
        functools.partial(combine_kernel, planes, cap),
        in_specs=[SCALARS] * 3 + [vec] * (1 + planes),
        out_specs=vec,
        out_shape=sds((rows, features), BF16),
        scratch_shapes=[
            pltpu.VMEM((planes * cap, features), F32),
            pltpu.VMEM((rows, features), F32),
        ],
        compiler_params=params(),
        name="combine",
    )(me, ids, weights, own, *received, resid)


def body(
    queries,
    latent_cache,
    lengths,
    hidden_in,
    route_ids,
    route_weights,
    value_up,
    out_proj,
    norm_gain,
    gate_up,
    down_proj,
):
    devices = lax.axis_size("dp")
    planes = devices // SPLIT
    rows = hidden_in.shape[0]
    picks = route_ids.shape[1]
    cap = max(2, (rows * picks + planes - 1) // planes)
    me = lax.axis_index("dp").astype(jnp.int32).reshape(1)

    def swap(x, mask):
        return lax.ppermute(x, "dp", [(i, i ^ mask) for i in range(devices)])

    def over_chips(messages):
        return [swap(x, k << 1) for k, x in enumerate(messages, 1)]

    def over_planes(messages):
        return [swap(x, k << 3) for k, x in enumerate(messages, 1)]

    latents = attention(queries, latent_cache, lengths)
    by_heads = lax.all_to_all(latents, "dp", split_axis=0, concat_axis=0, tiled=True)
    own, other = project(me, by_heads, value_up, out_proj, planes, rows)
    own, *out = add_and_cut(own, [swap(other, 1)], 4, "add_core")
    own, *out = add_and_cut(own, over_chips(out), planes, "add_chips", 1)
    resid, mine, *out = norm_and_pack(
        me, route_ids, own, over_planes(out), hidden_in, norm_gain[None], planes, cap
    )
    picked = stack([mine] + over_planes(out))
    chips = [picked] + over_chips([picked] * 3)
    pieces = chips + [swap(x, 1) for x in chips]
    own, other = expert(pieces, gate_up, down_proj)
    own, *out = add_and_cut(own, [swap(other, 1)], 4, "add_expert_core")
    own, *out = add_and_cut(own, over_chips(out), planes, "add_expert_chips", 1)
    return combine(me, route_ids, route_weights, own, over_planes(out), resid, planes, cap)


def solution(mesh):
    placed = (
        P(("groups", "dp"), None, None),
        P(("groups", "dp"), None, None),
        P(("groups", "dp")),
        P(("groups", "dp"), None),
        P(("groups", "dp"), None),
        P(("groups", "dp"), None),
        P("dp", None, None),
        P("dp", None),
        P(),
        P(None, None, "dp"),
        P("dp", None),
    )
    return jax.shard_map(
        body, mesh=mesh, in_specs=placed, out_specs=P(("groups", "dp"), None), check_vma=False
    )
```

```python
import functools

import jax
import jax.numpy as jnp
from jax import lax
from jax.experimental import pallas as pl
from jax.experimental.pallas import tpu as pltpu
from jax.sharding import PartitionSpec as P

LAT = 512
ROPE = 64
VH = 128
SPLIT = 8

MASKED = -1e30
EPSILON = 1e-06
VMEM = 24 * 1024 * 1024

F32 = jnp.float32
BF16 = jnp.bfloat16
SCALARS = pl.BlockSpec(memory_space=pltpu.SMEM)


def sds(shape, dtype):
    return jax.ShapeDtypeStruct(shape, dtype)


def params():
    return pltpu.CompilerParams(vmem_limit_bytes=VMEM)


def in_hbm(x):
    return pltpu.with_memory_space_constraint(x, pltpu.HBM)


def whole(shape):
    return pl.BlockSpec(shape, lambda *_: (0,) * len(shape))


def attention_kernel(rows, lengths, q_ref, k_ref, o_ref, lat):
    row = pl.program_id(0)
    heads = q_ref.shape[2]
    slots = k_ref.shape[2]
    keys = k_ref[0]
    scores = lax.dot_general(
        q_ref[0], keys, (((0,), (0,)), ((), ())), preferred_element_type=F32
    ) * ((VH + ROPE) ** -0.5)
    position = lax.broadcasted_iota(jnp.int32, scores.shape, 1)
    scores = jnp.where(position < lengths[row], scores, MASKED)
    terms = jnp.exp(scores - jnp.max(scores, axis=1, keepdims=True))
    total = jnp.sum(terms, axis=1, keepdims=True)
    numerator = lax.dot_general(
        terms.astype(BF16), keys[:LAT], (((1,), (1,)), ((), ())), preferred_element_type=F32
    )
    lat[pl.ds(pl.multiple_of(row * heads, heads), heads), :] = (numerator / total).astype(BF16)

    @pl.when(row == rows - 1)
    def _():
        size = rows * heads
        i = lax.broadcasted_iota(jnp.int32, (size, size), 0)
        k = lax.broadcasted_iota(jnp.int32, (size, size), 1)
        pick = jnp.where(k == (i % rows) * heads + i // rows, 1.0, 0.0).astype(BF16)
        o_ref[...] = jnp.dot(pick, lat[...], preferred_element_type=F32).astype(BF16)


def attention(queries, latent_cache, lengths):
    rows, heads, width = queries.shape
    slots = latent_cache.shape[1]
    q_t = jnp.swapaxes(queries, 1, 2)
    k_t = jnp.swapaxes(latent_cache, 1, 2)
    return pl.pallas_call(
        functools.partial(attention_kernel, rows),
        grid=(rows,),
        in_specs=[
            SCALARS,
            pl.BlockSpec((1, width, heads), lambda r: (r, 0, 0)),
            pl.BlockSpec((1, width, slots), lambda r: (r, 0, 0)),
        ],
        out_specs=whole((rows * heads, LAT)),
        out_shape=sds((rows * heads, LAT), BF16),
        scratch_shapes=[pltpu.VMEM((rows * heads, LAT), BF16)],
        compiler_params=params(),
        name="latent_attention",
    )(
        lengths,
        in_hbm(q_t),
        in_hbm(k_t),
    )


def fetch_kernel(parts, *refs):
    count = len(parts)
    ins, outs, sems = refs[:count], refs[count + 1 : -1], refs[-1]
    copies = []
    for ref, (axis, cuts) in zip(ins, parts):
        size = ref.shape[axis] // cuts
        for c in range(cuts):
            at = (slice(None),) * axis + (pl.ds(c * size, size),)
            src = ref.at[c] if axis == 0 and size == 1 else ref.at[at]
            n = len(copies)
            copies.append(pltpu.make_async_copy(src, outs[n], sems.at[n]))
    for copy in copies:
        copy.start()
    for copy in copies:
        copy.wait()


def fetch(weights, parts, after):
    shapes = []
    for w, (axis, cuts) in zip(weights, parts):
        shape = list(w.shape)
        shape[axis] //= cuts
        if shape[0] == 1:
            shape = shape[1:]
        shapes += [pltpu.VMEM(tuple(shape), w.dtype)] * cuts
    out = pl.pallas_call(
        functools.partial(fetch_kernel, parts),
        in_specs=[pl.BlockSpec(memory_space=pltpu.HBM)] * len(weights)
        + [pl.BlockSpec(memory_space=pl.ANY)],
        out_specs=[pl.BlockSpec(memory_space=pltpu.VMEM)] * len(shapes),
        out_shape=shapes,
        scratch_shapes=[pltpu.SemaphoreType.DMA((len(shapes),))],
        compiler_params=params(),
        name="fetch_weights",
    )(*[in_hbm(w) for w in weights], after)
    result = []
    for _, cuts in parts:
        result.append(out[:cuts])
        out = out[cuts:]
    return result


def project_kernel(planes, rows, me, x_ref, v_ref, w_ref, own_ref, other_ref, flat):
    heads = v_ref.shape[0]

    @pl.when(pl.program_id(0) == 0)
    def _():
        count = flat.shape[0]
        i = lax.broadcasted_iota(jnp.int32, (count, x_ref.shape[0]), 0)
        k = lax.broadcasted_iota(jnp.int32, (count, x_ref.shape[0]), 1)
        row = i % rows
        plane = (i // rows) % planes
        rest = i // (rows * planes)
        home = me[0] ^ (plane * 8 + (rest % 4) * 2 + rest // 4)
        target = home * (heads * rows) + row
        for h in range(heads):
            pick = jnp.where(k == target + h * rows, 1.0, 0.0).astype(BF16)
            mine = jnp.dot(pick, x_ref[...], preferred_element_type=F32).astype(BF16)
            flat[:, h * VH : (h + 1) * VH] = jnp.dot(
                mine, v_ref[h], preferred_element_type=F32
            ).astype(BF16)

    out = jnp.dot(flat[...], w_ref[...], preferred_element_type=F32)
    half = out.shape[0] // 2
    own_ref[...] = out[:half]
    other_ref[...] = out[half:].astype(BF16)


def project(me, by_heads, value_up, out_proj, planes, rows):
    count = planes * 8 * rows
    depth, features = out_proj.shape
    tile = features // 7
    half = count // 2
    return pl.pallas_call(
        functools.partial(project_kernel, planes, rows),
        grid=(features // tile,),
        in_specs=[
            SCALARS,
            whole(by_heads.shape),
            whole(value_up.shape),
            pl.BlockSpec((depth, tile), lambda t: (0, t)),
        ],
        out_specs=[
            pl.BlockSpec((half, tile), lambda t: (0, t)),
            pl.BlockSpec((half, tile), lambda t: (0, t)),
        ],
        out_shape=[sds((half, features), F32), sds((half, features), BF16)],
        scratch_shapes=[pltpu.VMEM((count, depth), BF16)],
        compiler_params=params(),
        name="projections",
    )(me, by_heads, value_up, in_hbm(out_proj))


def add_kernel(arrived, parts, *refs):
    total = refs[0][...]
    for ref in refs[1 : 1 + arrived]:
        total = total + ref[...].astype(F32)
    outs = refs[1 + arrived :]
    size = total.shape[0] // parts
    outs[0][...] = total[:size]
    for p in range(1, parts):
        outs[p][...] = total[p * size : (p + 1) * size].astype(BF16)


def add_and_cut(own, received, parts, name, steps=2):
    count, features = own.shape
    size = count // parts
    tile = features // steps
    return pl.pallas_call(
        functools.partial(add_kernel, len(received), parts),
        grid=(steps,),
        in_specs=[pl.BlockSpec((count, tile), lambda t: (0, t))] * (1 + len(received)),
        out_specs=[pl.BlockSpec((size, tile), lambda t: (0, t))] * parts,
        out_shape=[sds((size, features), F32)] + [sds((size, features), BF16)] * (parts - 1),
        compiler_params=params(),
        name=name,
    )(own, *received)


def norm_kernel(planes, cap, me, ids, own_ref, *refs):
    received = refs[: planes - 1]
    hidden_ref, gain_ref = refs[planes - 1 : planes + 1]
    resid_ref = refs[planes + 1]
    packs = refs[planes + 2 : 2 * planes + 2]
    normed, packed = refs[2 * planes + 2 :]
    total = own_ref[...]
    for ref in received:
        total = total + ref[...].astype(F32)
    resid = (hidden_ref[...].astype(F32) + total).astype(BF16)
    resid_ref[...] = resid
    wide = resid.astype(F32)
    scale = lax.rsqrt(jnp.mean(wide * wide, axis=1, keepdims=True) + EPSILON)
    normed[...] = (wide * scale * gain_ref[...].astype(F32)).astype(BF16).astype(F32)
    rows, picks = ids.shape
    plane = me[0] // 8
    for k in range(planes):
        expert = plane ^ k
        places = [jnp.int32(0)] * cap
        seen = jnp.int32(0)
        for r in range(rows):
            has = ids[r, 0] == expert
            for t in range(1, picks):
                has = has | (ids[r, t] == expert)
            for s in range(cap):
                places[s] = jnp.where(has & (seen == s), r, places[s])
            seen = seen + has.astype(jnp.int32)
        for s in range(cap):
            packed[k * cap + s : k * cap + s + 1, :] = normed[pl.ds(places[s], 1), :]
        packs[k][...] = packed[k * cap : (k + 1) * cap, :].astype(BF16)


def norm_and_pack(me, ids, own, received, hidden, gain, planes, cap):
    rows, features = own.shape
    vec = pl.BlockSpec(memory_space=pltpu.VMEM)
    return pl.pallas_call(
        functools.partial(norm_kernel, planes, cap),
        in_specs=[SCALARS, SCALARS] + [vec] * (2 + planes),
        out_specs=[vec] * (1 + planes),
        out_shape=[sds((rows, features), BF16)] + [sds((cap, features), BF16)] * planes,
        scratch_shapes=[
            pltpu.VMEM((rows, features), F32),
            pltpu.VMEM((planes * cap, features), F32),
        ],
        compiler_params=params(),
        name="norm_and_pack",
    )(me, ids, own, *received, hidden, gain)


def stack_kernel(*refs):
    wide = refs[-1]
    out = refs[-2]
    size = refs[0].shape[0]
    for k, ref in enumerate(refs[:-2]):
        wide[k * size : (k + 1) * size, :] = ref[...].astype(F32)
    out[...] = wide[...].astype(BF16)


def stack(pieces):
    size, features = pieces[0].shape
    vec = pl.BlockSpec(memory_space=pltpu.VMEM)
    shape = (size * len(pieces), features)
    return pl.pallas_call(
        stack_kernel,
        in_specs=[vec] * len(pieces),
        out_specs=vec,
        out_shape=sds(shape, BF16),
        scratch_shapes=[pltpu.VMEM(shape, F32)],
        compiler_params=params(),
        name="stack_rows",
    )(*pieces)


def expert_kernel(pieces, tiles, *refs):
    xs = refs[:pieces]
    gate_ref, up_ref, down_ref, own_ref, other_ref = refs[pieces:]
    tile = down_ref.shape[1] // tiles
    gate, up = 0.0, 0.0
    for t in range(tiles):
        at = slice(t * tile, (t + 1) * tile)
        x = jnp.concatenate([ref[:, at].astype(F32) for ref in xs], axis=0).astype(BF16)
        gate += jnp.dot(x, gate_ref[at, :], preferred_element_type=F32)
        up += jnp.dot(x, up_ref[at, :], preferred_element_type=F32)
    act = (gate / (1.0 + jnp.exp(-gate)) * up).astype(BF16)
    half = act.shape[0] // 2
    for t in range(tiles):
        at = slice(t * tile, (t + 1) * tile)
        out = jnp.dot(act, down_ref[:, at], preferred_element_type=F32)
        own_ref[:, at] = out[:half]
        other_ref[:, at] = out[half:].astype(BF16)


def expert(pieces, gate_up, down_proj, tiles=7):
    size, features = pieces[0].shape
    half = size * len(pieces) // 2
    vec = pl.BlockSpec(memory_space=pltpu.VMEM)
    return pl.pallas_call(
        functools.partial(expert_kernel, len(pieces), tiles),
        in_specs=[vec] * (len(pieces) + 3),
        out_specs=[vec, vec],
        out_shape=[sds((half, features), F32), sds((half, features), BF16)],
        compiler_params=params(),
        name="expert",
    )(*pieces, *gate_up, down_proj)


def combine_kernel(planes, cap, me, ids, weights, own_ref, *refs):
    received = refs[: planes - 1]
    resid_ref, out_ref, table, mixed = refs[planes - 1 :]
    table[:cap, :] = own_ref[...]
    for k, ref in enumerate(received):
        table[(k + 1) * cap : (k + 2) * cap, :] = ref[...].astype(F32)
    rows, picks = ids.shape
    plane = me[0] // 8
    for r in range(rows):
        total = None
        for t in range(picks):
            expert_id = ids[r, t]
            seen = jnp.int32(0)
            for b in range(r):
                for u in range(picks):
                    seen = seen + (ids[b, u] == expert_id).astype(jnp.int32)
            place = (expert_id ^ plane) * cap + seen
            term = weights[r, t] * table[pl.ds(place, 1), :]
            total = term if total is None else total + term
        mixed[r : r + 1, :] = total
    out_ref[...] = (resid_ref[...].astype(F32) + mixed[...]).astype(BF16)


def combine(me, ids, weights, own, received, resid, planes, cap):
    rows, features = resid.shape
    vec = pl.BlockSpec(memory_space=pltpu.VMEM)
    return pl.pallas_call(
        functools.partial(combine_kernel, planes, cap),
        in_specs=[SCALARS] * 3 + [vec] * (1 + planes),
        out_specs=vec,
        out_shape=sds((rows, features), BF16),
        scratch_shapes=[
            pltpu.VMEM((planes * cap, features), F32),
            pltpu.VMEM((rows, features), F32),
        ],
        compiler_params=params(),
        name="combine",
    )(me, ids, weights, own, *received, resid)


def body(
    queries,
    latent_cache,
    lengths,
    hidden_in,
    route_ids,
    route_weights,
    value_up,
    out_proj,
    norm_gain,
    gate_up,
    down_proj,
):
    devices = lax.axis_size("dp")
    planes = devices // SPLIT
    rows = hidden_in.shape[0]
    picks = route_ids.shape[1]
    cap = max(2, (rows * picks + planes - 1) // planes)
    me = lax.axis_index("dp").astype(jnp.int32).reshape(1)

    def swap(x, mask):
        return lax.ppermute(x, "dp", [(i, i ^ mask) for i in range(devices)])

    def over_chips(messages):
        return [swap(x, k << 1) for k, x in enumerate(messages, 1)]

    def over_planes(messages):
        return [swap(x, k << 3) for k, x in enumerate(messages, 1)]

    latents = attention(queries, latent_cache, lengths)
    by_heads = lax.all_to_all(latents, "dp", split_axis=0, concat_axis=0, tiled=True)
    own, other = project(me, by_heads, value_up, out_proj, planes, rows)
    own, *out = add_and_cut(own, [swap(other, 1)], 4, "add_core")
    gate_up, (down_proj,) = fetch([gate_up, down_proj], [(0, 2), (0, 1)], own)
    own, *out = add_and_cut(own, over_chips(out), planes, "add_chips", 1)
    resid, mine, *out = norm_and_pack(
        me, route_ids, own, over_planes(out), hidden_in, norm_gain[None], planes, cap
    )
    picked = stack([mine] + over_planes(out))
    chips = [picked] + over_chips([picked] * 3)
    pieces = chips + [swap(x, 1) for x in chips]
    own, other = expert(pieces, gate_up, down_proj)
    own, *out = add_and_cut(own, [swap(other, 1)], 4, "add_expert_core")
    own, *out = add_and_cut(own, over_chips(out), planes, "add_expert_chips", 1)
    return combine(me, route_ids, route_weights, own, over_planes(out), resid, planes, cap)


def solution(mesh):
    placed = (
        P(("groups", "dp"), None, None),
        P(("groups", "dp"), None, None),
        P(("groups", "dp")),
        P(("groups", "dp"), None),
        P(("groups", "dp"), None),
        P(("groups", "dp"), None),
        P("dp", None, None),
        P("dp", None),
        P(),
        P(None, None, "dp"),
        P("dp", None),
    )
    return jax.shard_map(
        body, mesh=mesh, in_specs=placed, out_specs=P(("groups", "dp"), None), check_vma=False
    )
```

```python
import functools

import jax
import jax.numpy as jnp
from jax import lax
from jax.experimental import pallas as pl
from jax.experimental.pallas import tpu as pltpu
from jax.sharding import PartitionSpec as P

LAT = 512
ROPE = 64
VH = 128
SPLIT = 8

MASKED = -1e30
EPSILON = 1e-06
VMEM = 24 * 1024 * 1024

F32 = jnp.float32
BF16 = jnp.bfloat16
SCALARS = pl.BlockSpec(memory_space=pltpu.SMEM)


def sds(shape, dtype):
    return jax.ShapeDtypeStruct(shape, dtype)


def params():
    return pltpu.CompilerParams(vmem_limit_bytes=VMEM)


def in_hbm(x):
    return pltpu.with_memory_space_constraint(x, pltpu.HBM)


def whole(shape):
    return pl.BlockSpec(shape, lambda *_: (0,) * len(shape))


def attention_kernel(lengths, q_hbm, k_hbm, o_ref, queries, keys, lat, sems):
    rows, _, heads = queries.shape
    copies = []
    for r in range(rows):
        for n, (src, dst) in enumerate(((q_hbm, queries), (k_hbm, keys))):
            copy = pltpu.make_async_copy(src.at[r], dst.at[r], sems.at[2 * r + n])
            copy.start()
            copies.append(copy)
    for r in range(rows):
        copies[2 * r].wait()
        copies[2 * r + 1].wait()
        scores = lax.dot_general(
            queries[r], keys[r], (((0,), (0,)), ((), ())), preferred_element_type=F32
        ) * ((VH + ROPE) ** -0.5)
        position = lax.broadcasted_iota(jnp.int32, scores.shape, 1)
        scores = jnp.where(position < lengths[r], scores, MASKED)
        terms = jnp.exp(scores - jnp.max(scores, axis=1, keepdims=True))
        total = jnp.sum(terms, axis=1, keepdims=True)
        numerator = lax.dot_general(
            terms.astype(BF16), keys[r, :LAT], (((1,), (1,)), ((), ())), preferred_element_type=F32
        )
        lat[r * heads : (r + 1) * heads, :] = (numerator / total).astype(BF16)
    size = rows * heads
    i = lax.broadcasted_iota(jnp.int32, (size, 1), 0)
    k = lax.broadcasted_iota(jnp.int32, (size, size), 1)
    pick = jnp.where(k == (i % rows) * heads + i // rows, 1.0, 0.0).astype(BF16)
    o_ref[...] = jnp.dot(pick, lat[...], preferred_element_type=F32).astype(BF16)


def attention(queries, latent_cache, lengths):
    rows, heads, width = queries.shape
    slots = latent_cache.shape[1]
    hbm = pl.BlockSpec(memory_space=pltpu.HBM)
    return pl.pallas_call(
        attention_kernel,
        in_specs=[SCALARS, hbm, hbm],
        out_specs=pl.BlockSpec(memory_space=pltpu.VMEM),
        out_shape=sds((rows * heads, LAT), BF16),
        scratch_shapes=[
            pltpu.VMEM((rows, width, heads), BF16),
            pltpu.VMEM((rows, width, slots), BF16),
            pltpu.VMEM((rows * heads, LAT), BF16),
            pltpu.SemaphoreType.DMA((2 * rows,)),
        ],
        compiler_params=params(),
        name="latent_attention",
    )(
        lengths,
        in_hbm(jnp.swapaxes(queries, 1, 2)),
        in_hbm(jnp.swapaxes(latent_cache, 1, 2)),
    )


def fetch_kernel(parts, *refs):
    count = len(parts)
    ins, outs, sems = refs[:count], refs[count + 1 : -1], refs[-1]
    copies = []
    for ref, (axis, cuts) in zip(ins, parts):
        size = ref.shape[axis] // cuts
        for c in range(cuts):
            at = (slice(None),) * axis + (pl.ds(c * size, size),)
            src = ref.at[c] if axis == 0 and size == 1 else ref.at[at]
            n = len(copies)
            copies.append(pltpu.make_async_copy(src, outs[n], sems.at[n]))
    for copy in copies:
        copy.start()
    for copy in copies:
        copy.wait()


def fetch(weights, parts, after):
    shapes = []
    for w, (axis, cuts) in zip(weights, parts):
        shape = list(w.shape)
        shape[axis] //= cuts
        if shape[0] == 1:
            shape = shape[1:]
        shapes += [pltpu.VMEM(tuple(shape), w.dtype)] * cuts
    out = pl.pallas_call(
        functools.partial(fetch_kernel, parts),
        in_specs=[pl.BlockSpec(memory_space=pltpu.HBM)] * len(weights)
        + [pl.BlockSpec(memory_space=pl.ANY)],
        out_specs=[pl.BlockSpec(memory_space=pltpu.VMEM)] * len(shapes),
        out_shape=shapes,
        scratch_shapes=[pltpu.SemaphoreType.DMA((len(shapes),))],
        compiler_params=params(),
        name="fetch_weights",
    )(*[in_hbm(w) for w in weights], after)
    result = []
    for _, cuts in parts:
        result.append(out[:cuts])
        out = out[cuts:]
    return result


def project_kernel(planes, rows, tiles, me, x_ref, v_ref, w_hbm, own_ref, other_ref, flat, w, sems):
    tile = w.shape[2]
    copies = []
    for t in range(tiles):
        copy = pltpu.make_async_copy(w_hbm.at[:, pl.ds(t * tile, tile)], w.at[t], sems.at[t])
        copy.start()
        copies.append(copy)
    heads = v_ref.shape[0]
    count = flat.shape[0]
    i = lax.broadcasted_iota(jnp.int32, (count, 1), 0)
    k = lax.broadcasted_iota(jnp.int32, (count, x_ref.shape[0]), 1)
    plane = (i // rows) % planes
    rest = i // (rows * planes)
    home = me[0] ^ (plane * 8 + (rest % 4) * 2 + rest // 4)
    target = home * (heads * rows) + i % rows
    for h in range(heads):
        pick = jnp.where(k == target + h * rows, 1.0, 0.0).astype(BF16)
        mine = jnp.dot(pick, x_ref[...], preferred_element_type=F32).astype(BF16)
        flat[:, h * VH : (h + 1) * VH] = jnp.dot(
            mine, v_ref[h], preferred_element_type=F32
        ).astype(BF16)
    half = count // 2
    for t in range(tiles):
        copies[t].wait()
        at = slice(t * tile, (t + 1) * tile)
        out = jnp.dot(flat[...], w[t], preferred_element_type=F32)
        own_ref[:, at] = out[:half]
        other_ref[:, at] = out[half:].astype(BF16)


def project(me, by_heads, value_up, out_proj, planes, rows, tiles=7):
    count = planes * 8 * rows
    depth, features = out_proj.shape
    half = count // 2
    vec = pl.BlockSpec(memory_space=pltpu.VMEM)
    return pl.pallas_call(
        functools.partial(project_kernel, planes, rows, tiles),
        in_specs=[SCALARS, vec, vec, pl.BlockSpec(memory_space=pltpu.HBM)],
        out_specs=[vec, vec],
        out_shape=[sds((half, features), F32), sds((half, features), BF16)],
        scratch_shapes=[
            pltpu.VMEM((count, depth), BF16),
            pltpu.VMEM((tiles, depth, features // tiles), BF16),
            pltpu.SemaphoreType.DMA((tiles,)),
        ],
        compiler_params=params(),
        name="projections",
    )(me, by_heads, value_up, in_hbm(out_proj))


def add_kernel(arrived, parts, tile, *refs):
    outs = refs[-parts:]
    size = outs[0].shape[0]
    for start in range(0, outs[0].shape[1], tile):
        at = slice(start, start + tile)
        for p in range(parts):
            rows = slice(p * size, (p + 1) * size)
            if arrived and size % 16 == 0:
                total = refs[0][rows, at]
                for ref in refs[1 : 1 + arrived]:
                    total = total + ref[rows, at].astype(F32)
            else:
                if p == 0:
                    full = refs[0][:, at]
                    for ref in refs[1 : 1 + arrived]:
                        full = full + ref[:, at].astype(F32)
                total = full[rows]
            outs[p][:, at] = total if p == 0 else total.astype(BF16)


def add_and_cut(own, received, parts, name, after=()):
    count, features = own.shape
    size = count // parts
    vec = pl.BlockSpec(memory_space=pltpu.VMEM)
    return pl.pallas_call(
        functools.partial(add_kernel, len(received), parts, 512),
        in_specs=[vec] * (1 + len(received)) + [pl.BlockSpec(memory_space=pl.ANY)] * len(after),
        out_specs=[vec] * parts,
        out_shape=[sds((size, features), F32)] + [sds((size, features), BF16)] * (parts - 1),
        compiler_params=params(),
        name=name,
    )(own, *received, *after)


def norm_kernel(planes, cap, me, ids, *refs):
    hidden_ref, gain_ref, resid_ref = refs[planes : planes + 3]
    packs = refs[-2 - planes : -2]
    normed, packed = refs[-2:]
    total = refs[0][...]
    for ref in refs[1:planes]:
        total = total + ref[...].astype(F32)
    resid = (hidden_ref[...].astype(F32) + total).astype(BF16)
    resid_ref[...] = resid
    wide = resid.astype(F32)
    scale = lax.rsqrt(jnp.mean(wide * wide, axis=1, keepdims=True) + EPSILON)
    normed[...] = (wide * scale * gain_ref[...].astype(F32)).astype(BF16).astype(F32)
    rows, picks = ids.shape
    plane = me[0] // 8
    for k in range(planes):
        expert = plane ^ k
        places = [jnp.int32(0)] * cap
        seen = jnp.int32(0)
        for r in range(rows):
            has = ids[r, 0] == expert
            for t in range(1, picks):
                has = has | (ids[r, t] == expert)
            for s in range(cap):
                places[s] = jnp.where(has & (seen == s), r, places[s])
            seen = seen + has.astype(jnp.int32)
        for s in range(cap):
            packed[k * cap + s : k * cap + s + 1, :] = normed[pl.ds(places[s], 1), :]
        packs[k][...] = packed[k * cap : (k + 1) * cap, :].astype(BF16)


def norm_and_pack(me, ids, sums, hidden, gain, planes, cap):
    rows, features = hidden.shape
    vec = pl.BlockSpec(memory_space=pltpu.VMEM)
    return pl.pallas_call(
        functools.partial(norm_kernel, planes, cap),
        in_specs=[SCALARS, SCALARS] + [vec] * (2 + len(sums)),
        out_specs=[vec] * (1 + planes),
        out_shape=[sds((rows, features), BF16)] + [sds((cap, features), BF16)] * planes,
        scratch_shapes=[
            pltpu.VMEM((rows, features), F32),
            pltpu.VMEM((planes * cap, features), F32),
        ],
        compiler_params=params(),
        name="norm_and_pack",
    )(me, ids, *sums, hidden, gain)


def stack_kernel(count, *refs):
    wide = refs[-1]
    out = refs[-2]
    size = refs[0].shape[0]
    for k, ref in enumerate(refs[:count]):
        wide[k * size : (k + 1) * size, :] = ref[...].astype(F32)
    out[...] = wide[...].astype(BF16)


def stack(pieces, after):
    size, features = pieces[0].shape
    vec = pl.BlockSpec(memory_space=pltpu.VMEM)
    shape = (size * len(pieces), features)
    return pl.pallas_call(
        functools.partial(stack_kernel, len(pieces)),
        in_specs=[vec] * len(pieces) + [pl.BlockSpec(memory_space=pl.ANY)] * len(after),
        out_specs=vec,
        out_shape=sds(shape, BF16),
        scratch_shapes=[pltpu.VMEM(shape, F32)],
        compiler_params=params(),
        name="stack_rows",
    )(*pieces, *after)


def expert_kernel(pieces, tiles, *refs):
    xs = refs[:pieces]
    gate_ref, up_ref, down_ref, own_ref, other_ref = refs[pieces:]
    tile = down_ref.shape[1] // tiles
    gate, up = 0.0, 0.0
    for t in range(tiles):
        at = slice(t * tile, (t + 1) * tile)
        x = jnp.concatenate([ref[:, at].astype(F32) for ref in xs], axis=0).astype(BF16)
        gate += jnp.dot(x, gate_ref[at, :], preferred_element_type=F32)
        up += jnp.dot(x, up_ref[at, :], preferred_element_type=F32)
    act = (gate / (1.0 + jnp.exp(-gate)) * up).astype(BF16)
    half = act.shape[0] // 2
    for t in range(tiles):
        at = slice(t * tile, (t + 1) * tile)
        out = jnp.dot(act, down_ref[:, at], preferred_element_type=F32)
        own_ref[:, at] = out[:half]
        other_ref[:, at] = out[half:].astype(BF16)


def expert(pieces, gate_up, down_proj, tiles=7):
    size, features = pieces[0].shape
    half = size * len(pieces) // 2
    vec = pl.BlockSpec(memory_space=pltpu.VMEM)
    return pl.pallas_call(
        functools.partial(expert_kernel, len(pieces), tiles),
        in_specs=[vec] * (len(pieces) + 3),
        out_specs=[vec, vec],
        out_shape=[sds((half, features), F32), sds((half, features), BF16)],
        compiler_params=params(),
        name="expert",
    )(*pieces, *gate_up, down_proj)


def combine_kernel(planes, cap, me, ids, weights, own_ref, *refs):
    received = refs[: planes - 1]
    resid_ref, out_ref, table, mixed = refs[planes - 1 :]
    table[:cap, :] = own_ref[...]
    for k, ref in enumerate(received):
        table[(k + 1) * cap : (k + 2) * cap, :] = ref[...].astype(F32)
    rows, picks = ids.shape
    plane = me[0] // 8
    for r in range(rows):
        total = None
        for t in range(picks):
            expert_id = ids[r, t]
            seen = jnp.int32(0)
            for b in range(r):
                for u in range(picks):
                    seen = seen + (ids[b, u] == expert_id).astype(jnp.int32)
            place = (expert_id ^ plane) * cap + seen
            term = weights[r, t] * table[pl.ds(place, 1), :]
            total = term if total is None else total + term
        mixed[r : r + 1, :] = total
    out_ref[...] = (resid_ref[...].astype(F32) + mixed[...]).astype(BF16)


def combine(me, ids, weights, own, received, resid, planes, cap):
    rows, features = resid.shape
    vec = pl.BlockSpec(memory_space=pltpu.VMEM)
    return pl.pallas_call(
        functools.partial(combine_kernel, planes, cap),
        in_specs=[SCALARS] * 3 + [vec] * (1 + planes),
        out_specs=vec,
        out_shape=sds((rows, features), BF16),
        scratch_shapes=[
            pltpu.VMEM((planes * cap, features), F32),
            pltpu.VMEM((rows, features), F32),
        ],
        compiler_params=params(),
        name="combine",
    )(me, ids, weights, own, *received, resid)


def body(
    queries,
    latent_cache,
    lengths,
    hidden_in,
    route_ids,
    route_weights,
    value_up,
    out_proj,
    norm_gain,
    gate_up,
    down_proj,
):
    devices = lax.axis_size("dp")
    planes = devices // SPLIT
    rows = hidden_in.shape[0]
    picks = route_ids.shape[1]
    cap = max(2, (rows * picks + planes - 1) // planes)
    me = lax.axis_index("dp").astype(jnp.int32).reshape(1)

    def swap(x, mask):
        return lax.ppermute(x, "dp", [(i, i ^ mask) for i in range(devices)])

    def over_chips(messages):
        return [swap(x, k << 1) for k, x in enumerate(messages, 1)]

    def over_planes(messages):
        return [swap(x, k << 3) for k, x in enumerate(messages, 1)]

    latents = attention(queries, latent_cache, lengths)
    by_heads = lax.all_to_all(latents, "dp", split_axis=0, concat_axis=0, tiled=True)
    own, other = project(me, by_heads, value_up, out_proj, planes, rows)
    own, *out = add_and_cut(own, [swap(other, 1)], 4, "add_core")
    own, *out = add_and_cut(own, over_chips(out), planes, "add_chips")
    sums = [own] + over_planes(out)
    resid, mine, *out = norm_and_pack(
        me, route_ids, sums, hidden_in, norm_gain[None], planes, cap
    )
    gate_up, (down_proj,) = fetch([gate_up, down_proj], [(0, 2), (0, 1)], resid)
    picked = stack([mine] + over_planes(out), gate_up[:1])
    chips = [picked] + over_chips([picked] * 3)
    pieces = chips + [swap(x, 1) for x in chips]
    own, other = expert(pieces, gate_up, down_proj)
    own, *out = add_and_cut(own, [swap(other, 1)], 4, "add_expert_core")
    own, *out = add_and_cut(own, over_chips(out), planes, "add_expert_chips")
    return combine(me, route_ids, route_weights, own, over_planes(out), resid, planes, cap)


def solution(mesh):
    placed = (
        P(("groups", "dp"), None, None),
        P(("groups", "dp"), None, None),
        P(("groups", "dp")),
        P(("groups", "dp"), None),
        P(("groups", "dp"), None),
        P(("groups", "dp"), None),
        P("dp", None, None),
        P("dp", None),
        P(),
        P(None, None, "dp"),
        P("dp", None),
    )
    return jax.shard_map(
        body, mesh=mesh, in_specs=placed, out_specs=P(("groups", "dp"), None), check_vma=False
    )
```

```python
import functools

import jax
import jax.numpy as jnp
from jax import lax
from jax.experimental import pallas as pl
from jax.experimental.pallas import tpu as pltpu
from jax.sharding import PartitionSpec as P

LAT = 512
ROPE = 64
VH = 128
SPLIT = 8

MASKED = -1e30
EPSILON = 1e-06
VMEM = 24 * 1024 * 1024

F32 = jnp.float32
BF16 = jnp.bfloat16
SCALARS = pl.BlockSpec(memory_space=pltpu.SMEM)


def sds(shape, dtype):
    return jax.ShapeDtypeStruct(shape, dtype)


def params():
    return pltpu.CompilerParams(vmem_limit_bytes=VMEM)


def in_hbm(x):
    return pltpu.with_memory_space_constraint(x, pltpu.HBM)


def whole(shape):
    return pl.BlockSpec(shape, lambda *_: (0,) * len(shape))


def attention_kernel(lengths, q_hbm, k_hbm, o_ref, queries, keys, lat, sems):
    rows, _, heads = queries.shape
    copies = []
    for r in range(rows):
        for n, (src, dst) in enumerate(((q_hbm, queries), (k_hbm, keys))):
            copy = pltpu.make_async_copy(src.at[r], dst.at[r], sems.at[2 * r + n])
            copy.start()
            copies.append(copy)
    for r in range(rows):
        copies[2 * r].wait()
        copies[2 * r + 1].wait()
        scores = lax.dot_general(
            queries[r], keys[r], (((0,), (0,)), ((), ())), preferred_element_type=F32
        ) * ((VH + ROPE) ** -0.5)
        position = lax.broadcasted_iota(jnp.int32, scores.shape, 1)
        scores = jnp.where(position < lengths[r], scores, MASKED)
        terms = jnp.exp(scores - jnp.max(scores, axis=1, keepdims=True))
        total = jnp.sum(terms, axis=1, keepdims=True)
        numerator = lax.dot_general(
            terms.astype(BF16), keys[r, :LAT], (((1,), (1,)), ((), ())), preferred_element_type=F32
        )
        lat[r * heads : (r + 1) * heads, :] = (numerator / total).astype(BF16)
    size = rows * heads
    i = lax.broadcasted_iota(jnp.int32, (size, 1), 0)
    k = lax.broadcasted_iota(jnp.int32, (size, size), 1)
    pick = jnp.where(k == (i % rows) * heads + i // rows, 1.0, 0.0).astype(BF16)
    o_ref[...] = jnp.dot(pick, lat[...], preferred_element_type=F32).astype(BF16)


def attention(queries, latent_cache, lengths):
    rows, heads, width = queries.shape
    slots = latent_cache.shape[1]
    hbm = pl.BlockSpec(memory_space=pltpu.HBM)
    return pl.pallas_call(
        attention_kernel,
        in_specs=[SCALARS, hbm, hbm],
        out_specs=pl.BlockSpec(memory_space=pltpu.VMEM),
        out_shape=sds((rows * heads, LAT), BF16),
        scratch_shapes=[
            pltpu.VMEM((rows, width, heads), BF16),
            pltpu.VMEM((rows, width, slots), BF16),
            pltpu.VMEM((rows * heads, LAT), BF16),
            pltpu.SemaphoreType.DMA((2 * rows,)),
        ],
        compiler_params=params(),
        name="latent_attention",
    )(
        lengths,
        in_hbm(jnp.swapaxes(queries, 1, 2)),
        in_hbm(jnp.swapaxes(latent_cache, 1, 2)),
    )


def fetch_kernel(parts, *refs):
    count = len(parts)
    ins, outs, sems = refs[:count], refs[count + 1 : -1], refs[-1]
    copies = []
    for ref, (axis, cuts) in zip(ins, parts):
        size = ref.shape[axis] // cuts
        for c in range(cuts):
            at = (slice(None),) * axis + (pl.ds(c * size, size),)
            src = ref.at[c] if axis == 0 and size == 1 else ref.at[at]
            n = len(copies)
            copies.append(pltpu.make_async_copy(src, outs[n], sems.at[n]))
    for copy in copies:
        copy.start()
    for copy in copies:
        copy.wait()


def fetch(weights, parts, after):
    shapes = []
    for w, (axis, cuts) in zip(weights, parts):
        shape = list(w.shape)
        shape[axis] //= cuts
        if shape[0] == 1:
            shape = shape[1:]
        shapes += [pltpu.VMEM(tuple(shape), w.dtype)] * cuts
    out = pl.pallas_call(
        functools.partial(fetch_kernel, parts),
        in_specs=[pl.BlockSpec(memory_space=pltpu.HBM)] * len(weights)
        + [pl.BlockSpec(memory_space=pl.ANY)],
        out_specs=[pl.BlockSpec(memory_space=pltpu.VMEM)] * len(shapes),
        out_shape=shapes,
        scratch_shapes=[pltpu.SemaphoreType.DMA((len(shapes),))],
        compiler_params=params(),
        name="fetch_weights",
    )(*[in_hbm(w) for w in weights], after)
    result = []
    for _, cuts in parts:
        result.append(out[:cuts])
        out = out[cuts:]
    return result


def project_kernel(planes, rows, tiles, me, x_ref, v_ref, w_hbm, *refs):
    own_ref, other_ref, flat, w, sems = refs[-5:]
    tile = w.shape[2]
    copies = []
    for t in range(tiles):
        copy = pltpu.make_async_copy(w_hbm.at[:, pl.ds(t * tile, tile)], w.at[t], sems.at[t])
        copy.start()
        copies.append(copy)
    heads = v_ref.shape[0]
    count = flat.shape[0]
    i = lax.broadcasted_iota(jnp.int32, (count, 1), 0)
    k = lax.broadcasted_iota(jnp.int32, (count, x_ref.shape[0]), 1)
    plane = (i // rows) % planes
    rest = i // (rows * planes)
    home = me[0] ^ (plane * 8 + (rest % 4) * 2 + rest // 4)
    target = home * (heads * rows) + i % rows
    for h in range(heads):
        pick = jnp.where(k == target + h * rows, 1.0, 0.0).astype(BF16)
        mine = jnp.dot(pick, x_ref[...], preferred_element_type=F32).astype(BF16)
        flat[:, h * VH : (h + 1) * VH] = jnp.dot(
            mine, v_ref[h], preferred_element_type=F32
        ).astype(BF16)
    half = count // 2
    for t in range(tiles):
        copies[t].wait()
        at = slice(t * tile, (t + 1) * tile)
        out = jnp.dot(flat[...], w[t], preferred_element_type=F32)
        own_ref[:, at] = out[:half]
        other_ref[:, at] = out[half:].astype(BF16)


def project(me, by_heads, value_up, out_proj, planes, rows, after, tiles=7):
    count = planes * 8 * rows
    depth, features = out_proj.shape
    half = count // 2
    vec = pl.BlockSpec(memory_space=pltpu.VMEM)
    return pl.pallas_call(
        functools.partial(project_kernel, planes, rows, tiles),
        in_specs=[SCALARS, vec, vec, pl.BlockSpec(memory_space=pltpu.HBM)]
        + [pl.BlockSpec(memory_space=pl.ANY)] * len(after),
        out_specs=[vec, vec],
        out_shape=[sds((half, features), F32), sds((half, features), BF16)],
        scratch_shapes=[
            pltpu.VMEM((count, depth), BF16),
            pltpu.VMEM((tiles, depth, features // tiles), BF16),
            pltpu.SemaphoreType.DMA((tiles,)),
        ],
        compiler_params=params(),
        name="projections",
    )(me, by_heads, value_up, in_hbm(out_proj), *after)


def add_kernel(arrived, parts, tile, *refs):
    outs = refs[-parts:]
    size = outs[0].shape[0]
    for start in range(0, outs[0].shape[1], tile):
        at = slice(start, start + tile)
        for p in range(parts):
            rows = slice(p * size, (p + 1) * size)
            if arrived and size % 16 == 0:
                total = refs[0][rows, at]
                for ref in refs[1 : 1 + arrived]:
                    total = total + ref[rows, at].astype(F32)
            else:
                if p == 0:
                    full = refs[0][:, at]
                    for ref in refs[1 : 1 + arrived]:
                        full = full + ref[:, at].astype(F32)
                total = full[rows]
            outs[p][:, at] = total if p == 0 else total.astype(BF16)


def add_and_cut(own, received, parts, name, after=()):
    count, features = own.shape
    size = count // parts
    vec = pl.BlockSpec(memory_space=pltpu.VMEM)
    return pl.pallas_call(
        functools.partial(add_kernel, len(received), parts, 512),
        in_specs=[vec] * (1 + len(received)) + [pl.BlockSpec(memory_space=pl.ANY)] * len(after),
        out_specs=[vec] * parts,
        out_shape=[sds((size, features), F32)] + [sds((size, features), BF16)] * (parts - 1),
        compiler_params=params(),
        name=name,
    )(own, *received, *after)


def routes_kernel(ids, weights, unused, out_ref):
    rows, picks = ids.shape
    i = lax.broadcasted_iota(jnp.int32, out_ref.shape, 0)
    k = lax.broadcasted_iota(jnp.int32, out_ref.shape, 1)
    table = jnp.zeros(out_ref.shape, F32)
    for r in range(rows):
        for t in range(picks):
            table = jnp.where((i == r) & (k == t), ids[r, t].astype(F32), table)
            table = jnp.where((i == r) & (k == picks + t), weights[r, t], table)
    out_ref[...] = table


def routes(ids, weights, after):
    return pl.pallas_call(
        routes_kernel,
        in_specs=[SCALARS, SCALARS, pl.BlockSpec(memory_space=pl.ANY)],
        out_specs=pl.BlockSpec(memory_space=pltpu.VMEM),
        out_shape=sds((8, 128), F32),
        compiler_params=params(),
        name="routes",
    )(ids, weights, after)


def column(values, count):
    i = lax.broadcasted_iota(jnp.int32, (count, 1), 0)
    out = jnp.full((count, 1), values[0])
    for n, value in enumerate(values[1:], 1):
        out = jnp.where(i == n, value, out)
    return out


def tables_kernel(rows, picks, planes, cap, me, ids, *refs):
    homes = refs[:planes]
    pick_ref, weight_ref, merge_ref = refs[planes:]
    plane = me[0] // 8
    found = {}
    for k in range(planes):
        expert = (plane ^ k).astype(F32)
        for h in range(planes):
            home = homes[h]
            places = [jnp.int32(-1)] * cap
            scales = [jnp.float32(0.0)] * cap
            seen = jnp.int32(0)
            for r in range(rows):
                has = home[r, 0] == expert
                scale = home[r, picks]
                for t in range(1, picks):
                    here = home[r, t] == expert
                    scale = jnp.where(here, home[r, picks + t], scale)
                    has = has | here
                for s in range(cap):
                    hit = has & (seen == s)
                    places[s] = jnp.where(hit, h * rows + r, places[s])
                    scales[s] = jnp.where(hit, scale, scales[s])
                seen = seen + has.astype(jnp.int32)
            found[k, h] = places, scales
    sources = [p for k in range(planes) for j in range(planes) for p in found[k, j ^ k][0]]
    scales = [w for j in range(planes) for w in found[0, j][1]]
    lane = lax.broadcasted_iota(jnp.int32, pick_ref.shape, 1)
    pick_ref[...] = jnp.where(lane == column(sources, len(sources)), 1.0, 0.0)
    weight_ref[...] = jnp.broadcast_to(column(scales, len(scales)), weight_ref.shape)
    lane = lax.broadcasted_iota(jnp.int32, merge_ref.shape, 1)
    merge = jnp.zeros(merge_ref.shape, jnp.bool_)
    for t in range(picks):
        slots = []
        for r in range(rows):
            seen = jnp.int32(0)
            for b in range(r):
                for u in range(picks):
                    seen = seen + (ids[b, u] == ids[r, t]).astype(jnp.int32)
            slots.append((ids[r, t] ^ plane) * cap + seen)
        merge = merge | (lane == column(slots, rows))
    merge_ref[...] = jnp.where(merge, 1.0, 0.0).astype(BF16)


def tables(me, ids, homes, cap):
    rows, picks = ids.shape
    planes = len(homes)
    vec = pl.BlockSpec(memory_space=pltpu.VMEM)
    return pl.pallas_call(
        functools.partial(tables_kernel, rows, picks, planes, cap),
        in_specs=[SCALARS] * (2 + planes),
        out_specs=[vec] * 3,
        out_shape=[
            sds((planes * planes * cap, planes * rows), F32),
            sds((planes * cap, 128), F32),
            sds((rows, planes * cap), BF16),
        ],
        compiler_params=params(),
        name="route_tables",
    )(me, ids, *homes)


def pick_rows(pick, values):
    high = values.astype(BF16)
    low = (values - high.astype(F32)).astype(BF16)
    return jnp.dot(pick, high, preferred_element_type=F32) + jnp.dot(
        pick, low, preferred_element_type=F32
    )


def add_and_pick_kernel(planes, tile, own_ref, a_ref, b_ref, c_ref, hidden_ref, pick_ref, *outs):
    size = outs[0].shape[0]
    rows = hidden_ref.shape[0]
    pick = pick_ref[...]
    near, far = pick[:size].astype(BF16), pick[size:].astype(BF16)
    for start in range(0, own_ref.shape[1], tile):
        at = slice(start, start + tile)
        total = own_ref[:, at]
        for ref in (a_ref, b_ref, c_ref):
            total = total + ref[:, at].astype(F32)
        home = total[:rows] + hidden_ref[:, at].astype(F32)
        total = jnp.concatenate([home, total[rows:]], axis=0)
        outs[0][:, at] = pick_rows(near, total)
        others = jnp.dot(far, total.astype(BF16), preferred_element_type=F32)
        for k in range(1, planes):
            outs[k][:, at] = others[(k - 1) * size : k * size].astype(BF16)


def add_and_pick(own, received, hidden, pick, planes):
    features = own.shape[1]
    size = pick.shape[0] // planes
    vec = pl.BlockSpec(memory_space=pltpu.VMEM)
    return pl.pallas_call(
        functools.partial(add_and_pick_kernel, planes, 1024),
        in_specs=[vec] * 6,
        out_specs=[vec] * planes,
        out_shape=[sds((size, features), F32)] + [sds((size, features), BF16)] * (planes - 1),
        compiler_params=params(),
        name="add_chips",
    )(own, *received, hidden, pick)


def norm_kernel(planes, *refs):
    gain_ref, resid_ref, normed_ref = refs[planes], refs[-2], refs[-1]
    total = refs[0][...]
    for ref in refs[1:planes]:
        total = total + ref[...].astype(F32)
    resid = total.astype(BF16)
    resid_ref[...] = resid
    wide = resid.astype(F32)
    scale = lax.rsqrt(jnp.mean(wide * wide, axis=1, keepdims=True) + EPSILON)
    normed_ref[...] = (wide * scale * gain_ref[...].astype(F32)).astype(BF16)


def norm(sums, gain, after):
    vec = pl.BlockSpec(memory_space=pltpu.VMEM)
    shape = sums[0].shape
    return pl.pallas_call(
        functools.partial(norm_kernel, len(sums)),
        in_specs=[vec] * (1 + len(sums)) + [pl.BlockSpec(memory_space=pl.ANY)] * len(after),
        out_specs=[vec, vec],
        out_shape=[sds(shape, BF16), sds(shape, BF16)],
        compiler_params=params(),
        name="norm",
    )(*sums, gain, *after)


def expert_kernel(pieces, tiles, *refs):
    xs = refs[:pieces]
    gate_ref, up_ref, down_ref, own_ref, other_ref = refs[pieces:]
    tile = down_ref.shape[1] // tiles
    gate, up = 0.0, 0.0
    for t in range(tiles):
        at = slice(t * tile, (t + 1) * tile)
        x = jnp.concatenate([ref[:, at].astype(F32) for ref in xs], axis=0).astype(BF16)
        gate += jnp.dot(x, gate_ref[at, :], preferred_element_type=F32)
        up += jnp.dot(x, up_ref[at, :], preferred_element_type=F32)
    act = (gate / (1.0 + jnp.exp(-gate)) * up).astype(BF16)
    half = act.shape[0] // 2
    for t in range(tiles):
        at = slice(t * tile, (t + 1) * tile)
        out = jnp.dot(act, down_ref[:, at], preferred_element_type=F32)
        own_ref[:, at] = out[:half]
        other_ref[:, at] = out[half:].astype(BF16)


def expert(pieces, gate_up, down_proj, tiles=7):
    size, features = pieces[0].shape
    half = size * len(pieces) // 2
    vec = pl.BlockSpec(memory_space=pltpu.VMEM)
    return pl.pallas_call(
        functools.partial(expert_kernel, len(pieces), tiles),
        in_specs=[vec] * (len(pieces) + 3),
        out_specs=[vec, vec],
        out_shape=[sds((half, features), F32), sds((half, features), BF16)],
        compiler_params=params(),
        name="expert",
    )(*pieces, *gate_up, down_proj)


def weigh_kernel(planes, share, tile, own_ref, a_ref, b_ref, c_ref, resid_ref, weight_ref, *outs):
    cap = outs[0].shape[0]
    for start in range(0, own_ref.shape[1], tile):
        at = slice(start, start + tile)
        total = own_ref[:, at]
        for ref in (a_ref, b_ref, c_ref):
            total = total + ref[:, at].astype(F32)
        total = total * weight_ref[:, :1] + resid_ref[:, at].astype(F32) * share
        outs[0][:, at] = total[:cap]
        for k in range(1, planes):
            outs[k][:, at] = total[k * cap : (k + 1) * cap].astype(BF16)


def weigh(own, received, resid, weight, planes, picks):
    count, features = own.shape
    cap = count // planes
    vec = pl.BlockSpec(memory_space=pltpu.VMEM)
    return pl.pallas_call(
        functools.partial(weigh_kernel, planes, 1.0 / picks, 1024),
        in_specs=[vec] * 6,
        out_specs=[vec] * planes,
        out_shape=[sds((cap, features), F32)] + [sds((cap, features), BF16)] * (planes - 1),
        compiler_params=params(),
        name="weigh",
    )(own, *received, resid, weight)


def combine_kernel(planes, merge_ref, *refs):
    out_ref = refs[planes]
    table = jnp.concatenate([ref[...].astype(F32) for ref in refs[:planes]], axis=0)
    out_ref[...] = pick_rows(merge_ref[...], table).astype(BF16)


def combine(merge, pieces):
    vec = pl.BlockSpec(memory_space=pltpu.VMEM)
    return pl.pallas_call(
        functools.partial(combine_kernel, len(pieces)),
        in_specs=[vec] * (1 + len(pieces)),
        out_specs=vec,
        out_shape=sds((merge.shape[0], pieces[0].shape[1]), BF16),
        compiler_params=params(),
        name="combine",
    )(merge, *pieces)


def body(
    queries,
    latent_cache,
    lengths,
    hidden_in,
    route_ids,
    route_weights,
    value_up,
    out_proj,
    norm_gain,
    gate_up,
    down_proj,
):
    devices = lax.axis_size("dp")
    planes = devices // SPLIT
    rows = hidden_in.shape[0]
    picks = route_ids.shape[1]
    cap = max(2, (rows * picks + planes - 1) // planes)
    me = lax.axis_index("dp").astype(jnp.int32).reshape(1)

    def swap(x, mask):
        return lax.ppermute(x, "dp", [(i, i ^ mask) for i in range(devices)])

    def over_chips(messages):
        return [swap(x, k << 1) for k, x in enumerate(messages, 1)]

    def over_planes(messages):
        return [swap(x, k << 3) for k, x in enumerate(messages, 1)]

    latents = attention(queries, latent_cache, lengths)
    by_heads = lax.all_to_all(latents, "dp", split_axis=0, concat_axis=0, tiled=True)
    mine = routes(route_ids, route_weights, latents)
    pick, weight, merge = tables(me, route_ids, [mine] + over_planes([mine] * (planes - 1)), cap)
    own, other = project(me, by_heads, value_up, out_proj, planes, rows, [pick])
    own, *out = add_and_cut(own, [swap(other, 1)], 4, "add_core")
    own, *out = add_and_pick(own, over_chips(out), hidden_in, pick, planes)
    gate_up, (down_proj,) = fetch([gate_up, down_proj], [(0, 2), (0, 1)], own)
    resid, picked = norm([own] + over_planes(out), norm_gain[None], gate_up[:1])
    chips = [picked] + over_chips([picked] * 3)
    pieces = chips + [swap(x, 1) for x in chips]
    own, other = expert(pieces, gate_up, down_proj)
    own, *out = add_and_cut(own, [swap(other, 1)], 4, "add_expert_core")
    own, *out = weigh(own, over_chips(out), resid, weight, planes, picks)
    return combine(merge, [own] + over_planes(out))


def solution(mesh):
    placed = (
        P(("groups", "dp"), None, None),
        P(("groups", "dp"), None, None),
        P(("groups", "dp")),
        P(("groups", "dp"), None),
        P(("groups", "dp"), None),
        P(("groups", "dp"), None),
        P("dp", None, None),
        P("dp", None),
        P(),
        P(None, None, "dp"),
        P("dp", None),
    )
    return jax.shard_map(
        body, mesh=mesh, in_specs=placed, out_specs=P(("groups", "dp"), None), check_vma=False
    )
```

```python
import functools

import jax
import jax.numpy as jnp
from jax import lax
from jax.experimental import pallas as pl
from jax.experimental.pallas import tpu as pltpu
from jax.sharding import PartitionSpec as P

LAT = 512
ROPE = 64
VH = 128
SPLIT = 8

MASKED = -1e30
EPSILON = 1e-06
VMEM = 24 * 1024 * 1024
TILES = 7
EARLY = 3

F32 = jnp.float32
BF16 = jnp.bfloat16
SCALARS = pl.BlockSpec(memory_space=pltpu.SMEM)


def sds(shape, dtype):
    return jax.ShapeDtypeStruct(shape, dtype)


def params():
    return pltpu.CompilerParams(vmem_limit_bytes=VMEM)


def in_hbm(x):
    return pltpu.with_memory_space_constraint(x, pltpu.HBM)


def whole(shape):
    return pl.BlockSpec(shape, lambda *_: (0,) * len(shape))


def attention_kernel(planes, me, lengths_hbm, q_hbm, k_hbm, *refs):
    outs = refs[:planes]
    lengths, queries, keys, lat, sems = refs[planes:]
    rows, _, heads = queries.shape
    live = pltpu.make_async_copy(lengths_hbm, lengths, sems.at[2 * rows])
    live.start()
    copies = []
    for r in range(rows):
        for n, (src, dst) in enumerate(((q_hbm, queries), (k_hbm, keys))):
            copy = pltpu.make_async_copy(src.at[r], dst.at[r], sems.at[2 * r + n])
            copy.start()
            copies.append(copy)
    live.wait()
    for r in range(rows):
        copies[2 * r].wait()
        copies[2 * r + 1].wait()
        scores = lax.dot_general(
            queries[r], keys[r], (((0,), (0,)), ((), ())), preferred_element_type=F32
        ) * ((VH + ROPE) ** -0.5)
        position = lax.broadcasted_iota(jnp.int32, scores.shape, 1)
        scores = jnp.where(position < lengths[r], scores, MASKED)
        terms = jnp.exp(scores - jnp.max(scores, axis=1, keepdims=True))
        total = jnp.sum(terms, axis=1, keepdims=True)
        numerator = lax.dot_general(
            terms.astype(BF16), keys[r, :LAT], (((1,), (1,)), ((), ())), preferred_element_type=F32
        )
        lat[r * heads : (r + 1) * heads, :] = (numerator / total).astype(BF16)
    each = heads // (planes * 8)
    size = rows * heads // planes
    i = lax.broadcasted_iota(jnp.int32, (size, 1), 0)
    k = lax.broadcasted_iota(jnp.int32, (size, rows * heads), 1)
    unit = i // (rows * each)
    for p in range(planes):
        head = (me[0] ^ (p * 8 + unit)) * each + (i // rows) % each
        pick = jnp.where(k == (i % rows) * heads + head, 1.0, 0.0).astype(BF16)
        outs[p][...] = jnp.dot(pick, lat[...], preferred_element_type=F32).astype(BF16)


def attention(me, queries, latent_cache, lengths, planes):
    rows, heads, width = queries.shape
    slots = latent_cache.shape[1]
    hbm = pl.BlockSpec(memory_space=pltpu.HBM)
    return pl.pallas_call(
        functools.partial(attention_kernel, planes),
        in_specs=[SCALARS, hbm, hbm, hbm],
        out_specs=[pl.BlockSpec(memory_space=pltpu.VMEM)] * planes,
        out_shape=[sds((rows * heads // planes, LAT), BF16)] * planes,
        scratch_shapes=[
            pltpu.SMEM((rows,), jnp.int32),
            pltpu.VMEM((rows, width, heads), BF16),
            pltpu.VMEM((rows, width, slots), BF16),
            pltpu.VMEM((rows * heads, LAT), BF16),
            pltpu.SemaphoreType.DMA((2 * rows + 1,)),
        ],
        compiler_params=params(),
        name="latent_attention",
    )(
        me,
        in_hbm(lengths),
        in_hbm(jnp.swapaxes(queries, 1, 2)),
        in_hbm(jnp.swapaxes(latent_cache, 1, 2)),
    )


def regroup_kernel(planes, chips, *refs):
    outs = refs[-chips:]
    size = refs[0].shape[0] // chips
    for q in range(chips):
        for p in range(planes):
            outs[q][p * size : (p + 1) * size, :] = refs[p][q * size : (q + 1) * size, :]


def regroup(pieces, chips, after):
    vec = pl.BlockSpec(memory_space=pltpu.VMEM)
    planes = len(pieces)
    size, width = pieces[0].shape
    return pl.pallas_call(
        functools.partial(regroup_kernel, planes, chips),
        in_specs=[vec] * planes + [pl.BlockSpec(memory_space=pl.ANY)] * len(after),
        out_specs=[vec] * chips,
        out_shape=[sds((planes * size // chips, width), BF16)] * chips,
        compiler_params=params(),
        name="regroup",
    )(*pieces, *after)


def fetch_kernel(parts, *refs):
    count = len(parts)
    ins, outs, sems = refs[:count], refs[count + 1 : -1], refs[-1]
    copies = []
    for ref, (axis, cuts, taken) in zip(ins, parts):
        size = ref.shape[axis] // cuts
        for c in range(taken):
            at = (slice(None),) * axis + (pl.ds(c * size, size),)
            src = ref.at[c] if axis == 0 and size == 1 else ref.at[at]
            n = len(copies)
            copies.append(pltpu.make_async_copy(src, outs[n], sems.at[n]))
    for copy in copies:
        copy.start()
    for copy in copies:
        copy.wait()


def fetch(weights, parts, after, name):
    shapes = []
    for w, (axis, cuts, taken) in zip(weights, parts):
        shape = list(w.shape)
        shape[axis] //= cuts
        if shape[0] == 1:
            shape = shape[1:]
        shapes += [pltpu.VMEM(tuple(shape), w.dtype)] * taken
    out = pl.pallas_call(
        functools.partial(fetch_kernel, parts),
        in_specs=[pl.BlockSpec(memory_space=pltpu.HBM)] * len(weights)
        + [pl.BlockSpec(memory_space=pl.ANY)],
        out_specs=[pl.BlockSpec(memory_space=pltpu.VMEM)] * len(shapes),
        out_shape=shapes,
        scratch_shapes=[pltpu.SemaphoreType.DMA((len(shapes),))],
        compiler_params=params(),
        name=name,
    )(*[in_hbm(w) for w in weights], after)
    result = []
    for _, _, taken in parts:
        result.append(list(out[:taken]))
        out = out[taken:]
    return result


def project_kernel(planes, rows, tiles, *refs):
    pieces, v_ref, w_hbm, early = refs[:8], refs[8], refs[9], refs[10 : 10 + EARLY]
    own_ref, other_ref, flat, late, sems = refs[-5:]
    tile = late.shape[2]
    copies = []
    for t in range(EARLY, tiles):
        n = t - EARLY
        copy = pltpu.make_async_copy(w_hbm.at[:, pl.ds(t * tile, tile)], late.at[n], sems.at[n])
        copy.start()
        copies.append(copy)
    heads = v_ref.shape[0]
    half = flat.shape[0] // 2
    i = lax.broadcasted_iota(jnp.int32, (half, 1), 0)
    k = lax.broadcasted_iota(jnp.int32, (half, half * 2 * heads), 1)
    for core in range(2):
        x = jnp.concatenate([ref[...] for ref in pieces[4 * core : 4 * core + 4]], axis=0)
        target = ((i // rows) * 2 + core) * (heads * rows) + i % rows
        for h in range(heads):
            pick = jnp.where(k == target + h * rows, 1.0, 0.0).astype(BF16)
            mine = jnp.dot(pick, x, preferred_element_type=F32).astype(BF16)
            flat[core * half : (core + 1) * half, h * VH : (h + 1) * VH] = jnp.dot(
                mine, v_ref[h], preferred_element_type=F32
            ).astype(BF16)
    for t in range(tiles):
        if t >= EARLY:
            copies[t - EARLY].wait()
        w = early[t][...] if t < EARLY else late[t - EARLY]
        at = slice(t * tile, (t + 1) * tile)
        out = jnp.dot(flat[...], w, preferred_element_type=F32)
        own_ref[:, at] = out[:half]
        other_ref[:, at] = out[half:].astype(BF16)


def project(pieces, value_up, early, out_proj, planes, rows):
    count = planes * 8 * rows
    depth, features = out_proj.shape
    tile = features // TILES
    half = count // 2
    vec = pl.BlockSpec(memory_space=pltpu.VMEM)
    return pl.pallas_call(
        functools.partial(project_kernel, planes, rows, TILES),
        in_specs=[vec] * 9
        + [pl.BlockSpec(memory_space=pltpu.HBM)]
        + [vec] * EARLY,
        out_specs=[vec, vec],
        out_shape=[sds((half, features), F32), sds((half, features), BF16)],
        scratch_shapes=[
            pltpu.VMEM((count, depth), BF16),
            pltpu.VMEM((TILES - EARLY, depth, tile), BF16),
            pltpu.SemaphoreType.DMA((TILES - EARLY,)),
        ],
        compiler_params=params(),
        name="projections",
    )(*pieces, value_up, in_hbm(out_proj), *early)


def add_kernel(arrived, parts, tile, *refs):
    outs = refs[-parts:]
    size = outs[0].shape[0]
    for start in range(0, outs[0].shape[1], tile):
        at = slice(start, start + tile)
        for p in range(parts):
            rows = slice(p * size, (p + 1) * size)
            if arrived and size % 16 == 0:
                total = refs[0][rows, at]
                for ref in refs[1 : 1 + arrived]:
                    total = total + ref[rows, at].astype(F32)
            else:
                if p == 0:
                    full = refs[0][:, at]
                    for ref in refs[1 : 1 + arrived]:
                        full = full + ref[:, at].astype(F32)
                total = full[rows]
            outs[p][:, at] = total if p == 0 else total.astype(BF16)


def add_and_cut(own, received, parts, name, after=()):
    count, features = own.shape
    size = count // parts
    vec = pl.BlockSpec(memory_space=pltpu.VMEM)
    return pl.pallas_call(
        functools.partial(add_kernel, len(received), parts, 512),
        in_specs=[vec] * (1 + len(received)) + [pl.BlockSpec(memory_space=pl.ANY)] * len(after),
        out_specs=[vec] * parts,
        out_shape=[sds((size, features), F32)] + [sds((size, features), BF16)] * (parts - 1),
        compiler_params=params(),
        name=name,
    )(own, *received, *after)


def routes_kernel(ids, weights, unused, out_ref):
    rows, picks = ids.shape
    i = lax.broadcasted_iota(jnp.int32, out_ref.shape, 0)
    k = lax.broadcasted_iota(jnp.int32, out_ref.shape, 1)
    table = jnp.zeros(out_ref.shape, F32)
    for r in range(rows):
        for t in range(picks):
            table = jnp.where((i == r) & (k == t), ids[r, t].astype(F32), table)
            table = jnp.where((i == r) & (k == picks + t), weights[r, t], table)
    out_ref[...] = table


def routes(ids, weights, after):
    return pl.pallas_call(
        routes_kernel,
        in_specs=[SCALARS, SCALARS, pl.BlockSpec(memory_space=pl.ANY)],
        out_specs=pl.BlockSpec(memory_space=pltpu.VMEM),
        out_shape=sds((8, 128), F32),
        compiler_params=params(),
        name="routes",
    )(ids, weights, after)


def column(values, count):
    i = lax.broadcasted_iota(jnp.int32, (count, 1), 0)
    out = jnp.full((count, 1), values[0])
    for n, value in enumerate(values[1:], 1):
        out = jnp.where(i == n, value, out)
    return out


def tables_kernel(rows, picks, planes, cap, me, ids, *refs):
    homes = refs[:planes]
    pick_ref, weight_ref, merge_ref = refs[planes:]
    plane = me[0] // 8
    found = {}
    for k in range(planes):
        expert = (plane ^ k).astype(F32)
        for h in range(planes):
            home = homes[h]
            places = [jnp.int32(-1)] * cap
            scales = [jnp.float32(0.0)] * cap
            seen = jnp.int32(0)
            for r in range(rows):
                has = home[r, 0] == expert
                scale = home[r, picks]
                for t in range(1, picks):
                    here = home[r, t] == expert
                    scale = jnp.where(here, home[r, picks + t], scale)
                    has = has | here
                for s in range(cap):
                    hit = has & (seen == s)
                    places[s] = jnp.where(hit, h * rows + r, places[s])
                    scales[s] = jnp.where(hit, scale, scales[s])
                seen = seen + has.astype(jnp.int32)
            found[k, h] = places, scales
    sources = [p for k in range(planes) for j in range(planes) for p in found[k, j ^ k][0]]
    scales = [w for j in range(planes) for w in found[0, j][1]]
    lane = lax.broadcasted_iota(jnp.int32, pick_ref.shape, 1)
    pick_ref[...] = jnp.where(lane == column(sources, len(sources)), 1.0, 0.0)
    weight_ref[...] = jnp.broadcast_to(column(scales, len(scales)), weight_ref.shape)
    lane = lax.broadcasted_iota(jnp.int32, merge_ref.shape, 1)
    merge = jnp.zeros(merge_ref.shape, jnp.bool_)
    for t in range(picks):
        slots = []
        for r in range(rows):
            seen = jnp.int32(0)
            for b in range(r):
                for u in range(picks):
                    seen = seen + (ids[b, u] == ids[r, t]).astype(jnp.int32)
            slots.append((ids[r, t] ^ plane) * cap + seen)
        merge = merge | (lane == column(slots, rows))
    merge_ref[...] = jnp.where(merge, 1.0, 0.0).astype(BF16)


def tables(me, ids, homes, cap):
    rows, picks = ids.shape
    planes = len(homes)
    vec = pl.BlockSpec(memory_space=pltpu.VMEM)
    return pl.pallas_call(
        functools.partial(tables_kernel, rows, picks, planes, cap),
        in_specs=[SCALARS] * (2 + planes),
        out_specs=[vec] * 3,
        out_shape=[
            sds((planes * planes * cap, planes * rows), F32),
            sds((planes * cap, 128), F32),
            sds((rows, planes * cap), BF16),
        ],
        compiler_params=params(),
        name="route_tables",
    )(me, ids, *homes)


def pick_rows(pick, values):
    high = values.astype(BF16)
    low = (values - high.astype(F32)).astype(BF16)
    return jnp.dot(pick, high, preferred_element_type=F32) + jnp.dot(
        pick, low, preferred_element_type=F32
    )


def add_and_pick_kernel(planes, tile, own_ref, a_ref, b_ref, c_ref, hidden_ref, pick_ref, *outs):
    size = outs[0].shape[0]
    rows = hidden_ref.shape[0]
    pick = pick_ref[...]
    near, far = pick[:size].astype(BF16), pick[size:].astype(BF16)
    for start in range(0, own_ref.shape[1], tile):
        at = slice(start, start + tile)
        total = own_ref[:, at]
        for ref in (a_ref, b_ref, c_ref):
            total = total + ref[:, at].astype(F32)
        home = total[:rows] + hidden_ref[:, at].astype(F32)
        total = jnp.concatenate([home, total[rows:]], axis=0)
        outs[0][:, at] = pick_rows(near, total)
        others = jnp.dot(far, total.astype(BF16), preferred_element_type=F32)
        for k in range(1, planes):
            outs[k][:, at] = others[(k - 1) * size : k * size].astype(BF16)


def add_and_pick(own, received, hidden, pick, planes):
    features = own.shape[1]
    size = pick.shape[0] // planes
    vec = pl.BlockSpec(memory_space=pltpu.VMEM)
    return pl.pallas_call(
        functools.partial(add_and_pick_kernel, planes, 1024),
        in_specs=[vec] * 6,
        out_specs=[vec] * planes,
        out_shape=[sds((size, features), F32)] + [sds((size, features), BF16)] * (planes - 1),
        compiler_params=params(),
        name="add_chips",
    )(own, *received, hidden, pick)


def norm_kernel(planes, *refs):
    gain_ref, resid_ref, normed_ref = refs[planes], refs[-2], refs[-1]
    total = refs[0][...]
    for ref in refs[1:planes]:
        total = total + ref[...].astype(F32)
    resid = total.astype(BF16)
    resid_ref[...] = resid
    wide = resid.astype(F32)
    scale = lax.rsqrt(jnp.mean(wide * wide, axis=1, keepdims=True) + EPSILON)
    normed_ref[...] = (wide * scale * gain_ref[...].astype(F32)).astype(BF16)


def norm(sums, gain, after):
    vec = pl.BlockSpec(memory_space=pltpu.VMEM)
    shape = sums[0].shape
    return pl.pallas_call(
        functools.partial(norm_kernel, len(sums)),
        in_specs=[vec] * (1 + len(sums)) + [pl.BlockSpec(memory_space=pl.ANY)] * len(after),
        out_specs=[vec, vec],
        out_shape=[sds(shape, BF16), sds(shape, BF16)],
        compiler_params=params(),
        name="norm",
    )(*sums, gain, *after)


def expert_kernel(pieces, tiles, *refs):
    xs = refs[:pieces]
    gate_ref, up_ref, down_ref, own_ref, other_ref = refs[pieces:]
    tile = down_ref.shape[1] // tiles
    gate, up = 0.0, 0.0
    for t in range(tiles):
        at = slice(t * tile, (t + 1) * tile)
        x = jnp.concatenate([ref[:, at].astype(F32) for ref in xs], axis=0).astype(BF16)
        gate += jnp.dot(x, gate_ref[at, :], preferred_element_type=F32)
        up += jnp.dot(x, up_ref[at, :], preferred_element_type=F32)
    act = (gate / (1.0 + jnp.exp(-gate)) * up).astype(BF16)
    half = act.shape[0] // 2
    for t in range(tiles):
        at = slice(t * tile, (t + 1) * tile)
        out = jnp.dot(act, down_ref[:, at], preferred_element_type=F32)
        own_ref[:, at] = out[:half]
        other_ref[:, at] = out[half:].astype(BF16)


def expert(pieces, gate_up, down_proj, tiles=7):
    size, features = pieces[0].shape
    half = size * len(pieces) // 2
    vec = pl.BlockSpec(memory_space=pltpu.VMEM)
    return pl.pallas_call(
        functools.partial(expert_kernel, len(pieces), tiles),
        in_specs=[vec] * (len(pieces) + 3),
        out_specs=[vec, vec],
        out_shape=[sds((half, features), F32), sds((half, features), BF16)],
        compiler_params=params(),
        name="expert",
    )(*pieces, *gate_up, down_proj)


def weigh_kernel(planes, share, tile, own_ref, a_ref, b_ref, c_ref, resid_ref, weight_ref, *outs):
    cap = outs[0].shape[0]
    for start in range(0, own_ref.shape[1], tile):
        at = slice(start, start + tile)
        total = own_ref[:, at]
        for ref in (a_ref, b_ref, c_ref):
            total = total + ref[:, at].astype(F32)
        total = total * weight_ref[:, :1] + resid_ref[:, at].astype(F32) * share
        outs[0][:, at] = total[:cap]
        for k in range(1, planes):
            outs[k][:, at] = total[k * cap : (k + 1) * cap].astype(BF16)


def weigh(own, received, resid, weight, planes, picks):
    count, features = own.shape
    cap = count // planes
    vec = pl.BlockSpec(memory_space=pltpu.VMEM)
    return pl.pallas_call(
        functools.partial(weigh_kernel, planes, 1.0 / picks, 1024),
        in_specs=[vec] * 6,
        out_specs=[vec] * planes,
        out_shape=[sds((cap, features), F32)] + [sds((cap, features), BF16)] * (planes - 1),
        compiler_params=params(),
        name="weigh",
    )(own, *received, resid, weight)


def combine_kernel(planes, merge_ref, *refs):
    out_ref = refs[planes]
    table = jnp.concatenate([ref[...].astype(F32) for ref in refs[:planes]], axis=0)
    out_ref[...] = pick_rows(merge_ref[...], table).astype(BF16)


def combine(merge, pieces):
    vec = pl.BlockSpec(memory_space=pltpu.VMEM)
    return pl.pallas_call(
        functools.partial(combine_kernel, len(pieces)),
        in_specs=[vec] * (1 + len(pieces)),
        out_specs=vec,
        out_shape=sds((merge.shape[0], pieces[0].shape[1]), BF16),
        compiler_params=params(),
        name="combine",
    )(merge, *pieces)


def body(
    queries,
    latent_cache,
    lengths,
    hidden_in,
    route_ids,
    route_weights,
    value_up,
    out_proj,
    norm_gain,
    gate_up,
    down_proj,
):
    devices = lax.axis_size("dp")
    planes = devices // SPLIT
    rows = hidden_in.shape[0]
    picks = route_ids.shape[1]
    cap = max(2, (rows * picks + planes - 1) // planes)
    me = lax.axis_index("dp").astype(jnp.int32).reshape(1)

    def swap(x, mask):
        return lax.ppermute(x, "dp", [(i, i ^ mask) for i in range(devices)])

    def over_chips(messages):
        return [swap(x, k << 1) for k, x in enumerate(messages, 1)]

    def over_planes(messages):
        return [swap(x, k << 3) for k, x in enumerate(messages, 1)]

    latents = attention(me, queries, latent_cache, lengths, planes)
    (early,) = fetch([out_proj], [(1, TILES, EARLY)], latents[0], "fetch_projections")
    by_chip = regroup([latents[0]] + over_planes(latents[1:]), 4, early[:1])
    chips = [by_chip[0]] + over_chips(by_chip[1:])
    pieces = chips + [swap(x, 1) for x in chips]
    own, other = project(pieces, value_up, early, out_proj, planes, rows)
    own, *out = add_and_cut(own, [swap(other, 1)], 4, "add_core")
    mine = routes(route_ids, route_weights, own)
    homes = [mine] + over_planes([mine] * (planes - 1))
    pick, weight, merge = tables(me, route_ids, homes, cap)
    own, *out = add_and_pick(own, over_chips(out), hidden_in, pick, planes)
    gate_up, (down_proj,) = fetch([gate_up, down_proj], [(0, 2, 2), (0, 1, 1)], own, "fetch_experts")
    resid, picked = norm([own] + over_planes(out), norm_gain[None], gate_up[:1])
    chips = [picked] + over_chips([picked] * 3)
    pieces = chips + [swap(x, 1) for x in chips]
    own, other = expert(pieces, gate_up, down_proj)
    own, *out = add_and_cut(own, [swap(other, 1)], 4, "add_expert_core")
    own, *out = weigh(own, over_chips(out), resid, weight, planes, picks)
    return combine(merge, [own] + over_planes(out))


def solution(mesh):
    placed = (
        P(("groups", "dp"), None, None),
        P(("groups", "dp"), None, None),
        P(("groups", "dp")),
        P(("groups", "dp"), None),
        P(("groups", "dp"), None),
        P(("groups", "dp"), None),
        P("dp", None, None),
        P("dp", None),
        P(),
        P(None, None, "dp"),
        P("dp", None),
    )
    return jax.shard_map(
        body, mesh=mesh, in_specs=placed, out_specs=P(("groups", "dp"), None), check_vma=False
    )
```

```python
import functools

import jax
import jax.numpy as jnp
from jax import lax
from jax.experimental import pallas as pl
from jax.experimental.pallas import tpu as pltpu
from jax.sharding import PartitionSpec as P

LAT = 512
ROPE = 64
VH = 128
SPLIT = 8

MASKED = -1e30
EPSILON = 1e-06
VMEM = 24 * 1024 * 1024
TILES = 7
EARLY = 2

F32 = jnp.float32
BF16 = jnp.bfloat16
SCALARS = pl.BlockSpec(memory_space=pltpu.SMEM)


def sds(shape, dtype):
    return jax.ShapeDtypeStruct(shape, dtype)


def params():
    return pltpu.CompilerParams(vmem_limit_bytes=VMEM)


def in_hbm(x):
    return pltpu.with_memory_space_constraint(x, pltpu.HBM)


def whole(shape):
    return pl.BlockSpec(shape, lambda *_: (0,) * len(shape))


def attention_kernel(lengths_hbm, q_hbm, k_hbm, o_ref, lengths, queries, keys, lat, sems):
    rows, _, heads = queries.shape
    live = pltpu.make_async_copy(lengths_hbm, lengths, sems.at[2 * rows])
    live.start()
    copies = []
    for r in range(rows):
        for n, (src, dst) in enumerate(((q_hbm, queries), (k_hbm, keys))):
            copy = pltpu.make_async_copy(src.at[r], dst.at[r], sems.at[2 * r + n])
            copy.start()
            copies.append(copy)
    live.wait()
    for r in range(rows):
        copies[2 * r].wait()
        copies[2 * r + 1].wait()
        scores = lax.dot_general(
            queries[r], keys[r], (((0,), (0,)), ((), ())), preferred_element_type=F32
        ) * ((VH + ROPE) ** -0.5)
        position = lax.broadcasted_iota(jnp.int32, scores.shape, 1)
        scores = jnp.where(position < lengths[r], scores, MASKED)
        terms = jnp.exp(scores - jnp.max(scores, axis=1, keepdims=True))
        total = jnp.sum(terms, axis=1, keepdims=True)
        numerator = lax.dot_general(
            terms.astype(BF16), keys[r, :LAT], (((1,), (1,)), ((), ())), preferred_element_type=F32
        )
        lat[r * heads : (r + 1) * heads, :] = (numerator / total).astype(BF16)
    size = rows * heads
    i = lax.broadcasted_iota(jnp.int32, (size, 1), 0)
    k = lax.broadcasted_iota(jnp.int32, (size, size), 1)
    pick = jnp.where(k == (i % rows) * heads + i // rows, 1.0, 0.0).astype(BF16)
    o_ref[...] = jnp.dot(pick, lat[...], preferred_element_type=F32).astype(BF16)


def attention(queries, latent_cache, lengths):
    rows, heads, width = queries.shape
    slots = latent_cache.shape[1]
    hbm = pl.BlockSpec(memory_space=pltpu.HBM)
    return pl.pallas_call(
        attention_kernel,
        in_specs=[hbm, hbm, hbm],
        out_specs=pl.BlockSpec(memory_space=pltpu.VMEM),
        out_shape=sds((rows * heads, LAT), BF16),
        scratch_shapes=[
            pltpu.SMEM((rows,), jnp.int32),
            pltpu.VMEM((rows, width, heads), BF16),
            pltpu.VMEM((rows, width, slots), BF16),
            pltpu.VMEM((rows * heads, LAT), BF16),
            pltpu.SemaphoreType.DMA((2 * rows + 1,)),
        ],
        compiler_params=params(),
        name="latent_attention",
    )(
        in_hbm(lengths),
        in_hbm(jnp.swapaxes(queries, 1, 2)),
        in_hbm(jnp.swapaxes(latent_cache, 1, 2)),
    )


def fetch_kernel(parts, *refs):
    count = len(parts)
    ins, outs, sems = refs[:count], refs[count + 1 : -1], refs[-1]
    copies = []
    for ref, (axis, cuts, taken) in zip(ins, parts):
        size = ref.shape[axis] // cuts
        for c in range(taken):
            at = (slice(None),) * axis + (pl.ds(c * size, size),)
            src = ref.at[c] if axis == 0 and size == 1 else ref.at[at]
            n = len(copies)
            copies.append(pltpu.make_async_copy(src, outs[n], sems.at[n]))
    for copy in copies:
        copy.start()
    for copy in copies:
        copy.wait()


def fetch(weights, parts, after, name):
    shapes = []
    for w, (axis, cuts, taken) in zip(weights, parts):
        shape = list(w.shape)
        shape[axis] //= cuts
        if shape[0] == 1:
            shape = shape[1:]
        shapes += [pltpu.VMEM(tuple(shape), w.dtype)] * taken
    out = pl.pallas_call(
        functools.partial(fetch_kernel, parts),
        in_specs=[pl.BlockSpec(memory_space=pltpu.HBM)] * len(weights)
        + [pl.BlockSpec(memory_space=pl.ANY)],
        out_specs=[pl.BlockSpec(memory_space=pltpu.VMEM)] * len(shapes),
        out_shape=shapes,
        scratch_shapes=[pltpu.SemaphoreType.DMA((len(shapes),))],
        compiler_params=params(),
        name=name,
    )(*[in_hbm(w) for w in weights], after)
    result = []
    for _, _, taken in parts:
        result.append(list(out[:taken]))
        out = out[taken:]
    return result


def project_kernel(planes, rows, me, x_ref, v_ref, w_hbm, *refs):
    early = refs[:EARLY]
    own_ref, other_ref, flat, late, sems = refs[-5:]
    tile = late.shape[2]
    copies = []
    for t in range(EARLY, TILES):
        n = t - EARLY
        copy = pltpu.make_async_copy(w_hbm.at[:, pl.ds(t * tile, tile)], late.at[n], sems.at[n])
        copy.start()
        copies.append(copy)
    heads = v_ref.shape[0]
    count = flat.shape[0]
    i = lax.broadcasted_iota(jnp.int32, (count, 1), 0)
    k = lax.broadcasted_iota(jnp.int32, (count, x_ref.shape[0]), 1)
    plane = (i // rows) % planes
    rest = i // (rows * planes)
    home = me[0] ^ (plane * 8 + (rest % 4) * 2 + rest // 4)
    target = home * (heads * rows) + i % rows
    for h in range(heads):
        pick = jnp.where(k == target + h * rows, 1.0, 0.0).astype(BF16)
        mine = jnp.dot(pick, x_ref[...], preferred_element_type=F32).astype(BF16)
        flat[:, h * VH : (h + 1) * VH] = jnp.dot(
            mine, v_ref[h], preferred_element_type=F32
        ).astype(BF16)
    half = count // 2
    for t in range(TILES):
        if t >= EARLY:
            copies[t - EARLY].wait()
        w = early[t][...] if t < EARLY else late[t - EARLY]
        at = slice(t * tile, (t + 1) * tile)
        out = jnp.dot(flat[...], w, preferred_element_type=F32)
        own_ref[:, at] = out[:half]
        other_ref[:, at] = out[half:].astype(BF16)


def project(me, by_heads, value_up, out_proj, early, planes, rows, after):
    count = planes * 8 * rows
    depth, features = out_proj.shape
    half = count // 2
    vec = pl.BlockSpec(memory_space=pltpu.VMEM)
    return pl.pallas_call(
        functools.partial(project_kernel, planes, rows),
        in_specs=[SCALARS, vec, vec, pl.BlockSpec(memory_space=pltpu.HBM)]
        + [vec] * EARLY
        + [pl.BlockSpec(memory_space=pl.ANY)] * len(after),
        out_specs=[vec, vec],
        out_shape=[sds((half, features), F32), sds((half, features), BF16)],
        scratch_shapes=[
            pltpu.VMEM((count, depth), BF16),
            pltpu.VMEM((TILES - EARLY, depth, features // TILES), BF16),
            pltpu.SemaphoreType.DMA((TILES - EARLY,)),
        ],
        compiler_params=params(),
        name="projections",
    )(me, by_heads, value_up, in_hbm(out_proj), *early, *after)


def add_kernel(arrived, parts, tile, *refs):
    outs = refs[-parts:]
    size = outs[0].shape[0]
    for start in range(0, outs[0].shape[1], tile):
        at = slice(start, start + tile)
        for p in range(parts):
            rows = slice(p * size, (p + 1) * size)
            if arrived and size % 16 == 0:
                total = refs[0][rows, at]
                for ref in refs[1 : 1 + arrived]:
                    total = total + ref[rows, at].astype(F32)
            else:
                if p == 0:
                    full = refs[0][:, at]
                    for ref in refs[1 : 1 + arrived]:
                        full = full + ref[:, at].astype(F32)
                total = full[rows]
            outs[p][:, at] = total if p == 0 else total.astype(BF16)


def add_and_cut(own, received, parts, name, after=()):
    count, features = own.shape
    size = count // parts
    vec = pl.BlockSpec(memory_space=pltpu.VMEM)
    return pl.pallas_call(
        functools.partial(add_kernel, len(received), parts, 512),
        in_specs=[vec] * (1 + len(received)) + [pl.BlockSpec(memory_space=pl.ANY)] * len(after),
        out_specs=[vec] * parts,
        out_shape=[sds((size, features), F32)] + [sds((size, features), BF16)] * (parts - 1),
        compiler_params=params(),
        name=name,
    )(own, *received, *after)


def routes_kernel(ids, weights, unused, out_ref):
    rows, picks = ids.shape
    i = lax.broadcasted_iota(jnp.int32, out_ref.shape, 0)
    k = lax.broadcasted_iota(jnp.int32, out_ref.shape, 1)
    table = jnp.zeros(out_ref.shape, F32)
    for r in range(rows):
        for t in range(picks):
            table = jnp.where((i == r) & (k == t), ids[r, t].astype(F32), table)
            table = jnp.where((i == r) & (k == picks + t), weights[r, t], table)
    out_ref[...] = table


def routes(ids, weights, after):
    return pl.pallas_call(
        routes_kernel,
        in_specs=[SCALARS, SCALARS, pl.BlockSpec(memory_space=pl.ANY)],
        out_specs=pl.BlockSpec(memory_space=pltpu.VMEM),
        out_shape=sds((8, 128), F32),
        compiler_params=params(),
        name="routes",
    )(ids, weights, after)


def column(values, count):
    i = lax.broadcasted_iota(jnp.int32, (count, 1), 0)
    out = jnp.full((count, 1), values[0])
    for n, value in enumerate(values[1:], 1):
        out = jnp.where(i == n, value, out)
    return out


def tables_kernel(rows, picks, planes, cap, me, ids, *refs):
    homes = refs[:planes]
    pick_ref, weight_ref, merge_ref = refs[planes + 1 :]
    plane = me[0] // 8
    found = {}
    for k in range(planes):
        expert = (plane ^ k).astype(F32)
        for h in range(planes):
            home = homes[h]
            places = [jnp.int32(-1)] * cap
            scales = [jnp.float32(0.0)] * cap
            seen = jnp.int32(0)
            for r in range(rows):
                has = home[r, 0] == expert
                scale = home[r, picks]
                for t in range(1, picks):
                    here = home[r, t] == expert
                    scale = jnp.where(here, home[r, picks + t], scale)
                    has = has | here
                for s in range(cap):
                    hit = has & (seen == s)
                    places[s] = jnp.where(hit, h * rows + r, places[s])
                    scales[s] = jnp.where(hit, scale, scales[s])
                seen = seen + has.astype(jnp.int32)
            found[k, h] = places, scales
    sources = [p for k in range(planes) for j in range(planes) for p in found[k, j ^ k][0]]
    scales = [w for j in range(planes) for w in found[0, j][1]]
    lane = lax.broadcasted_iota(jnp.int32, pick_ref.shape, 1)
    pick_ref[...] = jnp.where(lane == column(sources, len(sources)), 1.0, 0.0)
    weight_ref[...] = jnp.broadcast_to(column(scales, len(scales)), weight_ref.shape)
    lane = lax.broadcasted_iota(jnp.int32, merge_ref.shape, 1)
    merge = jnp.zeros(merge_ref.shape, jnp.bool_)
    for t in range(picks):
        slots = []
        for r in range(rows):
            seen = jnp.int32(0)
            for b in range(r):
                for u in range(picks):
                    seen = seen + (ids[b, u] == ids[r, t]).astype(jnp.int32)
            slots.append((ids[r, t] ^ plane) * cap + seen)
        merge = merge | (lane == column(slots, rows))
    merge_ref[...] = jnp.where(merge, 1.0, 0.0).astype(BF16)


def tables(me, ids, homes, cap, after):
    rows, picks = ids.shape
    planes = len(homes)
    vec = pl.BlockSpec(memory_space=pltpu.VMEM)
    return pl.pallas_call(
        functools.partial(tables_kernel, rows, picks, planes, cap),
        in_specs=[SCALARS] * (2 + planes) + [pl.BlockSpec(memory_space=pl.ANY)],
        out_specs=[vec] * 3,
        out_shape=[
            sds((planes * planes * cap, planes * rows), F32),
            sds((planes * cap, 128), F32),
            sds((rows, planes * cap), BF16),
        ],
        compiler_params=params(),
        name="route_tables",
    )(me, ids, *homes, after)


def pick_rows(pick, values):
    high = values.astype(BF16)
    low = (values - high.astype(F32)).astype(BF16)
    return jnp.dot(pick, high, preferred_element_type=F32) + jnp.dot(
        pick, low, preferred_element_type=F32
    )


def add_and_pick_kernel(planes, tile, own_ref, a_ref, b_ref, c_ref, hidden_ref, pick_ref, *outs):
    size = outs[0].shape[0]
    rows = hidden_ref.shape[0]
    pick = pick_ref[...]
    near, far = pick[:size].astype(BF16), pick[size:].astype(BF16)
    for start in range(0, own_ref.shape[1], tile):
        at = slice(start, start + tile)
        total = own_ref[:, at]
        for ref in (a_ref, b_ref, c_ref):
            total = total + ref[:, at].astype(F32)
        home = total[:rows] + hidden_ref[:, at].astype(F32)
        total = jnp.concatenate([home, total[rows:]], axis=0)
        outs[0][:, at] = pick_rows(near, total)
        others = jnp.dot(far, total.astype(BF16), preferred_element_type=F32)
        for k in range(1, planes):
            outs[k][:, at] = others[(k - 1) * size : k * size].astype(BF16)


def add_and_pick(own, received, hidden, pick, planes):
    features = own.shape[1]
    size = pick.shape[0] // planes
    vec = pl.BlockSpec(memory_space=pltpu.VMEM)
    return pl.pallas_call(
        functools.partial(add_and_pick_kernel, planes, 1024),
        in_specs=[vec] * 6,
        out_specs=[vec] * planes,
        out_shape=[sds((size, features), F32)] + [sds((size, features), BF16)] * (planes - 1),
        compiler_params=params(),
        name="add_chips",
    )(own, *received, hidden, pick)


def norm_kernel(planes, *refs):
    gain_ref, resid_ref, normed_ref = refs[planes], refs[-2], refs[-1]
    total = refs[0][...]
    for ref in refs[1:planes]:
        total = total + ref[...].astype(F32)
    resid = total.astype(BF16)
    resid_ref[...] = resid
    wide = resid.astype(F32)
    scale = lax.rsqrt(jnp.mean(wide * wide, axis=1, keepdims=True) + EPSILON)
    normed_ref[...] = (wide * scale * gain_ref[...].astype(F32)).astype(BF16)


def norm(sums, gain, after):
    vec = pl.BlockSpec(memory_space=pltpu.VMEM)
    shape = sums[0].shape
    return pl.pallas_call(
        functools.partial(norm_kernel, len(sums)),
        in_specs=[vec] * (1 + len(sums)) + [pl.BlockSpec(memory_space=pl.ANY)] * len(after),
        out_specs=[vec, vec],
        out_shape=[sds(shape, BF16), sds(shape, BF16)],
        compiler_params=params(),
        name="norm",
    )(*sums, gain, *after)


def expert_kernel(pieces, tiles, *refs):
    xs = refs[:pieces]
    gate_ref, up_ref, down_ref, own_ref, other_ref = refs[pieces:]
    tile = down_ref.shape[1] // tiles
    gate, up = 0.0, 0.0
    for t in range(tiles):
        at = slice(t * tile, (t + 1) * tile)
        x = jnp.concatenate([ref[:, at].astype(F32) for ref in xs], axis=0).astype(BF16)
        gate += jnp.dot(x, gate_ref[at, :], preferred_element_type=F32)
        up += jnp.dot(x, up_ref[at, :], preferred_element_type=F32)
    act = (gate / (1.0 + jnp.exp(-gate)) * up).astype(BF16)
    half = act.shape[0] // 2
    for t in range(tiles):
        at = slice(t * tile, (t + 1) * tile)
        out = jnp.dot(act, down_ref[:, at], preferred_element_type=F32)
        own_ref[:, at] = out[:half]
        other_ref[:, at] = out[half:].astype(BF16)


def expert(pieces, gate_up, down_proj, tiles=7):
    size, features = pieces[0].shape
    half = size * len(pieces) // 2
    vec = pl.BlockSpec(memory_space=pltpu.VMEM)
    return pl.pallas_call(
        functools.partial(expert_kernel, len(pieces), tiles),
        in_specs=[vec] * (len(pieces) + 3),
        out_specs=[vec, vec],
        out_shape=[sds((half, features), F32), sds((half, features), BF16)],
        compiler_params=params(),
        name="expert",
    )(*pieces, *gate_up, down_proj)


def weigh_kernel(planes, share, tile, own_ref, a_ref, b_ref, c_ref, resid_ref, weight_ref, *outs):
    cap = outs[0].shape[0]
    for start in range(0, own_ref.shape[1], tile):
        at = slice(start, start + tile)
        total = own_ref[:, at]
        for ref in (a_ref, b_ref, c_ref):
            total = total + ref[:, at].astype(F32)
        total = total * weight_ref[:, :1] + resid_ref[:, at].astype(F32) * share
        outs[0][:, at] = total[:cap]
        for k in range(1, planes):
            outs[k][:, at] = total[k * cap : (k + 1) * cap].astype(BF16)


def weigh(own, received, resid, weight, planes, picks):
    count, features = own.shape
    cap = count // planes
    vec = pl.BlockSpec(memory_space=pltpu.VMEM)
    return pl.pallas_call(
        functools.partial(weigh_kernel, planes, 1.0 / picks, 1024),
        in_specs=[vec] * 6,
        out_specs=[vec] * planes,
        out_shape=[sds((cap, features), F32)] + [sds((cap, features), BF16)] * (planes - 1),
        compiler_params=params(),
        name="weigh",
    )(own, *received, resid, weight)


def combine_kernel(planes, merge_ref, *refs):
    out_ref = refs[planes]
    table = jnp.concatenate([ref[...].astype(F32) for ref in refs[:planes]], axis=0)
    out_ref[...] = pick_rows(merge_ref[...], table).astype(BF16)


def combine(merge, pieces):
    vec = pl.BlockSpec(memory_space=pltpu.VMEM)
    return pl.pallas_call(
        functools.partial(combine_kernel, len(pieces)),
        in_specs=[vec] * (1 + len(pieces)),
        out_specs=vec,
        out_shape=sds((merge.shape[0], pieces[0].shape[1]), BF16),
        compiler_params=params(),
        name="combine",
    )(merge, *pieces)


def body(
    queries,
    latent_cache,
    lengths,
    hidden_in,
    route_ids,
    route_weights,
    value_up,
    out_proj,
    norm_gain,
    gate_up,
    down_proj,
):
    devices = lax.axis_size("dp")
    planes = devices // SPLIT
    rows = hidden_in.shape[0]
    picks = route_ids.shape[1]
    cap = max(2, (rows * picks + planes - 1) // planes)
    me = lax.axis_index("dp").astype(jnp.int32).reshape(1)

    def swap(x, mask):
        return lax.ppermute(x, "dp", [(i, i ^ mask) for i in range(devices)])

    def over_chips(messages):
        return [swap(x, k << 1) for k, x in enumerate(messages, 1)]

    def over_planes(messages):
        return [swap(x, k << 3) for k, x in enumerate(messages, 1)]

    latents = attention(queries, latent_cache, lengths)
    by_heads = lax.all_to_all(latents, "dp", split_axis=0, concat_axis=0, tiled=True)
    (early,) = fetch([out_proj], [(1, TILES, EARLY)], latents, "fetch_projections")
    mine = routes(route_ids, route_weights, latents)
    homes = [mine] + over_planes([mine] * (planes - 1))
    own, other = project(me, by_heads, value_up, out_proj, early, planes, rows, homes[1:])
    own, *out = add_and_cut(own, [swap(other, 1)], 4, "add_core")
    pick, weight, merge = tables(me, route_ids, homes, cap, own)
    own, *out = add_and_pick(own, over_chips(out), hidden_in, pick, planes)
    gate_up, (down_proj,) = fetch([gate_up, down_proj], [(0, 2, 2), (0, 1, 1)], own, "fetch_experts")
    resid, picked = norm([own] + over_planes(out), norm_gain[None], gate_up[:1])
    chips = [picked] + over_chips([picked] * 3)
    pieces = chips + [swap(x, 1) for x in chips]
    own, other = expert(pieces, gate_up, down_proj)
    own, *out = add_and_cut(own, [swap(other, 1)], 4, "add_expert_core")
    own, *out = weigh(own, over_chips(out), resid, weight, planes, picks)
    return combine(merge, [own] + over_planes(out))


def solution(mesh):
    placed = (
        P(("groups", "dp"), None, None),
        P(("groups", "dp"), None, None),
        P(("groups", "dp")),
        P(("groups", "dp"), None),
        P(("groups", "dp"), None),
        P(("groups", "dp"), None),
        P("dp", None, None),
        P("dp", None),
        P(),
        P(None, None, "dp"),
        P("dp", None),
    )
    return jax.shard_map(
        body, mesh=mesh, in_specs=placed, out_specs=P(("groups", "dp"), None), check_vma=False
    )
```

```python
import functools

import jax
import jax.numpy as jnp
from jax import lax
from jax.experimental import pallas as pl
from jax.experimental.pallas import tpu as pltpu
from jax.sharding import PartitionSpec as P

LAT = 512
ROPE = 64
VH = 128
SPLIT = 8

MASKED = -1e30
EPSILON = 1e-06
VMEM = 24 * 1024 * 1024
TILES = 7
EARLY = 2

F32 = jnp.float32
BF16 = jnp.bfloat16
SCALARS = pl.BlockSpec(memory_space=pltpu.SMEM)


def sds(shape, dtype):
    return jax.ShapeDtypeStruct(shape, dtype)


def params():
    return pltpu.CompilerParams(vmem_limit_bytes=VMEM)


def in_hbm(x):
    return pltpu.with_memory_space_constraint(x, pltpu.HBM)


def whole(shape):
    return pl.BlockSpec(shape, lambda *_: (0,) * len(shape))


def attention_kernel(lengths_hbm, q_hbm, k_hbm, o_ref, lengths, queries, keys, lat, sems):
    rows, _, heads = queries.shape
    live = pltpu.make_async_copy(lengths_hbm, lengths, sems.at[2 * rows])
    live.start()
    copies = []
    for r in range(rows):
        for n, (src, dst) in enumerate(((q_hbm, queries), (k_hbm, keys))):
            copy = pltpu.make_async_copy(src.at[r], dst.at[r], sems.at[2 * r + n])
            copy.start()
            copies.append(copy)
    live.wait()

    def score(r):
        copies[2 * r].wait()
        copies[2 * r + 1].wait()
        scores = lax.dot_general(
            queries[r], keys[r], (((0,), (0,)), ((), ())), preferred_element_type=F32
        ) * ((VH + ROPE) ** -0.5)
        position = lax.broadcasted_iota(jnp.int32, scores.shape, 1)
        return jnp.where(position < lengths[r], scores, MASKED)

    ready = score(0)
    for r in range(rows):
        scores = ready
        if r + 1 < rows:
            ready = score(r + 1)
        terms = jnp.exp(scores - jnp.max(scores, axis=1, keepdims=True))
        total = jnp.sum(terms, axis=1, keepdims=True)
        numerator = lax.dot_general(
            terms.astype(BF16), keys[r, :LAT], (((1,), (1,)), ((), ())), preferred_element_type=F32
        )
        lat[r * heads : (r + 1) * heads, :] = (numerator / total).astype(BF16)
    size = rows * heads
    i = lax.broadcasted_iota(jnp.int32, (size, 1), 0)
    k = lax.broadcasted_iota(jnp.int32, (size, size), 1)
    pick = jnp.where(k == (i % rows) * heads + i // rows, 1.0, 0.0).astype(BF16)
    o_ref[...] = jnp.dot(pick, lat[...], preferred_element_type=F32).astype(BF16)


def attention(queries, latent_cache, lengths):
    rows, heads, width = queries.shape
    slots = latent_cache.shape[1]
    hbm = pl.BlockSpec(memory_space=pltpu.HBM)
    return pl.pallas_call(
        attention_kernel,
        in_specs=[hbm, hbm, hbm],
        out_specs=pl.BlockSpec(memory_space=pltpu.VMEM),
        out_shape=sds((rows * heads, LAT), BF16),
        scratch_shapes=[
            pltpu.SMEM((rows,), jnp.int32),
            pltpu.VMEM((rows, width, heads), BF16),
            pltpu.VMEM((rows, width, slots), BF16),
            pltpu.VMEM((rows * heads, LAT), BF16),
            pltpu.SemaphoreType.DMA((2 * rows + 1,)),
        ],
        compiler_params=params(),
        name="latent_attention",
    )(
        in_hbm(lengths),
        in_hbm(jnp.swapaxes(queries, 1, 2)),
        in_hbm(jnp.swapaxes(latent_cache, 1, 2)),
    )


def fetch_kernel(parts, *refs):
    count = len(parts)
    ins, outs, sems = refs[:count], refs[count + 1 : -1], refs[-1]
    copies = []
    for ref, (axis, cuts, taken) in zip(ins, parts):
        size = ref.shape[axis] // cuts
        for c in range(taken):
            at = (slice(None),) * axis + (pl.ds(c * size, size),)
            src = ref.at[c] if axis == 0 and size == 1 else ref.at[at]
            n = len(copies)
            copies.append(pltpu.make_async_copy(src, outs[n], sems.at[n]))
    for copy in copies:
        copy.start()
    for copy in copies:
        copy.wait()


def fetch(weights, parts, after, name):
    shapes = []
    for w, (axis, cuts, taken) in zip(weights, parts):
        shape = list(w.shape)
        shape[axis] //= cuts
        if shape[0] == 1:
            shape = shape[1:]
        shapes += [pltpu.VMEM(tuple(shape), w.dtype)] * taken
    out = pl.pallas_call(
        functools.partial(fetch_kernel, parts),
        in_specs=[pl.BlockSpec(memory_space=pltpu.HBM)] * len(weights)
        + [pl.BlockSpec(memory_space=pl.ANY)],
        out_specs=[pl.BlockSpec(memory_space=pltpu.VMEM)] * len(shapes),
        out_shape=shapes,
        scratch_shapes=[pltpu.SemaphoreType.DMA((len(shapes),))],
        compiler_params=params(),
        name=name,
    )(*[in_hbm(w) for w in weights], after)
    result = []
    for _, _, taken in parts:
        result.append(list(out[:taken]))
        out = out[taken:]
    return result


def project_kernel(planes, rows, me, x_ref, v_ref, w_hbm, *refs):
    early = refs[:EARLY]
    own_ref, other_ref, flat, late, sems = refs[-5:]
    tile = late.shape[2]
    copies = []
    for t in range(EARLY, TILES):
        n = t - EARLY
        copy = pltpu.make_async_copy(w_hbm.at[:, pl.ds(t * tile, tile)], late.at[n], sems.at[n])
        copy.start()
        copies.append(copy)
    heads = v_ref.shape[0]
    count = flat.shape[0]
    i = lax.broadcasted_iota(jnp.int32, (heads * count, 1), 0)
    k = lax.broadcasted_iota(jnp.int32, (heads * count, x_ref.shape[0]), 1)
    plane = (i // rows) % planes
    rest = (i // (rows * planes)) % 8
    home = me[0] ^ (plane * 8 + (rest % 4) * 2 + rest // 4)
    target = (home * heads + i // count) * rows + i % rows
    pick = jnp.where(k == target, 1.0, 0.0).astype(BF16)
    mine = jnp.dot(pick, x_ref[...], preferred_element_type=F32).astype(BF16)
    for h in range(heads):
        flat[:, h * VH : (h + 1) * VH] = jnp.dot(
            mine[h * count : (h + 1) * count], v_ref[h], preferred_element_type=F32
        ).astype(BF16)
    half = count // 2
    for t in range(TILES):
        if t >= EARLY:
            copies[t - EARLY].wait()
        w = early[t][...] if t < EARLY else late[t - EARLY]
        at = slice(t * tile, (t + 1) * tile)
        out = jnp.dot(flat[...], w, preferred_element_type=F32)
        own_ref[:, at] = out[:half]
        other_ref[:, at] = out[half:].astype(BF16)


def project(me, by_heads, value_up, out_proj, early, planes, rows, after):
    count = planes * 8 * rows
    depth, features = out_proj.shape
    half = count // 2
    vec = pl.BlockSpec(memory_space=pltpu.VMEM)
    return pl.pallas_call(
        functools.partial(project_kernel, planes, rows),
        in_specs=[SCALARS, vec, vec, pl.BlockSpec(memory_space=pltpu.HBM)]
        + [vec] * EARLY
        + [pl.BlockSpec(memory_space=pl.ANY)] * len(after),
        out_specs=[vec, vec],
        out_shape=[sds((half, features), F32), sds((half, features), BF16)],
        scratch_shapes=[
            pltpu.VMEM((count, depth), BF16),
            pltpu.VMEM((TILES - EARLY, depth, features // TILES), BF16),
            pltpu.SemaphoreType.DMA((TILES - EARLY,)),
        ],
        compiler_params=params(),
        name="projections",
    )(me, by_heads, value_up, in_hbm(out_proj), *early, *after)


def add_kernel(arrived, parts, tile, *refs):
    outs = refs[-parts:]
    size = outs[0].shape[0]
    for start in range(0, outs[0].shape[1], tile):
        at = slice(start, start + tile)
        for p in range(parts):
            rows = slice(p * size, (p + 1) * size)
            if arrived and size % 16 == 0:
                total = refs[0][rows, at]
                for ref in refs[1 : 1 + arrived]:
                    total = total + ref[rows, at].astype(F32)
            else:
                if p == 0:
                    full = refs[0][:, at]
                    for ref in refs[1 : 1 + arrived]:
                        full = full + ref[:, at].astype(F32)
                total = full[rows]
            outs[p][:, at] = total if p == 0 else total.astype(BF16)


def add_and_cut(own, received, parts, name, after=()):
    count, features = own.shape
    size = count // parts
    vec = pl.BlockSpec(memory_space=pltpu.VMEM)
    return pl.pallas_call(
        functools.partial(add_kernel, len(received), parts, 512),
        in_specs=[vec] * (1 + len(received)) + [pl.BlockSpec(memory_space=pl.ANY)] * len(after),
        out_specs=[vec] * parts,
        out_shape=[sds((size, features), F32)] + [sds((size, features), BF16)] * (parts - 1),
        compiler_params=params(),
        name=name,
    )(own, *received, *after)


def routes_kernel(ids, weights, unused, out_ref):
    rows, picks = ids.shape
    i = lax.broadcasted_iota(jnp.int32, out_ref.shape, 0)
    k = lax.broadcasted_iota(jnp.int32, out_ref.shape, 1)
    table = jnp.zeros(out_ref.shape, F32)
    for r in range(rows):
        for t in range(picks):
            table = jnp.where((i == r) & (k == t), ids[r, t].astype(F32), table)
            table = jnp.where((i == r) & (k == picks + t), weights[r, t], table)
    out_ref[...] = table


def routes(ids, weights, after):
    return pl.pallas_call(
        routes_kernel,
        in_specs=[SCALARS, SCALARS, pl.BlockSpec(memory_space=pl.ANY)],
        out_specs=pl.BlockSpec(memory_space=pltpu.VMEM),
        out_shape=sds((8, 128), F32),
        compiler_params=params(),
        name="routes",
    )(ids, weights, after)


def column(values, count):
    i = lax.broadcasted_iota(jnp.int32, (count, 1), 0)
    out = jnp.full((count, 1), values[0])
    for n, value in enumerate(values[1:], 1):
        out = jnp.where(i == n, value, out)
    return out


def tables_kernel(rows, picks, planes, cap, me, ids, *refs):
    homes = refs[:planes]
    pick_ref, weight_ref, merge_ref = refs[planes + 1 :]
    plane = me[0] // 8
    found = {}
    for k in range(planes):
        expert = (plane ^ k).astype(F32)
        for h in range(planes):
            home = homes[h]
            places = [jnp.int32(-1)] * cap
            scales = [jnp.float32(0.0)] * cap
            seen = jnp.int32(0)
            for r in range(rows):
                has = home[r, 0] == expert
                scale = home[r, picks]
                for t in range(1, picks):
                    here = home[r, t] == expert
                    scale = jnp.where(here, home[r, picks + t], scale)
                    has = has | here
                for s in range(cap):
                    hit = has & (seen == s)
                    places[s] = jnp.where(hit, h * rows + r, places[s])
                    scales[s] = jnp.where(hit, scale, scales[s])
                seen = seen + has.astype(jnp.int32)
            found[k, h] = places, scales
    sources = [p for k in range(planes) for j in range(planes) for p in found[k, j ^ k][0]]
    scales = [w for j in range(planes) for w in found[0, j][1]]
    lane = lax.broadcasted_iota(jnp.int32, pick_ref.shape, 1)
    pick_ref[...] = jnp.where(lane == column(sources, len(sources)), 1.0, 0.0)
    weight_ref[...] = jnp.broadcast_to(column(scales, len(scales)), weight_ref.shape)
    lane = lax.broadcasted_iota(jnp.int32, merge_ref.shape, 1)
    merge = jnp.zeros(merge_ref.shape, jnp.bool_)
    for t in range(picks):
        slots = []
        for r in range(rows):
            seen = jnp.int32(0)
            for b in range(r):
                for u in range(picks):
                    seen = seen + (ids[b, u] == ids[r, t]).astype(jnp.int32)
            away = ids[r, t] ^ plane
            spot = jnp.where(away == 0, 0, jnp.where(away == 1, planes - 1, planes - away))
            slots.append(spot * cap + seen)
        merge = merge | (lane == column(slots, rows))
    merge_ref[...] = jnp.where(merge, 1.0, 0.0).astype(BF16)


def tables(me, ids, homes, cap, after):
    rows, picks = ids.shape
    planes = len(homes)
    vec = pl.BlockSpec(memory_space=pltpu.VMEM)
    return pl.pallas_call(
        functools.partial(tables_kernel, rows, picks, planes, cap),
        in_specs=[SCALARS] * (2 + planes) + [pl.BlockSpec(memory_space=pl.ANY)],
        out_specs=[vec] * 3,
        out_shape=[
            sds((planes * planes * cap, planes * rows), F32),
            sds((planes * cap, 128), F32),
            sds((rows, planes * cap), BF16),
        ],
        compiler_params=params(),
        name="route_tables",
    )(me, ids, *homes, after)


def pick_rows(pick, values):
    high = values.astype(BF16)
    low = (values - high.astype(F32)).astype(BF16)
    return jnp.dot(pick, high, preferred_element_type=F32) + jnp.dot(
        pick, low, preferred_element_type=F32
    )


def add_and_pick_kernel(planes, tile, own_ref, a_ref, b_ref, c_ref, hidden_ref, pick_ref, *outs):
    size = outs[0].shape[0]
    rows = hidden_ref.shape[0]
    pick = pick_ref[...]
    near, far = pick[:size].astype(BF16), pick[size:].astype(BF16)
    for start in range(0, own_ref.shape[1], tile):
        at = slice(start, start + tile)
        total = own_ref[:, at]
        for ref in (a_ref, b_ref, c_ref):
            total = total + ref[:, at].astype(F32)
        home = total[:rows] + hidden_ref[:, at].astype(F32)
        total = jnp.concatenate([home, total[rows:]], axis=0)
        outs[0][:, at] = pick_rows(near, total)
        others = jnp.dot(far, total.astype(BF16), preferred_element_type=F32)
        for k in range(1, planes):
            outs[k][:, at] = others[(k - 1) * size : k * size].astype(BF16)


def add_and_pick(own, received, hidden, pick, planes):
    features = own.shape[1]
    size = pick.shape[0] // planes
    vec = pl.BlockSpec(memory_space=pltpu.VMEM)
    return pl.pallas_call(
        functools.partial(add_and_pick_kernel, planes, 1024),
        in_specs=[vec] * 6,
        out_specs=[vec] * planes,
        out_shape=[sds((size, features), F32)] + [sds((size, features), BF16)] * (planes - 1),
        compiler_params=params(),
        name="add_chips",
    )(own, *received, hidden, pick)


def norm_kernel(planes, *refs):
    gain_ref, resid_ref, normed_ref = refs[planes], refs[-2], refs[-1]
    total = refs[0][...]
    for ref in refs[1:planes]:
        total = total + ref[...].astype(F32)
    resid = total.astype(BF16)
    resid_ref[...] = resid
    wide = resid.astype(F32)
    scale = lax.rsqrt(jnp.mean(wide * wide, axis=1, keepdims=True) + EPSILON)
    normed_ref[...] = (wide * scale * gain_ref[...].astype(F32)).astype(BF16)


def norm(sums, gain, after):
    vec = pl.BlockSpec(memory_space=pltpu.VMEM)
    shape = sums[0].shape
    return pl.pallas_call(
        functools.partial(norm_kernel, len(sums)),
        in_specs=[vec] * (1 + len(sums)) + [pl.BlockSpec(memory_space=pl.ANY)] * len(after),
        out_specs=[vec, vec],
        out_shape=[sds(shape, BF16), sds(shape, BF16)],
        compiler_params=params(),
        name="norm",
    )(*sums, gain, *after)


def expert_kernel(pieces, tiles, *refs):
    xs = refs[:pieces]
    gate_ref, up_ref, down_ref, own_ref, other_ref = refs[pieces:]
    tile = down_ref.shape[1] // tiles
    gate, up = 0.0, 0.0
    for t in range(tiles):
        at = slice(t * tile, (t + 1) * tile)
        x = jnp.concatenate([ref[:, at].astype(F32) for ref in xs], axis=0).astype(BF16)
        gate += jnp.dot(x, gate_ref[at, :], preferred_element_type=F32)
        up += jnp.dot(x, up_ref[at, :], preferred_element_type=F32)
    act = (gate / (1.0 + jnp.exp(-gate)) * up).astype(BF16)
    half = act.shape[0] // 2
    for t in range(tiles):
        at = slice(t * tile, (t + 1) * tile)
        out = jnp.dot(act, down_ref[:, at], preferred_element_type=F32)
        own_ref[:, at] = out[:half]
        other_ref[:, at] = out[half:].astype(BF16)


def expert(pieces, gate_up, down_proj, tiles=7):
    size, features = pieces[0].shape
    half = size * len(pieces) // 2
    vec = pl.BlockSpec(memory_space=pltpu.VMEM)
    return pl.pallas_call(
        functools.partial(expert_kernel, len(pieces), tiles),
        in_specs=[vec] * (len(pieces) + 3),
        out_specs=[vec, vec],
        out_shape=[sds((half, features), F32), sds((half, features), BF16)],
        compiler_params=params(),
        name="expert",
    )(*pieces, *gate_up, down_proj)


def weigh_kernel(planes, share, tile, own_ref, a_ref, b_ref, c_ref, resid_ref, weight_ref, *outs):
    cap = outs[0].shape[0]
    for start in range(0, own_ref.shape[1], tile):
        at = slice(start, start + tile)
        total = own_ref[:, at]
        for ref in (a_ref, b_ref, c_ref):
            total = total + ref[:, at].astype(F32)
        total = total * weight_ref[:, :1] + resid_ref[:, at].astype(F32) * share
        outs[0][:, at] = total[:cap]
        for k in range(1, planes):
            outs[k][:, at] = total[k * cap : (k + 1) * cap].astype(BF16)


def weigh(own, received, resid, weight, planes, picks):
    count, features = own.shape
    cap = count // planes
    vec = pl.BlockSpec(memory_space=pltpu.VMEM)
    return pl.pallas_call(
        functools.partial(weigh_kernel, planes, 1.0 / picks, 1024),
        in_specs=[vec] * 6,
        out_specs=[vec] * planes,
        out_shape=[sds((cap, features), F32)] + [sds((cap, features), BF16)] * (planes - 1),
        compiler_params=params(),
        name="weigh",
    )(own, *received, resid, weight)


def combine_kernel(planes, merge_ref, *refs):
    out_ref = refs[planes]
    table = jnp.concatenate([ref[...].astype(F32) for ref in refs[:planes]], axis=0)
    out_ref[...] = pick_rows(merge_ref[...], table).astype(BF16)


def combine(merge, pieces):
    vec = pl.BlockSpec(memory_space=pltpu.VMEM)
    return pl.pallas_call(
        functools.partial(combine_kernel, len(pieces)),
        in_specs=[vec] * (1 + len(pieces)),
        out_specs=vec,
        out_shape=sds((merge.shape[0], pieces[0].shape[1]), BF16),
        compiler_params=params(),
        name="combine",
    )(merge, *pieces)


def body(
    queries,
    latent_cache,
    lengths,
    hidden_in,
    route_ids,
    route_weights,
    value_up,
    out_proj,
    norm_gain,
    gate_up,
    down_proj,
):
    devices = lax.axis_size("dp")
    planes = devices // SPLIT
    rows = hidden_in.shape[0]
    picks = route_ids.shape[1]
    cap = max(2, (rows * picks + planes - 1) // planes)
    me = lax.axis_index("dp").astype(jnp.int32).reshape(1)

    def swap(x, mask):
        return lax.ppermute(x, "dp", [(i, i ^ mask) for i in range(devices)])

    def over_planes(messages):
        moved = [swap(x, k << 3) for k, x in enumerate(messages, 1)]
        return moved[1:][::-1] + moved[:1]

    def over_chips(messages):
        return [swap(x, k << 1) for k, x in enumerate(messages, 1)]

    latents = attention(queries, latent_cache, lengths)
    by_heads = lax.all_to_all(latents, "dp", split_axis=0, concat_axis=0, tiled=True)
    (early,) = fetch([out_proj], [(1, TILES, EARLY)], latents, "fetch_projections")
    mine = routes(route_ids, route_weights, latents)
    homes = over_planes([mine] * (planes - 1))
    homes = [mine] + homes[::-1]
    own, other = project(me, by_heads, value_up, out_proj, early, planes, rows, homes[1:])
    own, *out = add_and_cut(own, [swap(other, 1)], 4, "add_core")
    pick, weight, merge = tables(me, route_ids, homes, cap, own)
    own, *out = add_and_pick(own, over_chips(out), hidden_in, pick, planes)
    gate_up, (down_proj,) = fetch([gate_up, down_proj], [(0, 2, 2), (0, 1, 1)], own, "fetch_experts")
    resid, picked = norm([own] + over_planes(out), norm_gain[None], gate_up[:1])
    chips = [picked] + [swap(picked, k << 1) for k in (1, 2, 3)]
    pieces = chips + [swap(x, 1) for x in chips]
    own, other = expert(pieces, gate_up, down_proj)
    own, *out = add_and_cut(own, [swap(other, 1)], 4, "add_expert_core")
    own, *out = weigh(own, over_chips(out), resid, weight, planes, picks)
    return combine(merge, [own] + over_planes(out))


def solution(mesh):
    placed = (
        P(("groups", "dp"), None, None),
        P(("groups", "dp"), None, None),
        P(("groups", "dp")),
        P(("groups", "dp"), None),
        P(("groups", "dp"), None),
        P(("groups", "dp"), None),
        P("dp", None, None),
        P("dp", None),
        P(),
        P(None, None, "dp"),
        P("dp", None),
    )
    return jax.shard_map(
        body, mesh=mesh, in_specs=placed, out_specs=P(("groups", "dp"), None), check_vma=False
    )
```

```python
import functools

import jax
import jax.numpy as jnp
from jax import lax
from jax.experimental import pallas as pl
from jax.experimental.pallas import tpu as pltpu
from jax.sharding import PartitionSpec as P

LAT = 512
ROPE = 64
VH = 128
SPLIT = 8

MASKED = -1e30
EPSILON = 1e-06
VMEM = 24 * 1024 * 1024
TILES = 7
EARLY = 2
FIRST = 4

F32 = jnp.float32
BF16 = jnp.bfloat16
SCALARS = pl.BlockSpec(memory_space=pltpu.SMEM)


def sds(shape, dtype):
    return jax.ShapeDtypeStruct(shape, dtype)


def params():
    return pltpu.CompilerParams(vmem_limit_bytes=VMEM)


def in_hbm(x):
    return pltpu.with_memory_space_constraint(x, pltpu.HBM)


def whole(shape):
    return pl.BlockSpec(shape, lambda *_: (0,) * len(shape))


def attention_kernel(lengths_hbm, q_hbm, k_hbm, o_ref, lengths, queries, keys, lat, sems):
    rows, _, heads = queries.shape
    live = pltpu.make_async_copy(lengths_hbm, lengths, sems.at[2 * rows])
    live.start()
    copies = []
    for r in range(rows):
        for n, (src, dst) in enumerate(((q_hbm, queries), (k_hbm, keys))):
            copy = pltpu.make_async_copy(src.at[r], dst.at[r], sems.at[2 * r + n])
            copy.start()
            copies.append(copy)
    live.wait()

    def score(r):
        copies[2 * r].wait()
        copies[2 * r + 1].wait()
        scores = lax.dot_general(
            queries[r], keys[r], (((0,), (0,)), ((), ())), preferred_element_type=F32
        ) * ((VH + ROPE) ** -0.5)
        position = lax.broadcasted_iota(jnp.int32, scores.shape, 1)
        return jnp.where(position < lengths[r], scores, MASKED)

    ready = score(0)
    for r in range(rows):
        scores = ready
        if r + 1 < rows:
            ready = score(r + 1)
        terms = jnp.exp(scores - jnp.max(scores, axis=1, keepdims=True))
        total = jnp.sum(terms, axis=1, keepdims=True)
        numerator = lax.dot_general(
            terms.astype(BF16), keys[r, :LAT], (((1,), (1,)), ((), ())), preferred_element_type=F32
        )
        lat[r * heads : (r + 1) * heads, :] = (numerator / total).astype(BF16)
    size = rows * heads
    i = lax.broadcasted_iota(jnp.int32, (size, 1), 0)
    k = lax.broadcasted_iota(jnp.int32, (size, size), 1)
    pick = jnp.where(k == (i % rows) * heads + i // rows, 1.0, 0.0).astype(BF16)
    o_ref[...] = jnp.dot(pick, lat[...], preferred_element_type=F32).astype(BF16)


def attention(queries, latent_cache, lengths):
    rows, heads, width = queries.shape
    slots = latent_cache.shape[1]
    hbm = pl.BlockSpec(memory_space=pltpu.HBM)
    return pl.pallas_call(
        attention_kernel,
        in_specs=[hbm, hbm, hbm],
        out_specs=pl.BlockSpec(memory_space=pltpu.VMEM),
        out_shape=sds((rows * heads, LAT), BF16),
        scratch_shapes=[
            pltpu.SMEM((rows,), jnp.int32),
            pltpu.VMEM((rows, width, heads), BF16),
            pltpu.VMEM((rows, width, slots), BF16),
            pltpu.VMEM((rows * heads, LAT), BF16),
            pltpu.SemaphoreType.DMA((2 * rows + 1,)),
        ],
        compiler_params=params(),
        name="latent_attention",
    )(
        in_hbm(lengths),
        in_hbm(jnp.swapaxes(queries, 1, 2)),
        in_hbm(jnp.swapaxes(latent_cache, 1, 2)),
    )


def fetch_kernel(parts, *refs):
    count = len(parts)
    ins, outs, sems = refs[:count], refs[count + 1 : -1], refs[-1]
    copies = []
    for ref, (axis, cuts, first, taken) in zip(ins, parts):
        size = ref.shape[axis] // cuts
        for c in range(first, first + taken):
            at = (slice(None),) * axis + (pl.ds(c * size, size),)
            src = ref.at[c] if axis == 0 and size == 1 else ref.at[at]
            n = len(copies)
            copies.append(pltpu.make_async_copy(src, outs[n], sems.at[n]))
    for copy in copies:
        copy.start()
    for copy in copies:
        copy.wait()


def fetch(weights, parts, after, name):
    shapes = []
    for w, (axis, cuts, _, taken) in zip(weights, parts):
        shape = list(w.shape)
        shape[axis] //= cuts
        if shape[0] == 1:
            shape = shape[1:]
        shapes += [pltpu.VMEM(tuple(shape), w.dtype)] * taken
    out = pl.pallas_call(
        functools.partial(fetch_kernel, parts),
        in_specs=[pl.BlockSpec(memory_space=pltpu.HBM)] * len(weights)
        + [pl.BlockSpec(memory_space=pl.ANY)],
        out_specs=[pl.BlockSpec(memory_space=pltpu.VMEM)] * len(shapes),
        out_shape=shapes,
        scratch_shapes=[pltpu.SemaphoreType.DMA((len(shapes),))],
        compiler_params=params(),
        name=name,
    )(*[in_hbm(w) for w in weights], after)
    result = []
    for *_, taken in parts:
        result.append(list(out[:taken]))
        out = out[taken:]
    return result


def late_copies(w_hbm, tiles, late, sems):
    tile = late.shape[2]
    copies = []
    for n, t in enumerate(tiles):
        copy = pltpu.make_async_copy(w_hbm.at[:, pl.ds(t * tile, tile)], late.at[n], sems.at[n])
        copy.start()
        copies.append(copy)
    return copies


def multiply(flat, weights, own_ref, other_ref):
    half = flat.shape[0] // 2
    tile = own_ref.shape[1] // len(weights)
    for t, weight in enumerate(weights):
        at = slice(t * tile, (t + 1) * tile)
        out = jnp.dot(flat[...], weight(), preferred_element_type=F32)
        own_ref[:, at] = out[:half]
        other_ref[:, at] = out[half:].astype(BF16)


def landed(copies, late):
    def one(n):
        def get():
            copies[n].wait()
            return late[n]

        return get

    return [one(n) for n in range(len(copies))]


def project_first_kernel(planes, rows, me, x_ref, v_ref, w_hbm, *refs):
    own_ref, other_ref, flat, late, sems = refs[-5:]
    copies = late_copies(w_hbm, range(FIRST), late, sems)
    heads = v_ref.shape[0]
    count = flat.shape[0]
    i = lax.broadcasted_iota(jnp.int32, (heads * count, 1), 0)
    k = lax.broadcasted_iota(jnp.int32, (heads * count, x_ref.shape[0]), 1)
    plane = (i // rows) % planes
    rest = (i // (rows * planes)) % 8
    home = me[0] ^ (plane * 8 + (rest % 4) * 2 + rest // 4)
    target = (home * heads + i // count) * rows + i % rows
    pick = jnp.where(k == target, 1.0, 0.0).astype(BF16)
    mine = jnp.dot(pick, x_ref[...], preferred_element_type=F32).astype(BF16)
    for h in range(heads):
        flat[:, h * VH : (h + 1) * VH] = jnp.dot(
            mine[h * count : (h + 1) * count], v_ref[h], preferred_element_type=F32
        ).astype(BF16)
    multiply(flat, landed(copies, late), own_ref, other_ref)


def project_rest_kernel(flat, w_hbm, *refs):
    early = refs[:EARLY]
    own_ref, other_ref, late, sems = refs[-4:]
    copies = late_copies(w_hbm, range(FIRST + EARLY, TILES), late, sems)
    weights = [lambda ref=ref: ref[...] for ref in early]
    multiply(flat, weights + landed(copies, late), own_ref, other_ref)


def project(me, by_heads, value_up, out_proj, early, planes, rows, after):
    count = planes * 8 * rows
    depth, features = out_proj.shape
    tile = features // TILES
    half = count // 2
    vec = pl.BlockSpec(memory_space=pltpu.VMEM)
    hbm = pl.BlockSpec(memory_space=pltpu.HBM)

    def sums(tiles):
        return [sds((half, tiles * tile), F32), sds((half, tiles * tile), BF16)]

    def scratch(tiles):
        return [pltpu.VMEM((tiles, depth, tile), BF16), pltpu.SemaphoreType.DMA((tiles,))]

    own_a, other_a, flat = pl.pallas_call(
        functools.partial(project_first_kernel, planes, rows),
        in_specs=[SCALARS, vec, vec, hbm] + [pl.BlockSpec(memory_space=pl.ANY)] * len(after),
        out_specs=[vec] * 3,
        out_shape=sums(FIRST) + [sds((count, depth), BF16)],
        scratch_shapes=scratch(FIRST),
        compiler_params=params(),
        name="project_first",
    )(me, by_heads, value_up, in_hbm(out_proj), *after)
    own_b, other_b = pl.pallas_call(
        project_rest_kernel,
        in_specs=[vec, hbm] + [vec] * EARLY,
        out_specs=[vec] * 2,
        out_shape=sums(TILES - FIRST),
        scratch_shapes=scratch(TILES - FIRST - EARLY),
        compiler_params=params(),
        cost_estimate=pl.CostEstimate(
            flops=2 * count * depth * (TILES - FIRST) * tile,
            bytes_accessed=2 * depth * (TILES - FIRST) * tile * 2,
            transcendentals=0,
        ),
        name="project_rest",
    )(flat, in_hbm(out_proj), *early)
    return (own_a, own_b), (other_a, other_b)


def add_kernel(parts, tile, *refs):
    outs = refs[-parts:]
    ranges = (len(refs) - parts) // 2
    size = outs[0].shape[0]
    first = 0
    for own_ref, other_ref in zip(refs[:ranges], refs[ranges : 2 * ranges]):
        for start in range(0, own_ref.shape[1], tile):
            at = slice(start, start + tile)
            to = slice(first + start, first + start + tile)
            total = own_ref[:, at] + other_ref[:, at].astype(F32)
            outs[0][:, to] = total[:size]
            for p in range(1, parts):
                outs[p][:, to] = total[p * size : (p + 1) * size].astype(BF16)
        first += own_ref.shape[1]


def add_and_cut(own, received, parts, name):
    size = own[0].shape[0] // parts
    features = sum(x.shape[1] for x in own)
    vec = pl.BlockSpec(memory_space=pltpu.VMEM)
    return pl.pallas_call(
        functools.partial(add_kernel, parts, 512),
        in_specs=[vec] * (2 * len(own)),
        out_specs=[vec] * parts,
        out_shape=[sds((size, features), F32)] + [sds((size, features), BF16)] * (parts - 1),
        compiler_params=params(),
        name=name,
    )(*own, *received)


def routes_kernel(ids, weights, unused, out_ref):
    rows, picks = ids.shape
    i = lax.broadcasted_iota(jnp.int32, out_ref.shape, 0)
    k = lax.broadcasted_iota(jnp.int32, out_ref.shape, 1)
    table = jnp.zeros(out_ref.shape, F32)
    for r in range(rows):
        for t in range(picks):
            table = jnp.where((i == r) & (k == t), ids[r, t].astype(F32), table)
            table = jnp.where((i == r) & (k == picks + t), weights[r, t], table)
    out_ref[...] = table


def routes(ids, weights, after):
    return pl.pallas_call(
        routes_kernel,
        in_specs=[SCALARS, SCALARS, pl.BlockSpec(memory_space=pl.ANY)],
        out_specs=pl.BlockSpec(memory_space=pltpu.VMEM),
        out_shape=sds((8, 128), F32),
        compiler_params=params(),
        name="routes",
    )(ids, weights, after)


def column(values, count):
    i = lax.broadcasted_iota(jnp.int32, (count, 1), 0)
    out = jnp.full((count, 1), values[0])
    for n, value in enumerate(values[1:], 1):
        out = jnp.where(i == n, value, out)
    return out


def tables_kernel(rows, picks, planes, cap, me, ids, *refs):
    homes = refs[:planes]
    pick_ref, weight_ref, merge_ref = refs[planes + 1 :]
    plane = me[0] // 8
    found = {}
    for k in range(planes):
        expert = (plane ^ k).astype(F32)
        for h in range(planes):
            home = homes[h]
            places = [jnp.int32(-1)] * cap
            scales = [jnp.float32(0.0)] * cap
            seen = jnp.int32(0)
            for r in range(rows):
                has = home[r, 0] == expert
                scale = home[r, picks]
                for t in range(1, picks):
                    here = home[r, t] == expert
                    scale = jnp.where(here, home[r, picks + t], scale)
                    has = has | here
                for s in range(cap):
                    hit = has & (seen == s)
                    places[s] = jnp.where(hit, h * rows + r, places[s])
                    scales[s] = jnp.where(hit, scale, scales[s])
                seen = seen + has.astype(jnp.int32)
            found[k, h] = places, scales
    sources = [p for k in range(planes) for j in range(planes) for p in found[k, j ^ k][0]]
    scales = [w for j in range(planes) for w in found[0, j][1]]
    lane = lax.broadcasted_iota(jnp.int32, pick_ref.shape, 1)
    pick_ref[...] = jnp.where(lane == column(sources, len(sources)), 1.0, 0.0)
    weight_ref[...] = jnp.broadcast_to(column(scales, len(scales)), weight_ref.shape)
    lane = lax.broadcasted_iota(jnp.int32, merge_ref.shape, 1)
    merge = jnp.zeros(merge_ref.shape, jnp.bool_)
    for t in range(picks):
        slots = []
        for r in range(rows):
            seen = jnp.int32(0)
            for b in range(r):
                for u in range(picks):
                    seen = seen + (ids[b, u] == ids[r, t]).astype(jnp.int32)
            away = ids[r, t] ^ plane
            spot = jnp.where(away == 0, 0, jnp.where(away == 1, planes - 1, planes - away))
            slots.append(spot * cap + seen)
        merge = merge | (lane == column(slots, rows))
    merge_ref[...] = jnp.where(merge, 1.0, 0.0).astype(BF16)


def tables(me, ids, homes, cap, after):
    rows, picks = ids.shape
    planes = len(homes)
    vec = pl.BlockSpec(memory_space=pltpu.VMEM)
    return pl.pallas_call(
        functools.partial(tables_kernel, rows, picks, planes, cap),
        in_specs=[SCALARS] * (2 + planes) + [pl.BlockSpec(memory_space=pl.ANY)],
        out_specs=[vec] * 3,
        out_shape=[
            sds((planes * planes * cap, planes * rows), F32),
            sds((planes * cap, 128), F32),
            sds((rows, planes * cap), BF16),
        ],
        compiler_params=params(),
        name="route_tables",
    )(me, ids, *homes, after)


def pick_rows(pick, values):
    high = values.astype(BF16)
    low = (values - high.astype(F32)).astype(BF16)
    return jnp.dot(pick, high, preferred_element_type=F32) + jnp.dot(
        pick, low, preferred_element_type=F32
    )


def add_and_pick_kernel(planes, tile, first, own_ref, a_ref, b_ref, c_ref, hidden_ref, pick_ref, *outs):
    size = outs[0].shape[0]
    rows = hidden_ref.shape[0]
    pick = pick_ref[...]
    near, far = pick[:size].astype(BF16), pick[size:].astype(BF16)
    for start in range(0, own_ref.shape[1], tile):
        at = slice(start, start + tile)
        total = own_ref[:, at]
        for ref in (a_ref, b_ref, c_ref):
            total = total + ref[:, at].astype(F32)
        here = slice(first + start, first + start + tile)
        home = total[:rows] + hidden_ref[:, here].astype(F32)
        total = jnp.concatenate([home, total[rows:]], axis=0)
        outs[0][:, at] = pick_rows(near, total)
        others = jnp.dot(far, total.astype(BF16), preferred_element_type=F32)
        for k in range(1, planes):
            outs[k][:, at] = others[(k - 1) * size : k * size].astype(BF16)


def add_and_pick(own, received, hidden, pick, planes, first):
    features = own.shape[1]
    size = pick.shape[0] // planes
    vec = pl.BlockSpec(memory_space=pltpu.VMEM)
    return pl.pallas_call(
        functools.partial(add_and_pick_kernel, planes, 1024, first),
        in_specs=[vec] * 6,
        out_specs=[vec] * planes,
        out_shape=[sds((size, features), F32)] + [sds((size, features), BF16)] * (planes - 1),
        compiler_params=params(),
        name="add_chips",
    )(own, *received, hidden, pick)


def norm_kernel(planes, parts, *refs):
    gain_ref, resid_ref, normed_ref = refs[planes * parts], refs[-2], refs[-1]
    totals = []
    for p in range(parts):
        total = refs[p * planes][...]
        for ref in refs[p * planes + 1 : (p + 1) * planes]:
            total = total + ref[...].astype(F32)
        totals.append(total)
    resid = jnp.concatenate(totals[::-1], axis=1).astype(BF16)
    resid_ref[...] = resid
    wide = resid.astype(F32)
    scale = lax.rsqrt(jnp.mean(wide * wide, axis=1, keepdims=True) + EPSILON)
    normed_ref[...] = (wide * scale * gain_ref[...].astype(F32)).astype(BF16)


def norm(sums, gain, after):
    vec = pl.BlockSpec(memory_space=pltpu.VMEM)
    planes = len(sums[0])
    shape = (sums[0][0].shape[0], gain.shape[1])
    return pl.pallas_call(
        functools.partial(norm_kernel, planes, len(sums)),
        in_specs=[vec] * (1 + planes * len(sums))
        + [pl.BlockSpec(memory_space=pl.ANY)] * len(after),
        out_specs=[vec, vec],
        out_shape=[sds(shape, BF16), sds(shape, BF16)],
        compiler_params=params(),
        name="norm",
    )(*sums[1], *sums[0], gain, *after)


def expert_kernel(pieces, tiles, *refs):
    xs = refs[:pieces]
    gate_ref, up_ref, down_ref, own_ref, other_ref = refs[pieces:]
    tile = down_ref.shape[1] // tiles
    gate, up = 0.0, 0.0
    for t in range(tiles):
        at = slice(t * tile, (t + 1) * tile)
        x = jnp.concatenate([ref[:, at].astype(F32) for ref in xs], axis=0).astype(BF16)
        gate += jnp.dot(x, gate_ref[at, :], preferred_element_type=F32)
        up += jnp.dot(x, up_ref[at, :], preferred_element_type=F32)
    act = (gate / (1.0 + jnp.exp(-gate)) * up).astype(BF16)
    half = act.shape[0] // 2
    for t in range(tiles):
        at = slice(t * tile, (t + 1) * tile)
        out = jnp.dot(act, down_ref[:, at], preferred_element_type=F32)
        own_ref[:, at] = out[:half]
        other_ref[:, at] = out[half:].astype(BF16)


def expert(pieces, gate_up, down_proj, tiles=7):
    size, features = pieces[0].shape
    half = size * len(pieces) // 2
    vec = pl.BlockSpec(memory_space=pltpu.VMEM)
    return pl.pallas_call(
        functools.partial(expert_kernel, len(pieces), tiles),
        in_specs=[vec] * (len(pieces) + 3),
        out_specs=[vec, vec],
        out_shape=[sds((half, features), F32), sds((half, features), BF16)],
        compiler_params=params(),
        name="expert",
    )(*pieces, *gate_up, down_proj)


def weigh_kernel(planes, share, tile, own_ref, a_ref, b_ref, c_ref, resid_ref, weight_ref, *outs):
    cap = outs[0].shape[0]
    for start in range(0, own_ref.shape[1], tile):
        at = slice(start, start + tile)
        total = own_ref[:, at]
        for ref in (a_ref, b_ref, c_ref):
            total = total + ref[:, at].astype(F32)
        total = total * weight_ref[:, :1] + resid_ref[:, at].astype(F32) * share
        outs[0][:, at] = total[:cap]
        for k in range(1, planes):
            outs[k][:, at] = total[k * cap : (k + 1) * cap].astype(BF16)


def weigh(own, received, resid, weight, planes, picks):
    count, features = own.shape
    cap = count // planes
    vec = pl.BlockSpec(memory_space=pltpu.VMEM)
    return pl.pallas_call(
        functools.partial(weigh_kernel, planes, 1.0 / picks, 1024),
        in_specs=[vec] * 6,
        out_specs=[vec] * planes,
        out_shape=[sds((cap, features), F32)] + [sds((cap, features), BF16)] * (planes - 1),
        compiler_params=params(),
        name="weigh",
    )(own, *received, resid, weight)


def combine_kernel(planes, merge_ref, *refs):
    out_ref = refs[planes]
    table = jnp.concatenate([ref[...].astype(F32) for ref in refs[:planes]], axis=0)
    out_ref[...] = pick_rows(merge_ref[...], table).astype(BF16)


def combine(merge, pieces):
    vec = pl.BlockSpec(memory_space=pltpu.VMEM)
    return pl.pallas_call(
        functools.partial(combine_kernel, len(pieces)),
        in_specs=[vec] * (1 + len(pieces)),
        out_specs=vec,
        out_shape=sds((merge.shape[0], pieces[0].shape[1]), BF16),
        compiler_params=params(),
        name="combine",
    )(merge, *pieces)


def body(
    queries,
    latent_cache,
    lengths,
    hidden_in,
    route_ids,
    route_weights,
    value_up,
    out_proj,
    norm_gain,
    gate_up,
    down_proj,
):
    devices = lax.axis_size("dp")
    planes = devices // SPLIT
    rows = hidden_in.shape[0]
    picks = route_ids.shape[1]
    cap = max(2, (rows * picks + planes - 1) // planes)
    me = lax.axis_index("dp").astype(jnp.int32).reshape(1)

    def swap(x, mask):
        return lax.ppermute(x, "dp", [(i, i ^ mask) for i in range(devices)])

    def over_planes(messages):
        moved = [swap(x, k << 3) for k, x in enumerate(messages, 1)]
        return moved[1:][::-1] + moved[:1]

    def over_chips(messages):
        return [swap(x, k << 1) for k, x in enumerate(messages, 1)]

    latents = attention(queries, latent_cache, lengths)
    by_heads = lax.all_to_all(latents, "dp", split_axis=0, concat_axis=0, tiled=True)
    (early,) = fetch([out_proj], [(1, TILES, FIRST, EARLY)], latents, "fetch_projections")
    mine = routes(route_ids, route_weights, latents)
    homes = over_planes([mine] * (planes - 1))
    homes = [mine] + homes[::-1]
    own, other = project(me, by_heads, value_up, out_proj, early, planes, rows, homes[1:] + early[:1])
    parts = []
    for n in range(2):
        part, *out = add_and_cut(own[n : n + 1], [swap(other[n], 1)], 4, "add_core")
        parts.append((part, over_chips(out)))
    own = parts[0][0]
    pick, weight, merge = tables(me, route_ids, homes, cap, own)
    sums, first = [], 0
    for own, received in parts:
        own, *out = add_and_pick(own, received, hidden_in, pick, planes, first)
        sums.append([own] + over_planes(out))
        first += own.shape[1]
    gate_up, (down_proj,) = fetch(
        [gate_up, down_proj], [(0, 2, 0, 2), (0, 1, 0, 1)], sums[1][0], "fetch_experts"
    )
    resid, picked = norm(sums, norm_gain[None], gate_up[:1])
    chips = [picked] + [swap(picked, k << 1) for k in (1, 2, 3)]
    pieces = chips + [swap(x, 1) for x in chips]
    own, other = expert(pieces, gate_up, down_proj)
    own, *out = add_and_cut([own], [swap(other, 1)], 4, "add_expert_core")
    own, *out = weigh(own, over_chips(out), resid, weight, planes, picks)
    return combine(merge, [own] + over_planes(out))


def solution(mesh):
    placed = (
        P(("groups", "dp"), None, None),
        P(("groups", "dp"), None, None),
        P(("groups", "dp")),
        P(("groups", "dp"), None),
        P(("groups", "dp"), None),
        P(("groups", "dp"), None),
        P("dp", None, None),
        P("dp", None),
        P(),
        P(None, None, "dp"),
        P("dp", None),
    )
    return jax.shard_map(
        body, mesh=mesh, in_specs=placed, out_specs=P(("groups", "dp"), None), check_vma=False
    )
```

```python
import functools

import jax
import jax.numpy as jnp
from jax import lax
from jax.experimental import pallas as pl
from jax.experimental.pallas import tpu as pltpu
from jax.sharding import PartitionSpec as P

LAT = 512
ROPE = 64
VH = 128
SPLIT = 8

MASKED = -1e30
EPSILON = 1e-06
VMEM = 24 * 1024 * 1024
TILES = 7
EARLY = 2
FIRST = 4

F32 = jnp.float32
BF16 = jnp.bfloat16
SCALARS = pl.BlockSpec(memory_space=pltpu.SMEM)


def sds(shape, dtype):
    return jax.ShapeDtypeStruct(shape, dtype)


def params():
    return pltpu.CompilerParams(vmem_limit_bytes=VMEM)


def in_hbm(x):
    return pltpu.with_memory_space_constraint(x, pltpu.HBM)


def whole(shape):
    return pl.BlockSpec(shape, lambda *_: (0,) * len(shape))


def attention_kernel(lengths_hbm, q_hbm, k_hbm, o_ref, lengths, queries, keys, lat, sems):
    rows, _, heads = queries.shape
    live = pltpu.make_async_copy(lengths_hbm, lengths, sems.at[2 * rows])
    live.start()
    copies = []
    for r in range(rows):
        for n, (src, dst) in enumerate(((q_hbm, queries), (k_hbm, keys))):
            copy = pltpu.make_async_copy(src.at[r], dst.at[r], sems.at[2 * r + n])
            copy.start()
            copies.append(copy)
    live.wait()

    def score(r):
        copies[2 * r].wait()
        copies[2 * r + 1].wait()
        scores = lax.dot_general(
            queries[r], keys[r], (((0,), (0,)), ((), ())), preferred_element_type=F32
        ) * ((VH + ROPE) ** -0.5)
        position = lax.broadcasted_iota(jnp.int32, scores.shape, 1)
        return jnp.where(position < lengths[r], scores, MASKED)

    ready = score(0)
    for r in range(rows):
        scores = ready
        if r + 1 < rows:
            ready = score(r + 1)
        terms = jnp.exp(scores - jnp.max(scores, axis=1, keepdims=True))
        total = jnp.sum(terms, axis=1, keepdims=True)
        numerator = lax.dot_general(
            terms.astype(BF16), keys[r, :LAT], (((1,), (1,)), ((), ())), preferred_element_type=F32
        )
        lat[r * heads : (r + 1) * heads, :] = (numerator / total).astype(BF16)
    size = rows * heads
    i = lax.broadcasted_iota(jnp.int32, (size, 1), 0)
    k = lax.broadcasted_iota(jnp.int32, (size, size), 1)
    pick = jnp.where(k == (i % rows) * heads + i // rows, 1.0, 0.0).astype(BF16)
    o_ref[...] = jnp.dot(pick, lat[...], preferred_element_type=F32).astype(BF16)


def attention(queries, latent_cache, lengths):
    rows, heads, width = queries.shape
    slots = latent_cache.shape[1]
    hbm = pl.BlockSpec(memory_space=pltpu.HBM)
    return pl.pallas_call(
        attention_kernel,
        in_specs=[hbm, hbm, hbm],
        out_specs=pl.BlockSpec(memory_space=pltpu.VMEM),
        out_shape=sds((rows * heads, LAT), BF16),
        scratch_shapes=[
            pltpu.SMEM((rows,), jnp.int32),
            pltpu.VMEM((rows, width, heads), BF16),
            pltpu.VMEM((rows, width, slots), BF16),
            pltpu.VMEM((rows * heads, LAT), BF16),
            pltpu.SemaphoreType.DMA((2 * rows + 1,)),
        ],
        compiler_params=params(),
        name="latent_attention",
    )(
        in_hbm(lengths),
        in_hbm(jnp.swapaxes(queries, 1, 2)),
        in_hbm(jnp.swapaxes(latent_cache, 1, 2)),
    )


def fetch_kernel(parts, *refs):
    count = len(parts)
    ins, outs, sems = refs[:count], refs[count + 1 : -1], refs[-1]
    copies = []
    for ref, (axis, cuts, first, taken) in zip(ins, parts):
        size = ref.shape[axis] // cuts
        for c in range(first, first + taken):
            at = (slice(None),) * axis + (pl.ds(c * size, size),)
            src = ref.at[c] if axis == 0 and size == 1 else ref.at[at]
            n = len(copies)
            copies.append(pltpu.make_async_copy(src, outs[n], sems.at[n]))
    for copy in copies:
        copy.start()
    for copy in copies:
        copy.wait()


def fetch(weights, parts, after, name):
    shapes = []
    for w, (axis, cuts, _, taken) in zip(weights, parts):
        shape = list(w.shape)
        shape[axis] //= cuts
        if shape[0] == 1:
            shape = shape[1:]
        shapes += [pltpu.VMEM(tuple(shape), w.dtype)] * taken
    out = pl.pallas_call(
        functools.partial(fetch_kernel, parts),
        in_specs=[pl.BlockSpec(memory_space=pltpu.HBM)] * len(weights)
        + [pl.BlockSpec(memory_space=pl.ANY)],
        out_specs=[pl.BlockSpec(memory_space=pltpu.VMEM)] * len(shapes),
        out_shape=shapes,
        scratch_shapes=[pltpu.SemaphoreType.DMA((len(shapes),))],
        compiler_params=params(),
        name=name,
    )(*[in_hbm(w) for w in weights], after)
    result = []
    for *_, taken in parts:
        result.append(list(out[:taken]))
        out = out[taken:]
    return result


def late_copies(w_hbm, tiles, late, sems):
    tile = late.shape[2]
    copies = []
    for n, t in enumerate(tiles):
        copy = pltpu.make_async_copy(w_hbm.at[:, pl.ds(t * tile, tile)], late.at[n], sems.at[n])
        copy.start()
        copies.append(copy)
    return copies


def multiply(flat, weights, own_ref, other_ref):
    half = flat.shape[0] // 2
    tile = own_ref.shape[1] // len(weights)
    for t, weight in enumerate(weights):
        at = slice(t * tile, (t + 1) * tile)
        out = jnp.dot(flat[...], weight(), preferred_element_type=F32)
        own_ref[:, at] = out[:half]
        other_ref[:, at] = out[half:].astype(BF16)


def landed(copies, late):
    def one(n):
        def get():
            copies[n].wait()
            return late[n]

        return get

    return [one(n) for n in range(len(copies))]


def project_first_kernel(planes, rows, me, x_ref, v_ref, w_hbm, *refs):
    own_ref, other_ref, flat, late, sems = refs[-5:]
    copies = late_copies(w_hbm, range(FIRST), late, sems)
    heads = v_ref.shape[0]
    count = flat.shape[0]
    i = lax.broadcasted_iota(jnp.int32, (heads * count, 1), 0)
    k = lax.broadcasted_iota(jnp.int32, (heads * count, x_ref.shape[0]), 1)
    plane = (i // rows) % planes
    rest = (i // (rows * planes)) % 8
    home = me[0] ^ (plane * 8 + (rest % 4) * 2 + rest // 4)
    target = (home * heads + i // count) * rows + i % rows
    pick = jnp.where(k == target, 1.0, 0.0).astype(BF16)
    mine = jnp.dot(pick, x_ref[...], preferred_element_type=F32).astype(BF16)
    for h in range(heads):
        flat[:, h * VH : (h + 1) * VH] = jnp.dot(
            mine[h * count : (h + 1) * count], v_ref[h], preferred_element_type=F32
        ).astype(BF16)
    multiply(flat, landed(copies, late), own_ref, other_ref)


def project_rest_kernel(flat, w_hbm, *refs):
    early = refs[:EARLY]
    own_ref, other_ref, late, sems = refs[-4:]
    copies = late_copies(w_hbm, range(FIRST + EARLY, TILES), late, sems)
    weights = [lambda ref=ref: ref[...] for ref in early]
    multiply(flat, weights + landed(copies, late), own_ref, other_ref)


def project(me, by_heads, value_up, out_proj, early, planes, rows, after):
    count = planes * 8 * rows
    depth, features = out_proj.shape
    tile = features // TILES
    half = count // 2
    vec = pl.BlockSpec(memory_space=pltpu.VMEM)
    hbm = pl.BlockSpec(memory_space=pltpu.HBM)

    def sums(tiles):
        return [sds((half, tiles * tile), F32), sds((half, tiles * tile), BF16)]

    def scratch(tiles):
        return [pltpu.VMEM((tiles, depth, tile), BF16), pltpu.SemaphoreType.DMA((tiles,))]

    own_a, other_a, flat = pl.pallas_call(
        functools.partial(project_first_kernel, planes, rows),
        in_specs=[SCALARS, vec, vec, hbm] + [pl.BlockSpec(memory_space=pl.ANY)] * len(after),
        out_specs=[vec] * 3,
        out_shape=sums(FIRST) + [sds((count, depth), BF16)],
        scratch_shapes=scratch(FIRST),
        compiler_params=params(),
        name="project_first",
    )(me, by_heads, value_up, in_hbm(out_proj), *after)
    own_b, other_b = pl.pallas_call(
        project_rest_kernel,
        in_specs=[vec, hbm] + [vec] * EARLY,
        out_specs=[vec] * 2,
        out_shape=sums(TILES - FIRST),
        scratch_shapes=scratch(TILES - FIRST - EARLY),
        compiler_params=params(),
        cost_estimate=pl.CostEstimate(
            flops=2 * count * depth * (TILES - FIRST) * tile,
            bytes_accessed=2 * depth * (TILES - FIRST) * tile * 2,
            transcendentals=0,
        ),
        name="project_rest",
    )(flat, in_hbm(out_proj), *early)
    return (own_a, own_b), (other_a, other_b)


def add_kernel(parts, tile, *refs):
    outs = refs[-parts:]
    ranges = (len(refs) - parts) // 2
    size = outs[0].shape[0]
    first = 0
    for own_ref, other_ref in zip(refs[:ranges], refs[ranges : 2 * ranges]):
        for start in range(0, own_ref.shape[1], tile):
            at = slice(start, start + tile)
            to = slice(first + start, first + start + tile)
            total = own_ref[:, at] + other_ref[:, at].astype(F32)
            outs[0][:, to] = total[:size]
            for p in range(1, parts):
                outs[p][:, to] = total[p * size : (p + 1) * size].astype(BF16)
        first += own_ref.shape[1]


def add_and_cut(own, received, parts, name):
    size = own[0].shape[0] // parts
    features = sum(x.shape[1] for x in own)
    vec = pl.BlockSpec(memory_space=pltpu.VMEM)
    return pl.pallas_call(
        functools.partial(add_kernel, parts, 512),
        in_specs=[vec] * (2 * len(own)),
        out_specs=[vec] * parts,
        out_shape=[sds((size, features), F32)] + [sds((size, features), BF16)] * (parts - 1),
        compiler_params=params(),
        name=name,
    )(*own, *received)


def routes_kernel(ids, weights, unused, out_ref):
    rows, picks = ids.shape
    i = lax.broadcasted_iota(jnp.int32, out_ref.shape, 0)
    k = lax.broadcasted_iota(jnp.int32, out_ref.shape, 1)
    table = jnp.zeros(out_ref.shape, F32)
    for r in range(rows):
        for t in range(picks):
            table = jnp.where((i == r) & (k == t), ids[r, t].astype(F32), table)
            table = jnp.where((i == r) & (k == picks + t), weights[r, t], table)
    out_ref[...] = table


def routes(ids, weights, after):
    return pl.pallas_call(
        routes_kernel,
        in_specs=[SCALARS, SCALARS, pl.BlockSpec(memory_space=pl.ANY)],
        out_specs=pl.BlockSpec(memory_space=pltpu.VMEM),
        out_shape=sds((8, 128), F32),
        compiler_params=params(),
        name="routes",
    )(ids, weights, after)


def column(values, count):
    i = lax.broadcasted_iota(jnp.int32, (count, 1), 0)
    out = jnp.full((count, 1), values[0])
    for n, value in enumerate(values[1:], 1):
        out = jnp.where(i == n, value, out)
    return out


def tables_kernel(rows, picks, planes, cap, me, ids, *refs):
    homes = refs[:planes]
    pick_ref, weight_ref, merge_ref = refs[planes + 1 :]
    plane = me[0] // 8
    found = {}
    for k in range(planes):
        expert = (plane ^ k).astype(F32)
        for h in range(planes):
            home = homes[h]
            places = [jnp.int32(-1)] * cap
            scales = [jnp.float32(0.0)] * cap
            seen = jnp.int32(0)
            for r in range(rows):
                has = home[r, 0] == expert
                scale = home[r, picks]
                for t in range(1, picks):
                    here = home[r, t] == expert
                    scale = jnp.where(here, home[r, picks + t], scale)
                    has = has | here
                for s in range(cap):
                    hit = has & (seen == s)
                    places[s] = jnp.where(hit, h * rows + r, places[s])
                    scales[s] = jnp.where(hit, scale, scales[s])
                seen = seen + has.astype(jnp.int32)
            found[k, h] = places, scales
    sources = [p for k in range(planes) for j in range(planes) for p in found[k, j ^ k][0]]
    scales = [w for j in range(planes) for w in found[0, j][1]]
    lane = lax.broadcasted_iota(jnp.int32, pick_ref.shape, 1)
    pick_ref[...] = jnp.where(lane == column(sources, len(sources)), 1.0, 0.0)
    weight_ref[...] = jnp.broadcast_to(column(scales, len(scales)), weight_ref.shape)
    lane = lax.broadcasted_iota(jnp.int32, merge_ref.shape, 1)
    merge = jnp.zeros(merge_ref.shape, jnp.bool_)
    for t in range(picks):
        slots = []
        for r in range(rows):
            seen = jnp.int32(0)
            for b in range(r):
                for u in range(picks):
                    seen = seen + (ids[b, u] == ids[r, t]).astype(jnp.int32)
            away = ids[r, t] ^ plane
            spot = jnp.where(away == 0, 0, jnp.where(away == 1, planes - 1, away - 1))
            slots.append(spot * cap + seen)
        merge = merge | (lane == column(slots, rows))
    merge_ref[...] = jnp.where(merge, 1.0, 0.0).astype(BF16)


def tables(me, ids, homes, cap, after):
    rows, picks = ids.shape
    planes = len(homes)
    vec = pl.BlockSpec(memory_space=pltpu.VMEM)
    return pl.pallas_call(
        functools.partial(tables_kernel, rows, picks, planes, cap),
        in_specs=[SCALARS] * (2 + planes) + [pl.BlockSpec(memory_space=pl.ANY)],
        out_specs=[vec] * 3,
        out_shape=[
            sds((planes * planes * cap, planes * rows), F32),
            sds((planes * cap, 128), F32),
            sds((rows, planes * cap), BF16),
        ],
        compiler_params=params(),
        name="route_tables",
    )(me, ids, *homes, after)


def pick_rows(pick, values):
    high = values.astype(BF16)
    low = (values - high.astype(F32)).astype(BF16)
    return jnp.dot(pick, high, preferred_element_type=F32) + jnp.dot(
        pick, low, preferred_element_type=F32
    )


def add_and_pick_kernel(planes, tile, first, own_ref, a_ref, b_ref, c_ref, hidden_ref, pick_ref, *outs):
    size = outs[0].shape[0]
    rows = hidden_ref.shape[0]
    pick = pick_ref[...]
    near, far = pick[:size].astype(BF16), pick[size:].astype(BF16)
    for start in range(0, own_ref.shape[1], tile):
        at = slice(start, start + tile)
        total = own_ref[:, at]
        for ref in (a_ref, b_ref, c_ref):
            total = total + ref[:, at].astype(F32)
        here = slice(first + start, first + start + tile)
        home = total[:rows] + hidden_ref[:, here].astype(F32)
        total = jnp.concatenate([home, total[rows:]], axis=0)
        outs[0][:, at] = pick_rows(near, total)
        others = jnp.dot(far, total.astype(BF16), preferred_element_type=F32)
        for k in range(1, planes):
            outs[k][:, at] = others[(k - 1) * size : k * size].astype(BF16)


def add_and_pick(own, received, hidden, pick, planes, first):
    features = own.shape[1]
    size = pick.shape[0] // planes
    vec = pl.BlockSpec(memory_space=pltpu.VMEM)
    return pl.pallas_call(
        functools.partial(add_and_pick_kernel, planes, 1024, first),
        in_specs=[vec] * 6,
        out_specs=[vec] * planes,
        out_shape=[sds((size, features), F32)] + [sds((size, features), BF16)] * (planes - 1),
        compiler_params=params(),
        name="add_chips",
    )(own, *received, hidden, pick)


def norm_kernel(planes, parts, *refs):
    gain_ref, resid_ref, normed_ref = refs[planes * parts], refs[-2], refs[-1]
    totals = []
    for p in range(parts):
        total = refs[p * planes][...]
        for ref in refs[p * planes + 1 : (p + 1) * planes]:
            total = total + ref[...].astype(F32)
        totals.append(total)
    resid = jnp.concatenate(totals[::-1], axis=1).astype(BF16)
    resid_ref[...] = resid
    wide = resid.astype(F32)
    scale = lax.rsqrt(jnp.mean(wide * wide, axis=1, keepdims=True) + EPSILON)
    normed_ref[...] = (wide * scale * gain_ref[...].astype(F32)).astype(BF16)


def norm(sums, gain, after):
    vec = pl.BlockSpec(memory_space=pltpu.VMEM)
    planes = len(sums[0])
    shape = (sums[0][0].shape[0], gain.shape[1])
    return pl.pallas_call(
        functools.partial(norm_kernel, planes, len(sums)),
        in_specs=[vec] * (1 + planes * len(sums))
        + [pl.BlockSpec(memory_space=pl.ANY)] * len(after),
        out_specs=[vec, vec],
        out_shape=[sds(shape, BF16), sds(shape, BF16)],
        compiler_params=params(),
        name="norm",
    )(*sums[1], *sums[0], gain, *after)


def expert_kernel(pieces, tiles, *refs):
    xs = refs[:pieces]
    gate_ref, up_ref, down_ref, own_ref, other_ref = refs[pieces:]
    tile = down_ref.shape[1] // tiles
    gate, up = 0.0, 0.0
    for t in range(tiles):
        at = slice(t * tile, (t + 1) * tile)
        x = jnp.concatenate([ref[:, at].astype(F32) for ref in xs], axis=0).astype(BF16)
        gate += jnp.dot(x, gate_ref[at, :], preferred_element_type=F32)
        up += jnp.dot(x, up_ref[at, :], preferred_element_type=F32)
    act = (gate / (1.0 + jnp.exp(-gate)) * up).astype(BF16)
    half = act.shape[0] // 2
    for t in range(tiles):
        at = slice(t * tile, (t + 1) * tile)
        out = jnp.dot(act, down_ref[:, at], preferred_element_type=F32)
        own_ref[:, at] = out[:half]
        other_ref[:, at] = out[half:].astype(BF16)


def expert(pieces, gate_up, down_proj, tiles=7):
    size, features = pieces[0].shape
    half = size * len(pieces) // 2
    vec = pl.BlockSpec(memory_space=pltpu.VMEM)
    return pl.pallas_call(
        functools.partial(expert_kernel, len(pieces), tiles),
        in_specs=[vec] * (len(pieces) + 3),
        out_specs=[vec, vec],
        out_shape=[sds((half, features), F32), sds((half, features), BF16)],
        compiler_params=params(),
        name="expert",
    )(*pieces, *gate_up, down_proj)


def weigh_kernel(planes, share, tile, own_ref, a_ref, b_ref, c_ref, resid_ref, weight_ref, *outs):
    cap = outs[0].shape[0]
    for start in range(0, own_ref.shape[1], tile):
        at = slice(start, start + tile)
        total = own_ref[:, at]
        for ref in (a_ref, b_ref, c_ref):
            total = total + ref[:, at].astype(F32)
        total = total * weight_ref[:, :1] + resid_ref[:, at].astype(F32) * share
        outs[0][:, at] = total[:cap]
        for k in range(1, planes):
            outs[k][:, at] = total[k * cap : (k + 1) * cap].astype(BF16)


def weigh(own, received, resid, weight, planes, picks):
    count, features = own.shape
    cap = count // planes
    vec = pl.BlockSpec(memory_space=pltpu.VMEM)
    return pl.pallas_call(
        functools.partial(weigh_kernel, planes, 1.0 / picks, 1024),
        in_specs=[vec] * 6,
        out_specs=[vec] * planes,
        out_shape=[sds((cap, features), F32)] + [sds((cap, features), BF16)] * (planes - 1),
        compiler_params=params(),
        name="weigh",
    )(own, *received, resid, weight)


def combine_kernel(planes, merge_ref, *refs):
    out_ref = refs[planes]
    table = jnp.concatenate([ref[...].astype(F32) for ref in refs[:planes]], axis=0)
    out_ref[...] = pick_rows(merge_ref[...], table).astype(BF16)


def combine(merge, pieces):
    vec = pl.BlockSpec(memory_space=pltpu.VMEM)
    return pl.pallas_call(
        functools.partial(combine_kernel, len(pieces)),
        in_specs=[vec] * (1 + len(pieces)),
        out_specs=vec,
        out_shape=sds((merge.shape[0], pieces[0].shape[1]), BF16),
        compiler_params=params(),
        name="combine",
    )(merge, *pieces)


def body(
    queries,
    latent_cache,
    lengths,
    hidden_in,
    route_ids,
    route_weights,
    value_up,
    out_proj,
    norm_gain,
    gate_up,
    down_proj,
):
    devices = lax.axis_size("dp")
    planes = devices // SPLIT
    rows = hidden_in.shape[0]
    picks = route_ids.shape[1]
    cap = max(2, (rows * picks + planes - 1) // planes)
    me = lax.axis_index("dp").astype(jnp.int32).reshape(1)

    def swap(x, mask):
        return lax.ppermute(x, "dp", [(i, i ^ mask) for i in range(devices)])

    def over_planes(messages):
        moved = [swap(x, k << 3) for k, x in enumerate(messages, 1)]
        return moved[1:] + moved[:1]

    def over_chips(messages):
        return [swap(x, k << 1) for k, x in enumerate(messages, 1)]

    latents = attention(queries, latent_cache, lengths)
    by_heads = lax.all_to_all(latents, "dp", split_axis=0, concat_axis=0, tiled=True)
    (early,) = fetch([out_proj], [(1, TILES, FIRST, EARLY)], latents, "fetch_projections")
    mine = routes(route_ids, route_weights, latents)
    homes = over_planes([mine] * (planes - 1))
    homes = [mine] + homes[-1:] + homes[:-1]
    own, other = project(me, by_heads, value_up, out_proj, early, planes, rows, homes[1:] + early[:1])
    parts = []
    for n in range(2):
        part, *out = add_and_cut(own[n : n + 1], [swap(other[n], 1)], 4, "add_core")
        parts.append((part, over_chips(out)))
    own = parts[0][0]
    pick, weight, merge = tables(me, route_ids, homes, cap, own)
    sums, first = [], 0
    for own, received in parts:
        own, *out = add_and_pick(own, received, hidden_in, pick, planes, first)
        sums.append([own] + over_planes(out))
        first += own.shape[1]
    gate_up, (down_proj,) = fetch(
        [gate_up, down_proj], [(0, 2, 0, 2), (0, 1, 0, 1)], sums[1][0], "fetch_experts"
    )
    resid, picked = norm(sums, norm_gain[None], gate_up[:1])
    chips = [picked] + [swap(picked, k << 1) for k in (1, 2, 3)]
    pieces = chips + [swap(x, 1) for x in chips]
    own, other = expert(pieces, gate_up, down_proj)
    own, *out = add_and_cut([own], [swap(other, 1)], 4, "add_expert_core")
    own, *out = weigh(own, over_chips(out), resid, weight, planes, picks)
    return combine(merge, [own] + over_planes(out))


def solution(mesh):
    placed = (
        P(("groups", "dp"), None, None),
        P(("groups", "dp"), None, None),
        P(("groups", "dp")),
        P(("groups", "dp"), None),
        P(("groups", "dp"), None),
        P(("groups", "dp"), None),
        P("dp", None, None),
        P("dp", None),
        P(),
        P(None, None, "dp"),
        P("dp", None),
    )
    return jax.shard_map(
        body, mesh=mesh, in_specs=placed, out_specs=P(("groups", "dp"), None), check_vma=False
    )
```

```python
import functools

import jax
import jax.numpy as jnp
from jax import lax
from jax.experimental import pallas as pl
from jax.experimental.pallas import tpu as pltpu
from jax.sharding import PartitionSpec as P

LAT = 512
ROPE = 64
VH = 128
SPLIT = 8

MASKED = -1e30
EPSILON = 1e-06
VMEM = 24 * 1024 * 1024
TILES = 7
EARLY = 2
FIRST = 4

F32 = jnp.float32
BF16 = jnp.bfloat16
SCALARS = pl.BlockSpec(memory_space=pltpu.SMEM)


def sds(shape, dtype):
    return jax.ShapeDtypeStruct(shape, dtype)


def params():
    return pltpu.CompilerParams(vmem_limit_bytes=VMEM)


def in_hbm(x):
    return pltpu.with_memory_space_constraint(x, pltpu.HBM)


def whole(shape):
    return pl.BlockSpec(shape, lambda *_: (0,) * len(shape))


def attention_kernel(lengths_hbm, q_hbm, k_hbm, o_ref, lengths, queries, keys, lat, sems):
    rows, _, heads = queries.shape
    live = pltpu.make_async_copy(lengths_hbm, lengths, sems.at[2 * rows])
    live.start()
    copies = []
    for r in range(rows):
        for n, (src, dst) in enumerate(((q_hbm, queries), (k_hbm, keys))):
            copy = pltpu.make_async_copy(src.at[r], dst.at[r], sems.at[2 * r + n])
            copy.start()
            copies.append(copy)
    live.wait()

    def score(r):
        copies[2 * r].wait()
        copies[2 * r + 1].wait()
        scores = lax.dot_general(
            queries[r], keys[r], (((0,), (0,)), ((), ())), preferred_element_type=F32
        ) * ((VH + ROPE) ** -0.5)
        position = lax.broadcasted_iota(jnp.int32, scores.shape, 1)
        return jnp.where(position < lengths[r], scores, MASKED)

    ready = score(0)
    for r in range(rows):
        scores = ready
        if r + 1 < rows:
            ready = score(r + 1)
        terms = jnp.exp(scores - jnp.max(scores, axis=1, keepdims=True))
        total = jnp.sum(terms, axis=1, keepdims=True)
        numerator = lax.dot_general(
            terms.astype(BF16), keys[r, :LAT], (((1,), (1,)), ((), ())), preferred_element_type=F32
        )
        lat[r * heads : (r + 1) * heads, :] = (numerator / total).astype(BF16)
    size = rows * heads
    i = lax.broadcasted_iota(jnp.int32, (size, 1), 0)
    k = lax.broadcasted_iota(jnp.int32, (size, size), 1)
    pick = jnp.where(k == (i % rows) * heads + i // rows, 1.0, 0.0).astype(BF16)
    o_ref[...] = jnp.dot(pick, lat[...], preferred_element_type=F32).astype(BF16)


def attention(queries, latent_cache, lengths):
    rows, heads, width = queries.shape
    slots = latent_cache.shape[1]
    hbm = pl.BlockSpec(memory_space=pltpu.HBM)
    return pl.pallas_call(
        attention_kernel,
        in_specs=[hbm, hbm, hbm],
        out_specs=pl.BlockSpec(memory_space=pltpu.VMEM),
        out_shape=sds((rows * heads, LAT), BF16),
        scratch_shapes=[
            pltpu.SMEM((rows,), jnp.int32),
            pltpu.VMEM((rows, width, heads), BF16),
            pltpu.VMEM((rows, width, slots), BF16),
            pltpu.VMEM((rows * heads, LAT), BF16),
            pltpu.SemaphoreType.DMA((2 * rows + 1,)),
        ],
        compiler_params=params(),
        name="latent_attention",
    )(
        in_hbm(lengths),
        in_hbm(jnp.swapaxes(queries, 1, 2)),
        in_hbm(jnp.swapaxes(latent_cache, 1, 2)),
    )


def fetch_kernel(parts, *refs):
    count = len(parts)
    ins, outs, sems = refs[:count], refs[count + 1 : -1], refs[-1]
    copies = []
    for ref, (axis, cuts, first, taken) in zip(ins, parts):
        size = ref.shape[axis] // cuts
        for c in range(first, first + taken):
            at = (slice(None),) * axis + (pl.ds(c * size, size),)
            src = ref.at[c] if axis == 0 and size == 1 else ref.at[at]
            n = len(copies)
            copies.append(pltpu.make_async_copy(src, outs[n], sems.at[n]))
    for copy in copies:
        copy.start()
    for copy in copies:
        copy.wait()


def fetch(weights, parts, after, name):
    shapes = []
    for w, (axis, cuts, _, taken) in zip(weights, parts):
        shape = list(w.shape)
        shape[axis] //= cuts
        if shape[0] == 1:
            shape = shape[1:]
        shapes += [pltpu.VMEM(tuple(shape), w.dtype)] * taken
    out = pl.pallas_call(
        functools.partial(fetch_kernel, parts),
        in_specs=[pl.BlockSpec(memory_space=pltpu.HBM)] * len(weights)
        + [pl.BlockSpec(memory_space=pl.ANY)],
        out_specs=[pl.BlockSpec(memory_space=pltpu.VMEM)] * len(shapes),
        out_shape=shapes,
        scratch_shapes=[pltpu.SemaphoreType.DMA((len(shapes),))],
        compiler_params=params(),
        name=name,
    )(*[in_hbm(w) for w in weights], after)
    result = []
    for *_, taken in parts:
        result.append(list(out[:taken]))
        out = out[taken:]
    return result


def late_copies(w_hbm, tiles, late, sems):
    tile = late.shape[2]
    copies = []
    for n, t in enumerate(tiles):
        copy = pltpu.make_async_copy(w_hbm.at[:, pl.ds(t * tile, tile)], late.at[n], sems.at[n])
        copy.start()
        copies.append(copy)
    return copies


def multiply(flat, weights, own_ref, other_ref):
    half = flat.shape[0] // 2
    tile = own_ref.shape[1] // len(weights)
    for t, weight in enumerate(weights):
        at = slice(t * tile, (t + 1) * tile)
        out = jnp.dot(flat[...], weight(), preferred_element_type=F32)
        own_ref[:, at] = out[:half]
        other_ref[:, at] = out[half:].astype(BF16)


def landed(copies, late):
    def one(n):
        def get():
            copies[n].wait()
            return late[n]

        return get

    return [one(n) for n in range(len(copies))]


def project_first_kernel(planes, rows, me, x_ref, v_ref, w_hbm, *refs):
    own_ref, other_ref, flat, late, sems = refs[-5:]
    copies = late_copies(w_hbm, range(FIRST), late, sems)
    heads = v_ref.shape[0]
    count = flat.shape[0]
    i = lax.broadcasted_iota(jnp.int32, (heads * count, 1), 0)
    k = lax.broadcasted_iota(jnp.int32, (heads * count, x_ref.shape[0]), 1)
    plane = (i // rows) % planes
    rest = (i // (rows * planes)) % 8
    home = me[0] ^ (plane * 8 + (rest % 4) * 2 + rest // 4)
    target = (home * heads + i // count) * rows + i % rows
    pick = jnp.where(k == target, 1.0, 0.0).astype(BF16)
    mine = jnp.dot(pick, x_ref[...], preferred_element_type=F32).astype(BF16)
    for h in range(heads):
        flat[:, h * VH : (h + 1) * VH] = jnp.dot(
            mine[h * count : (h + 1) * count], v_ref[h], preferred_element_type=F32
        ).astype(BF16)
    multiply(flat, landed(copies, late), own_ref, other_ref)


def project_rest_kernel(flat, w_hbm, *refs):
    early = refs[:EARLY]
    own_ref, other_ref, late, sems = refs[-4:]
    copies = late_copies(w_hbm, range(FIRST + EARLY, TILES), late, sems)
    weights = [lambda ref=ref: ref[...] for ref in early]
    multiply(flat, weights + landed(copies, late), own_ref, other_ref)


def project(me, by_heads, value_up, out_proj, early, planes, rows, after):
    count = planes * 8 * rows
    depth, features = out_proj.shape
    tile = features // TILES
    half = count // 2
    vec = pl.BlockSpec(memory_space=pltpu.VMEM)
    hbm = pl.BlockSpec(memory_space=pltpu.HBM)

    def sums(tiles):
        return [sds((half, tiles * tile), F32), sds((half, tiles * tile), BF16)]

    def scratch(tiles):
        return [pltpu.VMEM((tiles, depth, tile), BF16), pltpu.SemaphoreType.DMA((tiles,))]

    own_a, other_a, flat = pl.pallas_call(
        functools.partial(project_first_kernel, planes, rows),
        in_specs=[SCALARS, vec, vec, hbm] + [pl.BlockSpec(memory_space=pl.ANY)] * len(after),
        out_specs=[vec] * 3,
        out_shape=sums(FIRST) + [sds((count, depth), BF16)],
        scratch_shapes=scratch(FIRST),
        compiler_params=params(),
        name="project_first",
    )(me, by_heads, value_up, in_hbm(out_proj), *after)
    own_b, other_b = pl.pallas_call(
        project_rest_kernel,
        in_specs=[vec, hbm] + [vec] * EARLY,
        out_specs=[vec] * 2,
        out_shape=sums(TILES - FIRST),
        scratch_shapes=scratch(TILES - FIRST - EARLY),
        compiler_params=params(),
        cost_estimate=pl.CostEstimate(
            flops=2 * count * depth * (TILES - FIRST) * tile,
            bytes_accessed=2 * depth * (TILES - FIRST) * tile * 2,
            transcendentals=0,
        ),
        name="project_rest",
    )(flat, in_hbm(out_proj), *early)
    return (own_a, own_b), (other_a, other_b)


def add_kernel(parts, ranges, tile, *refs):
    outs = refs[-parts:]
    size = outs[0].shape[0]
    first = 0
    for own_ref, other_ref in zip(refs[:ranges], refs[ranges : 2 * ranges]):
        for start in range(0, own_ref.shape[1], tile):
            at = slice(start, start + tile)
            to = slice(first + start, first + start + tile)
            total = own_ref[:, at] + other_ref[:, at].astype(F32)
            outs[0][:, to] = total[:size]
            for p in range(1, parts):
                outs[p][:, to] = total[p * size : (p + 1) * size].astype(BF16)
        first += own_ref.shape[1]


def add_and_cut(own, received, parts, name, after=()):
    size = own[0].shape[0] // parts
    features = sum(x.shape[1] for x in own)
    vec = pl.BlockSpec(memory_space=pltpu.VMEM)
    return pl.pallas_call(
        functools.partial(add_kernel, parts, len(own), 512),
        in_specs=[vec] * (2 * len(own)) + [pl.BlockSpec(memory_space=pl.ANY)] * len(after),
        out_specs=[vec] * parts,
        out_shape=[sds((size, features), F32)] + [sds((size, features), BF16)] * (parts - 1),
        compiler_params=params(),
        name=name,
    )(*own, *received, *after)


def routes_kernel(ids, weights, unused, out_ref):
    rows, picks = ids.shape
    i = lax.broadcasted_iota(jnp.int32, out_ref.shape, 0)
    k = lax.broadcasted_iota(jnp.int32, out_ref.shape, 1)
    table = jnp.zeros(out_ref.shape, F32)
    for r in range(rows):
        for t in range(picks):
            table = jnp.where((i == r) & (k == t), ids[r, t].astype(F32), table)
            table = jnp.where((i == r) & (k == picks + t), weights[r, t], table)
    out_ref[...] = table


def routes(ids, weights, after):
    return pl.pallas_call(
        routes_kernel,
        in_specs=[SCALARS, SCALARS, pl.BlockSpec(memory_space=pl.ANY)],
        out_specs=pl.BlockSpec(memory_space=pltpu.VMEM),
        out_shape=sds((8, 128), F32),
        compiler_params=params(),
        name="routes",
    )(ids, weights, after)


def column(values, count):
    i = lax.broadcasted_iota(jnp.int32, (count, 1), 0)
    out = jnp.full((count, 1), values[0])
    for n, value in enumerate(values[1:], 1):
        out = jnp.where(i == n, value, out)
    return out


def tables_kernel(rows, picks, planes, cap, me, ids, *refs):
    homes = refs[:planes]
    pick_ref, weight_ref, merge_ref = refs[planes + 1 :]
    plane = me[0] // 8
    found = {}
    for k in range(planes):
        expert = (plane ^ k).astype(F32)
        for h in range(planes):
            home = homes[h]
            places = [jnp.int32(-1)] * cap
            scales = [jnp.float32(0.0)] * cap
            seen = jnp.int32(0)
            for r in range(rows):
                has = home[r, 0] == expert
                scale = home[r, picks]
                for t in range(1, picks):
                    here = home[r, t] == expert
                    scale = jnp.where(here, home[r, picks + t], scale)
                    has = has | here
                for s in range(cap):
                    hit = has & (seen == s)
                    places[s] = jnp.where(hit, h * rows + r, places[s])
                    scales[s] = jnp.where(hit, scale, scales[s])
                seen = seen + has.astype(jnp.int32)
            found[k, h] = places, scales
    sources = [p for k in range(planes) for j in range(planes) for p in found[k, j ^ k][0]]
    scales = [w for j in range(planes) for w in found[0, j][1]]
    lane = lax.broadcasted_iota(jnp.int32, pick_ref.shape, 1)
    pick_ref[...] = jnp.where(lane == column(sources, len(sources)), 1.0, 0.0)
    weight_ref[...] = jnp.broadcast_to(column(scales, len(scales)), weight_ref.shape)
    lane = lax.broadcasted_iota(jnp.int32, merge_ref.shape, 1)
    merge = jnp.zeros(merge_ref.shape, jnp.bool_)
    for t in range(picks):
        slots = []
        for r in range(rows):
            seen = jnp.int32(0)
            for b in range(r):
                for u in range(picks):
                    seen = seen + (ids[b, u] == ids[r, t]).astype(jnp.int32)
            away = ids[r, t] ^ plane
            spot = jnp.where(away == 0, 0, jnp.where(away == 1, planes - 1, away - 1))
            slots.append(spot * cap + seen)
        merge = merge | (lane == column(slots, rows))
    merge_ref[...] = jnp.where(merge, 1.0, 0.0).astype(BF16)


def tables(me, ids, homes, cap, after):
    rows, picks = ids.shape
    planes = len(homes)
    vec = pl.BlockSpec(memory_space=pltpu.VMEM)
    return pl.pallas_call(
        functools.partial(tables_kernel, rows, picks, planes, cap),
        in_specs=[SCALARS] * (2 + planes) + [pl.BlockSpec(memory_space=pl.ANY)],
        out_specs=[vec] * 3,
        out_shape=[
            sds((planes * planes * cap, planes * rows), F32),
            sds((planes * cap, 128), F32),
            sds((rows, planes * cap), BF16),
        ],
        compiler_params=params(),
        name="route_tables",
    )(me, ids, *homes, after)


def pick_rows(pick, values):
    high = values.astype(BF16)
    low = (values - high.astype(F32)).astype(BF16)
    return jnp.dot(pick, high, preferred_element_type=F32) + jnp.dot(
        pick, low, preferred_element_type=F32
    )


def add_and_pick_kernel(planes, tile, first, own_ref, a_ref, b_ref, c_ref, hidden_ref, pick_ref, *outs):
    size = outs[0].shape[0]
    rows = hidden_ref.shape[0]
    pick = pick_ref[...]
    near, far = pick[:size].astype(BF16), pick[size:].astype(BF16)
    for start in range(0, own_ref.shape[1], tile):
        at = slice(start, start + tile)
        total = own_ref[:, at]
        for ref in (a_ref, b_ref, c_ref):
            total = total + ref[:, at].astype(F32)
        here = slice(first + start, first + start + tile)
        home = total[:rows] + hidden_ref[:, here].astype(F32)
        total = jnp.concatenate([home, total[rows:]], axis=0)
        outs[0][:, at] = pick_rows(near, total)
        others = jnp.dot(far, total.astype(BF16), preferred_element_type=F32)
        for k in range(1, planes):
            outs[k][:, at] = others[(k - 1) * size : k * size].astype(BF16)


def add_and_pick(own, received, hidden, pick, planes, first):
    features = own.shape[1]
    size = pick.shape[0] // planes
    vec = pl.BlockSpec(memory_space=pltpu.VMEM)
    return pl.pallas_call(
        functools.partial(add_and_pick_kernel, planes, 1024, first),
        in_specs=[vec] * 6,
        out_specs=[vec] * planes,
        out_shape=[sds((size, features), F32)] + [sds((size, features), BF16)] * (planes - 1),
        compiler_params=params(),
        name="add_chips",
    )(own, *received, hidden, pick)


def norm_kernel(planes, parts, *refs):
    gain_ref, resid_ref, normed_ref = refs[planes * parts], refs[-2], refs[-1]
    totals = []
    for p in range(parts):
        total = refs[p * planes][...]
        for ref in refs[p * planes + 1 : (p + 1) * planes]:
            total = total + ref[...].astype(F32)
        totals.append(total)
    resid = jnp.concatenate(totals[::-1], axis=1).astype(BF16)
    resid_ref[...] = resid
    wide = resid.astype(F32)
    scale = lax.rsqrt(jnp.mean(wide * wide, axis=1, keepdims=True) + EPSILON)
    normed_ref[...] = (wide * scale * gain_ref[...].astype(F32)).astype(BF16)


def norm(sums, gain, after):
    vec = pl.BlockSpec(memory_space=pltpu.VMEM)
    planes = len(sums[0])
    shape = (sums[0][0].shape[0], gain.shape[1])
    return pl.pallas_call(
        functools.partial(norm_kernel, planes, len(sums)),
        in_specs=[vec] * (1 + planes * len(sums))
        + [pl.BlockSpec(memory_space=pl.ANY)] * len(after),
        out_specs=[vec, vec],
        out_shape=[sds(shape, BF16), sds(shape, BF16)],
        compiler_params=params(),
        name="norm",
    )(*sums[1], *sums[0], gain, *after)


def expert_kernel(pieces, tiles, *refs):
    xs = refs[:pieces]
    gate_ref, up_ref, down_ref, own_ref, other_ref = refs[pieces:]
    tile = down_ref.shape[1] // tiles
    gate, up = 0.0, 0.0
    for t in range(tiles):
        at = slice(t * tile, (t + 1) * tile)
        x = jnp.concatenate([ref[:, at].astype(F32) for ref in xs], axis=0).astype(BF16)
        gate += jnp.dot(x, gate_ref[at, :], preferred_element_type=F32)
        up += jnp.dot(x, up_ref[at, :], preferred_element_type=F32)
    act = (gate / (1.0 + jnp.exp(-gate)) * up).astype(BF16)
    half = act.shape[0] // 2
    for t in range(tiles):
        at = slice(t * tile, (t + 1) * tile)
        out = jnp.dot(act, down_ref[:, at], preferred_element_type=F32)
        own_ref[:, at] = out[:half]
        other_ref[:, at] = out[half:].astype(BF16)


def expert(pieces, gate_up, down_proj, tiles=7):
    size, features = pieces[0].shape
    half = size * len(pieces) // 2
    vec = pl.BlockSpec(memory_space=pltpu.VMEM)
    return pl.pallas_call(
        functools.partial(expert_kernel, len(pieces), tiles),
        in_specs=[vec] * (len(pieces) + 3),
        out_specs=[vec, vec],
        out_shape=[sds((half, features), F32), sds((half, features), BF16)],
        compiler_params=params(),
        name="expert",
    )(*pieces, *gate_up, down_proj)


def weigh_kernel(planes, share, tile, own_ref, a_ref, b_ref, c_ref, resid_ref, weight_ref, *outs):
    cap = outs[0].shape[0]
    for start in range(0, own_ref.shape[1], tile):
        at = slice(start, start + tile)
        total = own_ref[:, at]
        for ref in (a_ref, b_ref, c_ref):
            total = total + ref[:, at].astype(F32)
        total = total * weight_ref[:, :1] + resid_ref[:, at].astype(F32) * share
        outs[0][:, at] = total[:cap]
        for k in range(1, planes):
            outs[k][:, at] = total[k * cap : (k + 1) * cap].astype(BF16)


def weigh(own, received, resid, weight, planes, picks):
    count, features = own.shape
    cap = count // planes
    vec = pl.BlockSpec(memory_space=pltpu.VMEM)
    return pl.pallas_call(
        functools.partial(weigh_kernel, planes, 1.0 / picks, 1024),
        in_specs=[vec] * 6,
        out_specs=[vec] * planes,
        out_shape=[sds((cap, features), F32)] + [sds((cap, features), BF16)] * (planes - 1),
        compiler_params=params(),
        name="weigh",
    )(own, *received, resid, weight)


def combine_kernel(planes, merge_ref, *refs):
    out_ref = refs[planes]
    table = jnp.concatenate([ref[...].astype(F32) for ref in refs[:planes]], axis=0)
    out_ref[...] = pick_rows(merge_ref[...], table).astype(BF16)


def combine(merge, pieces):
    vec = pl.BlockSpec(memory_space=pltpu.VMEM)
    return pl.pallas_call(
        functools.partial(combine_kernel, len(pieces)),
        in_specs=[vec] * (1 + len(pieces)),
        out_specs=vec,
        out_shape=sds((merge.shape[0], pieces[0].shape[1]), BF16),
        compiler_params=params(),
        name="combine",
    )(merge, *pieces)


def body(
    queries,
    latent_cache,
    lengths,
    hidden_in,
    route_ids,
    route_weights,
    value_up,
    out_proj,
    norm_gain,
    gate_up,
    down_proj,
):
    devices = lax.axis_size("dp")
    planes = devices // SPLIT
    rows = hidden_in.shape[0]
    picks = route_ids.shape[1]
    cap = max(2, (rows * picks + planes - 1) // planes)
    me = lax.axis_index("dp").astype(jnp.int32).reshape(1)

    def swap(x, mask):
        return lax.ppermute(x, "dp", [(i, i ^ mask) for i in range(devices)])

    def over_planes(messages):
        moved = [swap(x, k << 3) for k, x in enumerate(messages, 1)]
        return moved[1:] + moved[:1]

    def over_chips(messages):
        return [swap(x, k << 1) for k, x in enumerate(messages, 1)]

    latents = attention(queries, latent_cache, lengths)
    by_heads = lax.all_to_all(latents, "dp", split_axis=0, concat_axis=0, tiled=True)
    (early,) = fetch([out_proj], [(1, TILES, FIRST, EARLY)], latents, "fetch_projections")
    mine = routes(route_ids, route_weights, latents)
    homes = over_planes([mine] * (planes - 1))
    homes = [mine] + homes[-1:] + homes[:-1]
    own, other = project(me, by_heads, value_up, out_proj, early, planes, rows, homes[1:] + early[:1])
    pick, weight, merge = tables(me, route_ids, homes, cap, other[1])
    parts = []
    for n in range(2):
        part, *out = add_and_cut(own[n : n + 1], [swap(other[n], 1)], 4, "add_core", [pick])
        parts.append((part, over_chips(out)))
    sums, first = [], 0
    for own, received in parts:
        own, *out = add_and_pick(own, received, hidden_in, pick, planes, first)
        sums.append([own] + over_planes(out))
        first += own.shape[1]
    gate_up, (down_proj,) = fetch(
        [gate_up, down_proj], [(0, 2, 0, 2), (0, 1, 0, 1)], sums[1][0], "fetch_experts"
    )
    resid, picked = norm(sums, norm_gain[None], gate_up[:1])
    chips = [picked] + [swap(picked, k << 1) for k in (1, 2, 3)]
    pieces = chips + [swap(x, 1) for x in chips]
    own, other = expert(pieces, gate_up, down_proj)
    own, *out = add_and_cut([own], [swap(other, 1)], 4, "add_expert_core")
    own, *out = weigh(own, over_chips(out), resid, weight, planes, picks)
    return combine(merge, [own] + over_planes(out))


def solution(mesh):
    placed = (
        P(("groups", "dp"), None, None),
        P(("groups", "dp"), None, None),
        P(("groups", "dp")),
        P(("groups", "dp"), None),
        P(("groups", "dp"), None),
        P(("groups", "dp"), None),
        P("dp", None, None),
        P("dp", None),
        P(),
        P(None, None, "dp"),
        P("dp", None),
    )
    return jax.shard_map(
        body, mesh=mesh, in_specs=placed, out_specs=P(("groups", "dp"), None), check_vma=False
    )
```
